128 devices in a mesh: row: 8 (over x_lo, y), col: 8 (over z, x_hi), ch: 2 (over core).
Axes of the slice: x: 4 (x_hi: 2, x_lo: 2; x = x_hi * 2 + x_lo), y: 4, z: 4, core: 2. Of those that a mesh axis runs over, the one named last changes fastest.
Arguments:
- pair: bfloat16 [512, 512, 128], P('row', 'col'), may hold values from -6 to 6
- cotangent: bfloat16 [512, 512, 128], P('row', 'col'), may hold values from -6 to 6
- pair_mask: int32 [512, 512], P('row', 'col'), may hold values 0 or 1
- norm_gain: float32 [128], replicated, may hold values from 0.1 to 1.9
- norm_bias: float32 [128], replicated, may hold values from -3 to 3
- w_left: bfloat16 [128, 128], P(None, 'ch'), may hold values from -0.5 to 0.5
- w_left_gate: bfloat16 [128, 128], P(None, 'ch'), may hold values from -0.5 to 0.5
- w_right: bfloat16 [128, 128], P(None, 'ch'), may hold values from -0.5 to 0.5
- w_right_gate: bfloat16 [128, 128], P(None, 'ch'), may hold values from -0.5 to 0.5
- w_out_gate: bfloat16 [128, 128], replicated, may hold values from -0.5 to 0.5
- out_norm_gain: float32 [128], P('ch'), may hold values from 0.1 to 1.9
- out_norm_bias: float32 [128], P('ch'), may hold values from -3 to 3
- w_out: bfloat16 [128, 128], P('ch'), may hold values from -0.5 to 0.5
Outputs:
- d_pair: float32 [512, 512, 128], P('row', 'col')
- d_norm_gain: float32 [128], replicated
- d_norm_bias: float32 [128], replicated
- d_left: float32 [128, 128], P(None, 'ch')
- d_left_gate: float32 [128, 128], P(None, 'ch')
- d_right: float32 [128, 128], P(None, 'ch')
- d_right_gate: float32 [128, 128], P(None, 'ch')
- d_out_gate: float32 [128, 128], replicated
- d_out_norm_gain: float32 [128], P('ch')
- d_out_norm_bias: float32 [128], P('ch')
- d_out: float32 [128, 128], P('ch')
The draws below stay inside these ranges and needn't reach their ends.
All inputs are finite; a program needn't handle non-finite values. No bound on the sum of `pair_mask` on one device may be relied on, other than what follows from the above.
Results may differ from the reference program's by a relative error of at most 0.02.
Values may be sent and summed in bfloat16 or wider, within the bound.
No kernel may reach another device: no remote copies, remote signals or barrier semaphores. Data moves between devices by JAX's collectives and lax.ppermute only.
A program may use at most 192 MiB of HBM per device.

```python
import jax
import jax.numpy as jnp
from jax import lax

C = 128
H = 128
N = 512


def set_ends(array, rng, least, high):
    index_at = [jax.random.randint(jax.random.fold_in(rng, axis), (), 0, length) for axis, length in enumerate(array.shape)]
    longest = array.shape.index(max(array.shape))
    beside = index_at[:longest] + [(index_at[longest] + 1) % array.shape[longest]] + index_at[longest + 1:]
    return array.at[tuple(index_at)].set(least).at[tuple(beside)].set(high)


def shard_levels(key, extent, shards, smallest, largest):
    level = 1.0
    for axis_at, blocks in shards:
        heights = jax.random.uniform(jax.random.fold_in(jax.random.fold_in(key, 6), axis_at), (blocks,), jnp.float32, smallest / len(shards), largest / len(shards))
        level = level * jnp.repeat(jnp.exp(heights), extent[axis_at] // blocks).reshape((-1,) + (1,) * (len(extent) - 1 - axis_at))
    return level


def scatter_about(stream_key, dims, deviation, limit, cuts=(), dtype=jnp.bfloat16):
    drawn = jax.random.normal(stream_key, dims, jnp.float32) * deviation
    if len(cuts) > 0:
        drawn = shard_levels(stream_key, dims, cuts, -0.22, 0.18) * drawn
    return jnp.clip(drawn, min=-limit, max=limit).astype(dtype)


def setup_inputs(seed: int = 0) -> dict:
    seeds = jax.random.split(jax.random.key(seed), 14)
    return {
        "pair": scatter_about(seeds[0], (N, N, C), 1.0, 6.0, ((0, 8), (1, 8))),
        "cotangent": scatter_about(seeds[1], (N, N, C), 1.0, 6.0, ((0, 8), (1, 8))),
        "pair_mask": set_ends((jax.random.randint(seeds[2], (N, N), 0, 8) < 7).astype(jnp.int32), jax.random.fold_in(seeds[2], 1), 0, 1),
        "norm_gain": jnp.clip(1.0 + 0.18 * jax.random.normal(seeds[3], (C,), jnp.float32), 0.1, 1.9),
        "norm_bias": scatter_about(seeds[4], (C,), 0.5, 3.0, (), jnp.float32),
        "w_left": scatter_about(seeds[5], (C, H), C ** -0.5, 0.5, ((1, 2),)),
        "w_left_gate": scatter_about(seeds[6], (C, H), C ** -0.5, 0.5, ((1, 2),)),
        "w_right": scatter_about(seeds[7], (C, H), C ** -0.5, 0.5, ((1, 2),)),
        "w_right_gate": scatter_about(seeds[8], (C, H), C ** -0.5, 0.5, ((1, 2),)),
        "w_out_gate": scatter_about(seeds[9], (C, C), C ** -0.5, 0.5),
        "out_norm_gain": jnp.clip(1.0 + 0.18 * jax.random.normal(seeds[10], (H,), jnp.float32), 0.1, 1.9),
        "out_norm_bias": scatter_about(seeds[11], (H,), 0.5, 3.0, ((0, 2),), jnp.float32),
        "w_out": scatter_about(seeds[12], (H, C), H ** -0.5, 0.5, ((0, 2),)),
    }


def norm_parts(values):
    mean = lax.optimization_barrier(jnp.mean(values, axis=-1, keepdims=True))
    centred = values - mean
    inverse = 1.0 / jnp.sqrt(lax.optimization_barrier(jnp.mean(centred * centred, axis=-1, keepdims=True)) + 1e-05)
    return (centred * inverse, inverse)

def reference(pair, cotangent, pair_mask, norm_gain, norm_bias, w_left, w_left_gate, w_right, w_right_gate, w_out_gate, out_norm_gain, out_norm_bias, w_out):
    f32 = jnp.float32
    bf16 = jnp.bfloat16
    zhat, inverse_one = norm_parts(pair.astype(f32))
    normed = (zhat * norm_gain + norm_bias).astype(bf16)
    normf = normed.astype(f32)

    def project(weight):
        return jnp.einsum('ijc,ch->ijh', normf, weight.astype(f32))
    maskf = pair_mask.astype(f32)[:, :, None]
    left_lin = project(w_left)
    left_sig = jax.nn.sigmoid(project(w_left_gate))
    left = (maskf * left_sig * left_lin).astype(bf16)
    right_lin = project(w_right)
    right_sig = jax.nn.sigmoid(project(w_right_gate))
    right = (maskf * right_sig * right_lin).astype(bf16)
    leftf = left.astype(f32)
    rightf = right.astype(f32)
    tri = jnp.einsum('ikh,jkh->ijh', leftf, rightf)
    that, inverse_two = norm_parts(tri)
    tnorm = (that * out_norm_gain + out_norm_bias).astype(bf16)
    tnormf = tnorm.astype(f32)
    proj = jnp.einsum('ijh,hc->ijc', tnormf, w_out.astype(f32))
    gate = jax.nn.sigmoid(project(w_out_gate))
    cotf = cotangent.astype(f32)
    d_proj = (cotf * gate).astype(bf16).astype(f32)
    d_gpre = (cotf * proj * gate * (1.0 - gate)).astype(bf16).astype(f32)
    d_out = jnp.einsum('ijh,ijc->hc', tnormf, d_proj)
    d_tnorm = jnp.einsum('ijc,hc->ijh', d_proj, w_out.astype(f32))
    d_out_norm_gain = lax.optimization_barrier(jnp.sum(d_tnorm * that, axis=(0, 1)))
    d_out_norm_bias = lax.optimization_barrier(jnp.sum(d_tnorm, axis=(0, 1)))
    dth = d_tnorm * out_norm_gain
    d_tri = (dth - lax.optimization_barrier(jnp.mean(dth, axis=-1, keepdims=True)) - that * lax.optimization_barrier(jnp.mean(dth * that, axis=-1, keepdims=True))) * inverse_two
    d_trif = d_tri.astype(bf16).astype(f32)
    d_left_full = jnp.einsum('ijh,jkh->ikh', d_trif, rightf)
    d_right_full = jnp.einsum('ijh,ikh->jkh', d_trif, leftf)
    d_llin = (d_left_full * maskf * left_sig).astype(bf16).astype(f32)
    d_lgp = (d_left_full * maskf * left_lin * left_sig * (1.0 - left_sig)).astype(bf16).astype(f32)
    d_rlin = (d_right_full * maskf * right_sig).astype(bf16).astype(f32)
    d_rgp = (d_right_full * maskf * right_lin * right_sig * (1.0 - right_sig)).astype(bf16).astype(f32)

    def weight_grad(delta):
        return jnp.einsum('ijc,ijh->ch', normf, delta)

    def back(delta, weight):
        return jnp.einsum('ijh,ch->ijc', delta, weight.astype(f32))
    d_normed = back(d_llin, w_left) + back(d_lgp, w_left_gate) + back(d_rlin, w_right) + back(d_rgp, w_right_gate)
    d_normed = d_normed + back(d_gpre, w_out_gate)
    d_norm_gain = lax.optimization_barrier(jnp.sum(d_normed * zhat, axis=(0, 1)))
    d_norm_bias = lax.optimization_barrier(jnp.sum(d_normed, axis=(0, 1)))
    dzh = d_normed * norm_gain
    d_pair = (dzh - lax.optimization_barrier(jnp.mean(dzh, axis=-1, keepdims=True)) - zhat * lax.optimization_barrier(jnp.mean(dzh * zhat, axis=-1, keepdims=True))) * inverse_one
    return (d_pair, d_norm_gain, d_norm_bias, weight_grad(d_llin), weight_grad(d_lgp), weight_grad(d_rlin), weight_grad(d_rgp), weight_grad(d_gpre), d_out_norm_gain, d_out_norm_bias, d_out)
```

```python
import functools

import jax
import jax.numpy as jnp
from jax import lax
from jax.experimental import pallas as pl
from jax.experimental.pallas import tpu as pltpu
from jax.sharding import PartitionSpec as P

f32 = jnp.float32
bf16 = jnp.bfloat16
ALL = ("row", "col", "ch")
TILES = 16
EPS = 1e-05
VMEM_LIMIT = 48 * 1024 * 1024


def matmul(a, b):
    return lax.dot_general(a, b, (((1,), (0,)), ((), ())), preferred_element_type=f32)


def matmul_nt(a, b):
    return lax.dot_general(a, b, (((1,), (1,)), ((), ())), preferred_element_type=f32)


def matmul_tn(a, b):
    return lax.dot_general(a, b, (((0,), (0,)), ((), ())), preferred_element_type=f32)


def sigmoid(x):
    return 0.5 * jnp.tanh(0.5 * x) + 0.5


def column(row):
    return jnp.broadcast_to(row, (128, 128)).T


def norm_over_rows(x):
    mean = jnp.mean(x, axis=0, keepdims=True)
    centred = x - mean
    inverse = lax.rsqrt(jnp.mean(centred * centred, axis=0, keepdims=True) + EPS)
    return centred * inverse, inverse


def pair_tile(ref, q):
    return jnp.concatenate([ref[q], ref[TILES + q]], axis=0).astype(f32).T


def mask_rows(mask):
    return jnp.concatenate([mask[:TILES], mask[TILES:]], axis=1).astype(f32)


def exchange(a, b):
    return (
        jnp.concatenate([a[..., :64], b[..., :64]], axis=-1),
        jnp.concatenate([a[..., 64:], b[..., 64:]], axis=-1),
    )


def load_matrix(blocks, at, out):
    for pair in range(4):
        low, high = exchange(
            blocks[:, 2 * pair, :, at : at + 16, :], blocks[:, 2 * pair + 1, :, at : at + 16, :]
        )
        out[:, pair * 128 : (pair + 1) * 128] = jnp.stack([low, high], axis=2).reshape(512, 128)


def store_matrix(matrix, blocks, at):
    for pair in range(4):
        part = matrix[:, pair * 128 : (pair + 1) * 128].reshape(8, 2, 2, 16, 128)
        first, second = exchange(part[:, :, 0], part[:, :, 1])
        blocks[:, 2 * pair, :, at : at + 16, :] = first
        blocks[:, 2 * pair + 1, :, at : at + 16, :] = second


def first_kernel(
    ch_ref, pair_ref, mask_ref, gain_ref, bias_ref, own_ref, other_ref,
    send_ref, normed_ref, zhat_ref, inverse_ref, w_ref, w_out_ref, cols_ref, left_s, right_s, mask_s,
):
    is_first = ch_ref[0] == 0
    own, other = own_ref[...], other_ref[...]
    low = jnp.where(is_first, own, other)
    high = jnp.where(is_first, other, own)
    for n in range(4):
        w_ref[n * 128 : n * 128 + 64] = low[n * 64 : n * 64 + 64].astype(bf16)
        w_ref[n * 128 + 64 : n * 128 + 128] = high[n * 64 : n * 64 + 64].astype(bf16)
    w_out_ref[:64] = low[256:320].astype(bf16)
    w_out_ref[64:] = high[256:320].astype(bf16)
    low_col, high_col = column(low[320:321]), column(high[320:321])
    cols_ref[0, :64] = low_col[:64]
    cols_ref[0, 64:] = high_col[:64]
    cols_ref[1, :64] = low_col[64:]
    cols_ref[1, 64:] = high_col[64:]
    gain, bias = column(gain_ref[...]), column(bias_ref[...])
    cols_ref[2] = gain
    mask_s[...] = mask_rows(mask_ref[...])
    for q in range(TILES):
        lanes = slice(q * 128, (q + 1) * 128)
        zhat, inverse = norm_over_rows(pair_tile(pair_ref, q))
        zhat_ref[:, lanes] = zhat
        inverse_ref[q : q + 1] = inverse
        normed = (zhat * gain + bias).astype(bf16)
        normed_ref[:, lanes] = normed
        y = matmul(w_ref[...], normed)
        m = mask_s[q : q + 1]
        left_s[pl.ds(q, 128, stride=TILES)] = m * sigmoid(y[128:256]) * y[:128]
        right_s[pl.ds(q, 128, stride=TILES)] = m * sigmoid(y[384:]) * y[256:384]
    send_ref[:, :TILES] = left_s[...].astype(bf16).reshape(128, TILES, 128)
    send_ref[:, TILES:] = right_s[...].astype(bf16).reshape(128, TILES, 128)


def triangle_kernel(blocks_ref, send_ref, left_ref, right_ref):
    load_matrix(blocks_ref, 0, left_ref)
    load_matrix(blocks_ref, 16, right_ref)
    tri = matmul_nt(left_ref[...], right_ref[...]).astype(bf16)
    store_matrix(tri, send_ref, 0)


def middle_kernel(
    ch_ref, tri_ref, normed_ref, cot_ref, w_gate_ref, w_out_ref, cols_ref,
    send_ref, gpre_ref, early_ref, tri_s, d_tri_s, tnorm_s, d_proj_s,
):
    tri_s[...] = tri_ref[...].astype(f32).reshape(128 * TILES, 128)
    w_out = w_out_ref[...]
    w_out_t = w_out.astype(f32).T.astype(bf16)
    w_gate_t = w_gate_ref[...].astype(f32).T.astype(bf16)
    gain, bias = cols_ref[0], cols_ref[1]
    gain_sum = jnp.zeros((128, 128), f32)
    bias_sum = jnp.zeros((128, 128), f32)
    for q in range(TILES):
        lanes = slice(q * 128, (q + 1) * 128)
        that, inverse = norm_over_rows(tri_s[pl.ds(q, 128, stride=TILES)])
        tnorm = (that * gain + bias).astype(bf16)
        tnorm_s[:, lanes] = tnorm
        proj = matmul(w_out_t, tnorm)
        gate = sigmoid(matmul(w_gate_t, normed_ref[:, lanes]))
        cot = pair_tile(cot_ref, q)
        d_proj = (cot * gate).astype(bf16)
        d_proj_s[:, lanes] = d_proj
        gpre_ref[:, lanes] = (cot * proj * gate * (1.0 - gate)).astype(bf16)
        d_tnorm = matmul(w_out, d_proj)
        gain_sum = gain_sum + d_tnorm * that
        bias_sum = bias_sum + d_tnorm
        dth = d_tnorm * gain
        d_tri_s[pl.ds(q, 128, stride=TILES)] = (
            dth
            - jnp.mean(dth, axis=0, keepdims=True)
            - that * jnp.mean(dth * that, axis=0, keepdims=True)
        ) * inverse
    send_ref[...] = d_tri_s[...].astype(bf16).reshape(128, TILES, 128)
    early_ref[0] = matmul_nt(d_proj_s[...], tnorm_s[...])
    early_ref[1] = matmul_nt(normed_ref[...], gpre_ref[...])
    early_ref[2] = jnp.broadcast_to(jnp.sum(gain_sum, axis=1, keepdims=True), (128, 128))
    early_ref[3] = jnp.broadcast_to(jnp.sum(bias_sum, axis=1, keepdims=True), (128, 128))


def back_kernel(blocks_ref, left_ref, right_ref, send_ref, d_tri_s):
    load_matrix(blocks_ref, 0, d_tri_s)
    d_tri = d_tri_s[...]
    store_matrix(matmul(d_tri, right_ref[...]).astype(bf16), send_ref, 0)
    store_matrix(matmul_tn(d_tri, left_ref[...]).astype(bf16), send_ref, 16)


def last_kernel(
    d_ref, mask_ref, normed_ref, zhat_ref, inverse_ref, gpre_ref, w_ref, w_gate_ref, cols_ref, early_ref,
    d_pair_ref, send_ref, d_s, delta_s, mask_s, grads_s,
):
    d_s[...] = d_ref[...].astype(f32).reshape(128 * 2 * TILES, 128)
    mask_s[...] = mask_rows(mask_ref[...])
    w_back = jnp.concatenate(
        [w_ref[n * 128 : (n + 1) * 128].astype(f32).T.astype(bf16) for n in range(4)]
        + [w_gate_ref[...]],
        axis=1,
    )
    gain = cols_ref[2]
    gain_sum = jnp.zeros((128, 128), f32)
    bias_sum = jnp.zeros((128, 128), f32)
    delta_s[512:] = gpre_ref[...]
    for q in range(TILES):
        lanes = slice(q * 128, (q + 1) * 128)
        y = matmul(w_ref[...], normed_ref[:, lanes])
        m = mask_s[q : q + 1]
        for side in range(2):
            d_full = d_s[pl.ds(side * TILES + q, 128, stride=2 * TILES)] * m
            lin = y[side * 256 : side * 256 + 128]
            sig = sigmoid(y[side * 256 + 128 : side * 256 + 256])
            d_lin = d_full * sig
            delta_s[side * 256 : side * 256 + 128, lanes] = d_lin.astype(bf16)
            delta_s[side * 256 + 128 : side * 256 + 256, lanes] = (
                d_lin * lin * (1.0 - sig)
            ).astype(bf16)
        d_normed = matmul(w_back, delta_s[:, lanes])
        zhat = zhat_ref[:, lanes]
        gain_sum = gain_sum + d_normed * zhat
        bias_sum = bias_sum + d_normed
        dzh = d_normed * gain
        d_pair = (
            dzh
            - jnp.mean(dzh, axis=0, keepdims=True)
            - zhat * jnp.mean(dzh * zhat, axis=0, keepdims=True)
        ) * inverse_ref[q : q + 1]
        rows = d_pair.T
        d_pair_ref[q] = rows[:64]
        d_pair_ref[TILES + q] = rows[64:]
    grads = matmul_nt(normed_ref[...], delta_s[:512])
    for n in range(4):
        grads_s[pl.ds(n, 128, stride=8)] = grads[:, n * 128 : (n + 1) * 128]
    grads_s[pl.ds(4, 128, stride=8)] = early_ref[0]
    grads_s[pl.ds(5, 128, stride=8)] = early_ref[1]
    lane = lax.broadcasted_iota(jnp.int32, (128, 128), 1)
    sums = jnp.where(
        lane < 64,
        jnp.where(
            lane < 32,
            jnp.sum(gain_sum, axis=1, keepdims=True),
            jnp.sum(bias_sum, axis=1, keepdims=True),
        ),
        jnp.where(lane < 96, early_ref[2], early_ref[3]),
    )
    grads_s[pl.ds(6, 128, stride=8)] = sums
    grads_s[pl.ds(7, 128, stride=8)] = jnp.zeros((128, 128), f32)
    send_ref[...] = grads_s[...].reshape(128, 8, 128).astype(bf16)


def sum_kernel(grads_ref, send_ref):
    total = jnp.sum(grads_ref[...].astype(f32), axis=0)
    send_ref[...] = jnp.broadcast_to(total.astype(bf16)[None], (128, 8, 128))


def end_kernel(
    ch_ref, grads_ref, own_ref, other_ref,
    d_pair_ref, gain_ref, bias_ref, left_ref, left_gate_ref, right_ref, right_gate_ref, gate_ref,
    out_gain_ref, out_bias_ref, out_ref, grads_s, sems,
):
    ch = ch_ref[0]
    first = pltpu.make_async_copy(own_ref, d_pair_ref.at[pl.ds(ch * 32, 32)], sems.at[0])
    second = pltpu.make_async_copy(other_ref, d_pair_ref.at[pl.ds(32 - ch * 32, 32)], sems.at[1])
    first.start()
    second.start()
    grads_s[...] = grads_ref[...].astype(f32).reshape(1024, 128)
    is_first = ch == 0
    for n, ref in enumerate((left_ref, left_gate_ref, right_ref, right_gate_ref)):
        whole = grads_s[pl.ds(n, 128, stride=8)]
        ref[...] = jnp.where(is_first, whole[:, :64], whole[:, 64:])
    d_out = grads_s[pl.ds(4, 128, stride=8)].T
    out_ref[...] = jnp.where(is_first, d_out[:64], d_out[64:])
    gate_ref[...] = grads_s[pl.ds(5, 128, stride=8)]
    sums = grads_s[pl.ds(6, 128, stride=8)].T
    gain_ref[...] = sums[0:1]
    bias_ref[...] = sums[32:33]
    out_gain_ref[...] = jnp.where(is_first, sums[64:65, :64], sums[64:65, 64:])
    out_bias_ref[...] = jnp.where(is_first, sums[96:97, :64], sums[96:97, 64:])
    first.wait()
    second.wait()


def whole(shape):
    return pl.BlockSpec(shape, lambda *_: (0,) * len(shape))


def half(shape):
    return pl.BlockSpec(shape, lambda _, ch: (ch[0],) + (0,) * (len(shape) - 1))


def call(kernel, in_specs, out_shapes, scratch, *args, out_specs=None):
    return pl.pallas_call(
        kernel,
        out_shape=[jax.ShapeDtypeStruct(s, t) for s, t in out_shapes],
        grid_spec=pltpu.PrefetchScalarGridSpec(
            num_scalar_prefetch=1,
            grid=(1,),
            in_specs=in_specs,
            out_specs=out_specs or [whole(s) for s, _ in out_shapes],
            scratch_shapes=scratch,
        ),
        compiler_params=pltpu.CompilerParams(vmem_limit_bytes=VMEM_LIMIT),
    )(*args)


def drop_first(kernel):
    def inner(_, *refs):
        kernel(*refs)

    return inner


def to_all(x):
    return lax.all_to_all(x, ALL, 0, 0, tiled=True)


def body(
    pair, cotangent, pair_mask, norm_gain, norm_bias, w_left, w_left_gate, w_right, w_right_gate,
    w_out_gate, out_norm_gain, out_norm_bias, w_out,
):
    pairs = 128 * TILES
    ch = lax.axis_index("ch").astype(jnp.int32).reshape(1)
    with jax.named_scope("weights"):
        packed = jnp.concatenate(
            [w.T for w in (w_left, w_left_gate, w_right, w_right_gate)] + [w_out], axis=0
        ).astype(f32)
        norms = jnp.concatenate([out_norm_gain, out_norm_bias])[None]
        packed = jnp.concatenate([packed, norms, jnp.zeros((7, 128), f32)], axis=0)
        other = lax.ppermute(packed, "ch", [(0, 1), (1, 0)])
    half_pairs = half((32, 64, 128))
    half_mask = half((32, 64))
    row = whole((1, 128))
    with jax.named_scope("first"):
        send, normed, zhat, inverse, w_all, w_out_all, cols = call(
            first_kernel,
            [half_pairs, half_mask, row, row, whole((328, 128)), whole((328, 128))],
            [
                ((128, 2 * TILES, 128), bf16),
                ((128, pairs), bf16),
                ((128, pairs), f32),
                ((TILES, 128), f32),
                ((512, 128), bf16),
                ((128, 128), bf16),
                ((3, 128, 128), f32),
            ],
            [pltpu.VMEM((pairs, 128), f32), pltpu.VMEM((pairs, 128), f32), pltpu.VMEM((TILES, 128), f32)],
            ch, pair, pair_mask, norm_gain[None], norm_bias[None], packed, other,
        )
    with jax.named_scope("left_right"):
        blocks = to_all(send).reshape(8, 8, 2, 2 * TILES, 128)
    with jax.named_scope("triangle"):
        send, left, right = call(
            drop_first(triangle_kernel),
            [whole((8, 8, 2, 2 * TILES, 128))],
            [((8, 8, 2, TILES, 128), bf16), ((512, 512), bf16), ((512, 512), bf16)],
            [],
            ch, blocks,
        )
    with jax.named_scope("tri"):
        tri = to_all(send.reshape(128, TILES, 128))
    with jax.named_scope("middle"):
        send, gpre, early = call(
            middle_kernel,
            [
                whole((128, TILES, 128)), whole((128, pairs)), half_pairs, whole((128, 128)),
                whole((128, 128)), whole((3, 128, 128)),
            ],
            [((128, TILES, 128), bf16), ((128, pairs), bf16), ((4, 128, 128), f32)],
            [
                pltpu.VMEM((pairs, 128), f32),
                pltpu.VMEM((pairs, 128), f32),
                pltpu.VMEM((128, pairs), bf16),
                pltpu.VMEM((128, pairs), bf16),
            ],
            ch, tri, normed, cotangent, w_out_gate, w_out_all, cols,
        )
    with jax.named_scope("d_tri"):
        blocks = to_all(send).reshape(8, 8, 2, TILES, 128)
    with jax.named_scope("back"):
        (send,) = call(
            drop_first(back_kernel),
            [whole((8, 8, 2, TILES, 128)), whole((512, 512)), whole((512, 512))],
            [((8, 8, 2, 2 * TILES, 128), bf16)],
            [pltpu.VMEM((512, 512), bf16)],
            ch, blocks, left, right,
        )
    with jax.named_scope("d_left_right"):
        d_full = to_all(send.reshape(128, 2 * TILES, 128))
    with jax.named_scope("last"):
        d_own, send = call(
            drop_first(last_kernel),
            [
                whole((128, 2 * TILES, 128)), half_mask, whole((128, pairs)), whole((128, pairs)),
                whole((TILES, 128)), whole((128, pairs)), whole((512, 128)), whole((128, 128)),
                whole((3, 128, 128)), whole((4, 128, 128)),
            ],
            [((32, 64, 128), f32), ((128, 8, 128), bf16)],
            [
                pltpu.VMEM((2 * pairs, 128), f32),
                pltpu.VMEM((640, pairs), bf16),
                pltpu.VMEM((TILES, 128), f32),
                pltpu.VMEM((1024, 128), f32),
            ],
            ch, d_full, pair_mask, normed, zhat, inverse, gpre, w_all, w_out_gate, cols, early,
        )
    with jax.named_scope("d_pair"):
        d_other = lax.ppermute(d_own, "ch", [(0, 1), (1, 0)])
    with jax.named_scope("grads"):
        parts = to_all(send)
        (send,) = call(
            drop_first(sum_kernel), [whole((128, 8, 128))], [((128, 8, 128), bf16)], [], ch, parts
        )
        parts = to_all(send)
    with jax.named_scope("end"):
        anywhere = pl.BlockSpec(memory_space=pl.ANY)
        shapes = [
            ((64, 64, 128), f32), ((1, 128), f32), ((1, 128), f32), ((128, 64), f32), ((128, 64), f32),
            ((128, 64), f32), ((128, 64), f32), ((128, 128), f32), ((1, 64), f32), ((1, 64), f32),
            ((64, 128), f32),
        ]
        outs = call(
            end_kernel,
            [whole((128, 8, 128)), anywhere, anywhere],
            shapes,
            [pltpu.VMEM((1024, 128), f32), pltpu.SemaphoreType.DMA((2,))],
            ch, parts, d_own, d_other,
            out_specs=[anywhere] + [whole(s) for s, _ in shapes[1:]],
        )
    return tuple(o[0] if o.shape[0] == 1 else o for o in outs)


def solution(mesh):
    placed = (
        P("row", "col", None), P("row", "col", None), P("row", "col"), P(), P(), P(None, "ch"),
        P(None, "ch"), P(None, "ch"), P(None, "ch"), P(), P("ch"), P("ch"), P("ch", None),
    )
    return jax.shard_map(
        body,
        mesh=mesh,
        in_specs=placed,
        out_specs=(
            P("row", "col", None), P(), P(), P(None, "ch"), P(None, "ch"), P(None, "ch"),
            P(None, "ch"), P(), P("ch"), P("ch"), P("ch", None),
        ),
        check_vma=False,
    )
```

```python
import jax
import jax.numpy as jnp
from jax import lax
from jax.experimental import pallas as pl
from jax.experimental.pallas import tpu as pltpu
from jax.sharding import PartitionSpec as P

f32 = jnp.float32
bf16 = jnp.bfloat16
ALL = ("row", "col", "ch")
TILES = 16
EPS = 1e-05
VMEM_LIMIT = 48 * 1024 * 1024


def matmul(a, b):
    return lax.dot_general(a, b, (((1,), (0,)), ((), ())), preferred_element_type=f32)


def matmul_nt(a, b):
    return lax.dot_general(a, b, (((1,), (1,)), ((), ())), preferred_element_type=f32)


def matmul_tn(a, b):
    return lax.dot_general(a, b, (((0,), (0,)), ((), ())), preferred_element_type=f32)


def sigmoid(x):
    return 0.5 * jnp.tanh(0.5 * x) + 0.5


def column(row):
    return jnp.broadcast_to(row, (128, 128)).T


def norm_over_rows(x):
    mean = jnp.mean(x, axis=0, keepdims=True)
    centred = x - mean
    inverse = lax.rsqrt(jnp.mean(centred * centred, axis=0, keepdims=True) + EPS)
    return centred * inverse, inverse


def pair_tiles(ref, start, q):
    tiles = [
        jnp.concatenate([ref[start + q + n], ref[start + TILES + q + n]], axis=0).astype(f32).T
        for n in range(2)
    ]
    return jnp.concatenate(tiles, axis=1)


def mask_rows(mask):
    return jnp.concatenate([mask[:TILES], mask[TILES:]], axis=1).astype(f32)


def mask_pair(rows, start):
    return jnp.concatenate([rows[pl.ds(start, 1)], rows[pl.ds(start + 1, 1)]], axis=1)


def store_tiles(ref, start, stride, value):
    count = value.shape[0]
    ref[pl.ds(start, count, stride=stride)] = value[:, :128]
    ref[pl.ds(start + 1, count, stride=stride)] = value[:, 128:]


def load_tiles(ref, start, stride, count=128):
    return jnp.concatenate(
        [ref[pl.ds(start + n, count, stride=stride)] for n in range(2)], axis=1
    )


def both_halves(is_first, own_ref, other_ref, start, count):
    own, other = own_ref[start : start + count], other_ref[start : start + count]
    return jnp.concatenate(
        [jnp.where(is_first, own, other), jnp.where(is_first, other, own)], axis=0
    )


def exchange(a, b):
    return (
        jnp.concatenate([a[..., :64], b[..., :64]], axis=-1),
        jnp.concatenate([a[..., 64:], b[..., 64:]], axis=-1),
    )


def load_matrix(blocks, out):
    for pair in range(4):
        low, high = exchange(blocks[:, 2 * pair], blocks[:, 2 * pair + 1])
        out[:, pair * 128 : (pair + 1) * 128] = jnp.stack([low, high], axis=2).reshape(512, 128)


def store_matrix(matrix, blocks, at):
    for pair in range(4):
        part = matrix[:, pair * 128 : (pair + 1) * 128].reshape(8, 2, 2, 16, 128)
        first, second = exchange(part[:, :, 0], part[:, :, 1])
        blocks[:, 2 * pair, :, at : at + 16, :] = first
        blocks[:, 2 * pair + 1, :, at : at + 16, :] = second


def first_kernel(
    pair_hbm, mask_hbm, gain_hbm, bias_hbm, left_hbm, left_gate_hbm, right_hbm, right_gate_hbm,
    w_out_hbm, out_gain_hbm, out_bias_hbm, cot_hbm, w_gate_hbm,
    send_ref, normed_ref, zhat_ref, inverse_ref, mask_ref, gain_ref, packed_ref, cot_ref, w_gate_ref,
    pair_s, mask_s, norm_s, w_s, w_out_s, out_gain_s, out_bias_s, rows_s, send_s, sems,
):
    ch = lax.axis_index("ch")
    own, other = ch * 32, 32 - ch * 32
    copies = [
        (gain_hbm, norm_s.at[0]),
        (bias_hbm, norm_s.at[1]),
        (left_hbm, w_s.at[0:64]),
        (left_gate_hbm, w_s.at[64:128]),
        (right_hbm, w_s.at[128:192]),
        (right_gate_hbm, w_s.at[192:256]),
        (mask_hbm, mask_s),
        (pair_hbm.at[pl.ds(own, 32)], pair_s.at[pl.ds(own, 32)]),
        (w_out_hbm, w_out_s),
        (out_gain_hbm, out_gain_s),
        (out_bias_hbm, out_bias_s),
        (pair_hbm.at[pl.ds(other, 32)], pair_s.at[pl.ds(other, 32)]),
        (cot_hbm.at[pl.ds(own, 32)], cot_ref),
        (w_gate_hbm, w_gate_ref),
    ]
    copies = [
        pltpu.make_async_copy(source, target, sems.at[n])
        for n, (source, target) in enumerate(copies)
    ]
    for copy in copies:
        copy.start()
    for copy in copies[:8]:
        copy.wait()
    gain, bias = column(norm_s[0]), column(norm_s[1])
    gain_ref[...] = gain
    gain = jnp.concatenate([gain, gain], axis=1)
    bias = jnp.concatenate([bias, bias], axis=1)
    for side in range(2):
        rows_s[side * TILES : (side + 1) * TILES] = mask_rows(mask_s[side * 32 : side * 32 + 32])
    mask_ref[...] = rows_s[pl.ds(pl.multiple_of(ch * TILES, TILES), TILES)]
    w = w_s[...]
    for part in range(2):
        if part == 1:
            for copy in copies[8:12]:
                copy.wait()
        start = own if part == 0 else other
        row = start // 2
        for q in range(0, TILES, 2):
            zhat, inverse = norm_over_rows(pair_tiles(pair_s, start, q))
            normed = (zhat * gain + bias).astype(bf16)
            if part == 0:
                lanes = slice(q * 128, (q + 2) * 128)
                zhat_ref[:, lanes] = zhat
                inverse_ref[q : q + 1] = inverse[:, :128]
                inverse_ref[q + 1 : q + 2] = inverse[:, 128:]
                normed_ref[:, lanes] = normed
            y = matmul(w, normed)
            m = mask_pair(rows_s, row + q)
            store_tiles(send_s, row + q, 64, m * sigmoid(y[64:128]) * y[:64])
            store_tiles(send_s, row + 32 + q, 64, m * sigmoid(y[192:]) * y[128:192])
    send_ref[...] = send_s[...].astype(bf16).reshape(64, 64, 128)
    packed_ref[:256] = w.astype(f32)
    packed_ref[256:320] = w_out_s[...].astype(f32)
    norms = jnp.concatenate([out_gain_s[...], out_bias_s[...]], axis=1)
    packed_ref[320:] = jnp.broadcast_to(norms, (8, 128))
    for copy in copies[12:]:
        copy.wait()


def triangle_kernel(blocks_ref, send_ref, left_ref, right_ref):
    load_matrix(blocks_ref.at[:, :, 0], left_ref)
    load_matrix(blocks_ref.at[:, :, 1], right_ref)
    tri = matmul_nt(left_ref[...], right_ref[...]).astype(bf16)
    store_matrix(tri, send_ref, 0)


def middle_kernel(
    tri_ref, normed_ref, cot_ref, w_gate_ref, own_ref, other_ref,
    send_ref, gpre_ref, early_ref, tri_s, d_tri_s, tnorm_s, d_proj_s,
):
    ch = lax.axis_index("ch")
    is_first = ch == 0
    for side in range(2):
        tri_s[side * 1024 : (side + 1) * 1024] = tri_ref[:, side].astype(f32).reshape(1024, 128)
    w_out = both_halves(is_first, own_ref, other_ref, 256, 64)
    w_out_t = w_out.T.astype(bf16)
    w_out = w_out.astype(bf16)
    w_gate_t = w_gate_ref[...].astype(f32).T.astype(bf16)
    own_col, other_col = column(own_ref[320:321]), column(other_ref[320:321])
    low = jnp.where(is_first, own_col, other_col)
    high = jnp.where(is_first, other_col, own_col)
    gain = jnp.concatenate([low[:64], high[:64]], axis=0)
    bias = jnp.concatenate([low[64:], high[64:]], axis=0)
    gain = jnp.concatenate([gain, gain], axis=1)
    bias = jnp.concatenate([bias, bias], axis=1)
    gain_sum = jnp.zeros((128, 256), f32)
    bias_sum = jnp.zeros((128, 256), f32)
    for q in range(0, TILES, 2):
        lanes = slice(q * 128, (q + 2) * 128)
        that, inverse = norm_over_rows(load_tiles(tri_s, q, TILES))
        tnorm = (that * gain + bias).astype(bf16)
        tnorm_s[:, lanes] = tnorm
        proj = matmul(w_out_t, tnorm)
        gate = sigmoid(matmul(w_gate_t, normed_ref[:, lanes]))
        cot = pair_tiles(cot_ref, 0, q)
        gated = cot * gate
        d_proj = gated.astype(bf16)
        d_proj_s[:, lanes] = d_proj
        gpre_ref[:, lanes] = (gated * proj * (1.0 - gate)).astype(bf16)
        d_tnorm = matmul(w_out, d_proj)
        gain_sum = gain_sum + d_tnorm * that
        bias_sum = bias_sum + d_tnorm
        dth = d_tnorm * gain
        d_tri = (
            dth
            - jnp.mean(dth, axis=0, keepdims=True)
            - that * jnp.mean(dth * that, axis=0, keepdims=True)
        ) * inverse
        store_tiles(d_tri_s, q, TILES, d_tri)
    for side in range(2):
        part = d_tri_s[side * 1024 : (side + 1) * 1024]
        send_ref[:, side] = part.astype(bf16).reshape(64, TILES, 128)
    early_ref[0] = matmul_nt(d_proj_s[...], tnorm_s[...])
    early_ref[1] = matmul_nt(normed_ref[...], gpre_ref[...])
    early_ref[2] = jnp.broadcast_to(jnp.sum(gain_sum, axis=1, keepdims=True), (128, 128))
    early_ref[3] = jnp.broadcast_to(jnp.sum(bias_sum, axis=1, keepdims=True), (128, 128))


def back_kernel(blocks_ref, left_ref, right_ref, send_ref, d_tri_s):
    load_matrix(blocks_ref, d_tri_s)
    d_tri = d_tri_s[...]
    store_matrix(matmul(d_tri, right_ref[...]).astype(bf16), send_ref, 0)
    store_matrix(matmul_tn(d_tri, left_ref[...]).astype(bf16), send_ref, 16)


def last_kernel(
    d_ref, mask_ref, normed_ref, zhat_ref, inverse_ref, gpre_ref, own_ref, other_ref, w_gate_ref, gain_ref,
    early_ref, d_pair_ref, d_own_ref, send_ref, d_s, delta_s, grads_s, sems,
):
    ch = lax.axis_index("ch")
    is_first = ch == 0
    for side in range(2):
        d_s[side * 2048 : (side + 1) * 2048] = d_ref[:, side].astype(f32).reshape(2048, 128)
    weights = [both_halves(is_first, own_ref, other_ref, n * 64, 64) for n in range(4)]
    w = jnp.concatenate(weights, axis=0).astype(bf16)
    w_back = jnp.concatenate([x.T.astype(bf16) for x in weights] + [w_gate_ref[...]], axis=1)
    gain = jnp.concatenate([gain_ref[...]] * 2, axis=1)
    gain_sum = jnp.zeros((128, 256), f32)
    bias_sum = jnp.zeros((128, 256), f32)
    delta_s[512:] = gpre_ref[...]
    for q in range(0, TILES, 2):
        lanes = slice(q * 128, (q + 2) * 128)
        y = matmul(w, normed_ref[:, lanes])
        m = mask_pair(mask_ref, q)
        for side in range(2):
            d_full = load_tiles(d_s, side * TILES + q, 2 * TILES) * m
            lin = y[side * 256 : side * 256 + 128]
            sig = sigmoid(y[side * 256 + 128 : side * 256 + 256])
            d_lin = d_full * sig
            delta_s[side * 256 : side * 256 + 128, lanes] = d_lin.astype(bf16)
            delta_s[side * 256 + 128 : side * 256 + 256, lanes] = (
                d_lin * lin * (1.0 - sig)
            ).astype(bf16)
        d_normed = matmul(w_back, delta_s[:, lanes])
        zhat = zhat_ref[:, lanes]
        gain_sum = gain_sum + d_normed * zhat
        bias_sum = bias_sum + d_normed
        dzh = d_normed * gain
        d_pair = (
            dzh
            - jnp.mean(dzh, axis=0, keepdims=True)
            - zhat * jnp.mean(dzh * zhat, axis=0, keepdims=True)
        ) * mask_pair(inverse_ref, q)
        for n in range(2):
            rows = d_pair[:, n * 128 : (n + 1) * 128].T
            d_own_ref[q + n] = rows[:64]
            d_own_ref[TILES + q + n] = rows[64:]
    copy = pltpu.make_async_copy(d_own_ref, d_pair_ref.at[pl.ds(ch * 32, 32)], sems.at[0])
    copy.start()
    grads = matmul_nt(normed_ref[...], delta_s[:512])
    for n in range(4):
        grads_s[pl.ds(n, 128, stride=8)] = grads[:, n * 128 : (n + 1) * 128]
    grads_s[pl.ds(4, 128, stride=8)] = early_ref[0]
    grads_s[pl.ds(5, 128, stride=8)] = early_ref[1]
    lane = lax.broadcasted_iota(jnp.int32, (128, 128), 1)
    sums = jnp.where(
        lane < 64,
        jnp.where(
            lane < 32,
            jnp.sum(gain_sum, axis=1, keepdims=True),
            jnp.sum(bias_sum, axis=1, keepdims=True),
        ),
        jnp.where(lane < 96, early_ref[2], early_ref[3]),
    )
    grads_s[pl.ds(6, 128, stride=8)] = sums
    grads_s[pl.ds(7, 128, stride=8)] = jnp.zeros((128, 128), f32)
    send_ref[...] = grads_s[...].reshape(128, 8, 128).astype(bf16)
    copy.wait()


def sum_kernel(grads_ref, send_ref):
    total = jnp.sum(grads_ref[...].astype(f32), axis=0)
    send_ref[...] = jnp.broadcast_to(total.astype(bf16)[None], (128, 8, 128))


def end_kernel(
    grads_ref, other_ref, _,
    d_pair_ref, gain_ref, bias_ref, left_ref, left_gate_ref, right_ref, right_gate_ref, gate_ref,
    out_gain_ref, out_bias_ref, out_ref, grads_s, sems,
):
    ch = lax.axis_index("ch")
    is_first = ch == 0
    copy = pltpu.make_async_copy(other_ref, d_pair_ref.at[pl.ds(32 - ch * 32, 32)], sems.at[0])
    copy.start()
    grads_s[...] = grads_ref[...].astype(f32).reshape(1024, 128)
    for n, ref in enumerate((left_ref, left_gate_ref, right_ref, right_gate_ref, out_ref)):
        whole = grads_s[pl.ds(n, 128, stride=8)].T
        ref[...] = jnp.where(is_first, whole[:64], whole[64:])
    gate_ref[...] = grads_s[pl.ds(5, 128, stride=8)]
    sums = grads_s[pl.ds(6, 128, stride=8)].T
    gain_ref[...] = sums[0:1]
    bias_ref[...] = sums[32:33]
    out_gain_ref[...] = jnp.where(is_first, sums[64:65, :64], sums[64:65, 64:])
    out_bias_ref[...] = jnp.where(is_first, sums[96:97, :64], sums[96:97, 64:])
    copy.wait()


VMEM = pl.BlockSpec(memory_space=pltpu.VMEM)
HBM = pl.BlockSpec(memory_space=pltpu.HBM)


def call(kernel, out_shapes, scratch, *args, in_specs=None, out_specs=None, aliases=None):
    return pl.pallas_call(
        kernel,
        out_shape=[jax.ShapeDtypeStruct(s, t) for s, t in out_shapes],
        in_specs=in_specs or [VMEM] * len(args),
        out_specs=out_specs or [VMEM] * len(out_shapes),
        scratch_shapes=scratch,
        input_output_aliases=aliases or {},
        compiler_params=pltpu.CompilerParams(vmem_limit_bytes=VMEM_LIMIT),
    )(*args)


def to_all(x):
    return lax.all_to_all(x, ALL, 0, 0, tiled=True)


def body(
    pair, cotangent, pair_mask, norm_gain, norm_bias, w_left, w_left_gate, w_right, w_right_gate,
    w_out_gate, out_norm_gain, out_norm_bias, w_out,
):
    pairs = 128 * TILES
    swap = [(0, 1), (1, 0)]
    with jax.named_scope("first"):
        inputs = (
            pair, pair_mask, norm_gain[None], norm_bias[None], w_left.T, w_left_gate.T, w_right.T,
            w_right_gate.T, w_out, out_norm_gain[None], out_norm_bias[None], cotangent, w_out_gate,
        )
        inputs = [pltpu.with_memory_space_constraint(x, pltpu.HBM) for x in inputs]
        send, normed, zhat, inverse, mask, gain, packed, cot, w_gate = call(
            first_kernel,
            [
                ((64, 64, 128), bf16),
                ((128, pairs), bf16),
                ((128, pairs), f32),
                ((TILES, 128), f32),
                ((TILES, 128), f32),
                ((128, 128), f32),
                ((328, 128), f32),
                ((32, 64, 128), bf16),
                ((128, 128), bf16),
            ],
            [
                pltpu.VMEM((64, 64, 128), bf16),
                pltpu.VMEM((64, 64), jnp.int32),
                pltpu.VMEM((2, 1, 128), f32),
                pltpu.VMEM((256, 128), bf16),
                pltpu.VMEM((64, 128), bf16),
                pltpu.VMEM((1, 64), f32),
                pltpu.VMEM((1, 64), f32),
                pltpu.VMEM((2 * TILES, 128), f32),
                pltpu.VMEM((64 * 64, 128), f32),
                pltpu.SemaphoreType.DMA((14,)),
            ],
            *inputs,
            in_specs=[HBM] * 13,
        )
    with jax.named_scope("weights"):
        other = lax.ppermute(packed, "ch", swap)
    with jax.named_scope("left_right"):
        blocks = lax.all_to_all(send, ("row", "col"), 0, 0, tiled=True)
    with jax.named_scope("triangle"):
        send, left, right = call(
            triangle_kernel,
            [((8, 8, 2, TILES, 128), bf16), ((512, 512), bf16), ((512, 512), bf16)],
            [],
            blocks.reshape(8, 8, 2, 2, TILES, 128),
        )
    with jax.named_scope("tri"):
        tri = to_all(send.reshape(128, TILES, 128))
    with jax.named_scope("middle"):
        send, gpre, early = call(
            middle_kernel,
            [((64, 2, TILES, 128), bf16), ((128, pairs), bf16), ((4, 128, 128), f32)],
            [
                pltpu.VMEM((pairs, 128), f32),
                pltpu.VMEM((pairs, 128), f32),
                pltpu.VMEM((128, pairs), bf16),
                pltpu.VMEM((128, pairs), bf16),
            ],
            tri.reshape(64, 2, TILES, 128), normed, cot, w_gate, packed, other,
        )
    with jax.named_scope("d_tri"):
        blocks = to_all(send.reshape(128, TILES, 128))
    with jax.named_scope("back"):
        (send,) = call(
            back_kernel,
            [((8, 8, 2, 2 * TILES, 128), bf16)],
            [pltpu.VMEM((512, 512), bf16)],
            blocks.reshape(8, 8, 2, TILES, 128), left, right,
        )
    with jax.named_scope("d_left_right"):
        d_full = to_all(send.reshape(128, 2 * TILES, 128))
    with jax.named_scope("last"):
        d_pair, d_own, send = call(
            last_kernel,
            [((64, 64, 128), f32), ((32, 64, 128), f32), ((128, 8, 128), bf16)],
            [
                pltpu.VMEM((2 * pairs, 128), f32),
                pltpu.VMEM((640, pairs), bf16),
                pltpu.VMEM((1024, 128), f32),
                pltpu.SemaphoreType.DMA((1,)),
            ],
            d_full.reshape(64, 2, 2 * TILES, 128), mask, normed, zhat, inverse, gpre, packed, other,
            w_gate, gain, early,
            out_specs=[HBM, VMEM, VMEM],
        )
    with jax.named_scope("d_pair"):
        d_other = lax.ppermute(d_own, "ch", swap)
    with jax.named_scope("grads"):
        parts = to_all(send)
        (send,) = call(sum_kernel, [((128, 8, 128), bf16)], [], parts)
        parts = to_all(send)
    with jax.named_scope("end"):
        shapes = [
            ((64, 64, 128), f32), ((1, 128), f32), ((1, 128), f32), ((64, 128), f32), ((64, 128), f32),
            ((64, 128), f32), ((64, 128), f32), ((128, 128), f32), ((1, 64), f32), ((1, 64), f32),
            ((64, 128), f32),
        ]
        d_pair, gain, bias, left, left_gate, right, right_gate, gate, out_gain, out_bias, out = call(
            end_kernel,
            shapes,
            [pltpu.VMEM((1024, 128), f32), pltpu.SemaphoreType.DMA((1,))],
            parts, d_other, d_pair,
            in_specs=[VMEM, VMEM, HBM],
            out_specs=[HBM] + [VMEM] * 10,
            aliases={2: 0},
        )
    return (
        d_pair, gain[0], bias[0], left.T, left_gate.T, right.T, right_gate.T, gate, out_gain[0],
        out_bias[0], out,
    )


def solution(mesh):
    placed = (
        P("row", "col", None), P("row", "col", None), P("row", "col"), P(), P(), P(None, "ch"),
        P(None, "ch"), P(None, "ch"), P(None, "ch"), P(), P("ch"), P("ch"), P("ch", None),
    )
    return jax.shard_map(
        body,
        mesh=mesh,
        in_specs=placed,
        out_specs=(
            P("row", "col", None), P(), P(), P(None, "ch"), P(None, "ch"), P(None, "ch"),
            P(None, "ch"), P(), P("ch"), P("ch"), P("ch", None),
        ),
        check_vma=False,
    )
```

```python
import jax
import jax.numpy as jnp
from jax import lax
from jax.experimental import pallas as pl
from jax.experimental.pallas import tpu as pltpu
from jax.sharding import PartitionSpec as P

f32 = jnp.float32
bf16 = jnp.bfloat16
ALL = ("row", "col", "ch")
TILES = 16
EPS = 1e-05
VMEM_LIMIT = 10 * 1024 * 1024


def matmul(a, b):
    return lax.dot_general(a, b, (((1,), (0,)), ((), ())), preferred_element_type=f32)


def matmul_nt(a, b):
    return lax.dot_general(a, b, (((1,), (1,)), ((), ())), preferred_element_type=f32)


def matmul_tn(a, b):
    return lax.dot_general(a, b, (((0,), (0,)), ((), ())), preferred_element_type=f32)


def sigmoid(x):
    return 0.5 * jnp.tanh(0.5 * x) + 0.5


def column(row):
    return jnp.broadcast_to(row, (128, 128)).T


def norm_over_rows(x):
    mean = jnp.mean(x, axis=0, keepdims=True)
    centred = x - mean
    inverse = lax.rsqrt(jnp.mean(centred * centred, axis=0, keepdims=True) + EPS)
    return centred * inverse, inverse


def pair_tiles(ref, start, q):
    tiles = [
        jnp.concatenate([ref[start + q + n], ref[start + TILES + q + n]], axis=0).T.astype(f32)
        for n in range(2)
    ]
    return jnp.concatenate(tiles, axis=1)


def mask_rows(mask):
    return jnp.concatenate([mask[:TILES], mask[TILES:]], axis=1).astype(f32)


def mask_pair(rows, start):
    return jnp.concatenate([rows[pl.ds(start, 1)], rows[pl.ds(start + 1, 1)]], axis=1)


def store_rows(ref, row, value):
    rows, block, _ = ref.shape
    ref.reshape(rows * block, 128)[pl.ds(row, rows, stride=block)] = value


def load_rows(ref, row):
    rows, block, _ = ref.shape
    return ref.reshape(rows * block, 128)[pl.ds(row, rows, stride=block)]


def store_tiles(ref, row, value):
    store_rows(ref, row, value[:, :128])
    store_rows(ref, row + 1, value[:, 128:])


def load_tiles(ref, row):
    return jnp.concatenate([load_rows(ref, row + n) for n in range(2)], axis=1)


def both_halves(is_first, own_ref, other_ref, start, count):
    own, other = own_ref[start : start + count], other_ref[start : start + count]
    return jnp.concatenate(
        [jnp.where(is_first, own, other), jnp.where(is_first, other, own)], axis=0
    )


def exchange(a, b):
    return (
        jnp.concatenate([a[..., :64], b[..., :64]], axis=-1),
        jnp.concatenate([a[..., 64:], b[..., 64:]], axis=-1),
    )


def load_matrix(blocks, out):
    for pair in range(4):
        low, high = exchange(blocks[:, 2 * pair], blocks[:, 2 * pair + 1])
        out[:, pair * 128 : (pair + 1) * 128] = jnp.stack([low, high], axis=2).reshape(512, 128)


def store_matrix(matrix, blocks, at):
    for pair in range(4):
        part = matrix[:, pair * 128 : (pair + 1) * 128].reshape(8, 2, 2, 16, 128)
        first, second = exchange(part[:, :, 0], part[:, :, 1])
        blocks[:, 2 * pair, :, at : at + 16, :] = first
        blocks[:, 2 * pair + 1, :, at : at + 16, :] = second


def start_copies(sems, *pairs):
    copies = [
        pltpu.make_async_copy(source, target, sems.at[n]) for n, (source, target) in enumerate(pairs)
    ]
    for copy in copies:
        copy.start()
    return copies


def first_kernel(
    pair_hbm, mask_hbm, gain_hbm, bias_hbm, left_hbm, left_gate_hbm, right_hbm, right_gate_hbm,
    w_out_hbm, out_gain_hbm, out_bias_hbm, cot_hbm, w_gate_hbm,
    send_ref, stack_ref, mask_ref, packed_ref, cot_ref, w_gate_ref,
    zhat_hbm, inverse_hbm, gain_out_hbm, zhat_ref, inverse_ref, gain_ref,
    pair_s, mask_s, norm_s, w_s, w_out_s, out_gain_s, out_bias_s, rows_s, send_s, sems, out_sems,
):
    ch = lax.axis_index("ch")
    own, other = ch * 32, 32 - ch * 32
    copies = start_copies(
        sems,
        (gain_hbm, norm_s.at[0]),
        (bias_hbm, norm_s.at[1]),
        (left_hbm, w_s.at[0:64]),
        (left_gate_hbm, w_s.at[64:128]),
        (right_hbm, w_s.at[128:192]),
        (right_gate_hbm, w_s.at[192:256]),
        (mask_hbm, mask_s),
        (pair_hbm.at[pl.ds(own, 32)], pair_s.at[pl.ds(own, 32)]),
        (w_out_hbm, w_out_s),
        (out_gain_hbm, out_gain_s),
        (out_bias_hbm, out_bias_s),
        (pair_hbm.at[pl.ds(other, 32)], pair_s.at[pl.ds(other, 32)]),
        (cot_hbm.at[pl.ds(own, 32)], cot_ref),
        (w_gate_hbm, w_gate_ref),
    )
    for copy in copies[:8]:
        copy.wait()
    gain, bias = column(norm_s[0]), column(norm_s[1])
    gain_ref[...] = gain
    gain = jnp.concatenate([gain, gain], axis=1)
    bias = jnp.concatenate([bias, bias], axis=1)
    for side in range(2):
        rows_s[side * TILES : (side + 1) * TILES] = mask_rows(mask_s[side * 32 : side * 32 + 32])
    mask_ref[...] = rows_s[pl.ds(pl.multiple_of(ch * TILES, TILES), TILES)]
    w = w_s[...]
    for part in range(2):
        if part == 1:
            for copy in copies[8:12]:
                copy.wait()
            packed_ref[:256] = w.astype(f32)
            packed_ref[256:320] = w_out_s[...].astype(f32)
            norms = jnp.concatenate([out_gain_s[...], out_bias_s[...]], axis=1)
            packed_ref[320:] = jnp.broadcast_to(norms, (8, 128))
            results = start_copies(
                out_sems, (zhat_ref, zhat_hbm), (inverse_ref, inverse_hbm), (gain_ref, gain_out_hbm)
            )
        start = own if part == 0 else other
        row = start // 2
        for q in range(0, TILES, 2):
            zhat, inverse = norm_over_rows(pair_tiles(pair_s, start, q))
            normed = (zhat * gain + bias).astype(bf16)
            if part == 0:
                lanes = slice(q * 128, (q + 2) * 128)
                zhat_ref[:, lanes] = zhat
                inverse_ref[q : q + 1] = inverse[:, :128]
                inverse_ref[q + 1 : q + 2] = inverse[:, 128:]
                stack_ref[:128, lanes] = normed
                stack_ref[128:, lanes] = zhat.astype(bf16)
            y = matmul(w, normed)
            m = mask_pair(rows_s, row + q)
            store_tiles(send_s, row + q, m * sigmoid(y[64:128]) * y[:64])
            store_tiles(send_s, row + 32 + q, m * sigmoid(y[192:]) * y[128:192])
    send_ref[...] = send_s[:, :64].astype(bf16)
    for copy in copies[12:] + results:
        copy.wait()


def triangle_kernel(blocks_ref, send_ref, left_ref, right_ref):
    load_matrix(blocks_ref.at[:, :, 0], left_ref)
    load_matrix(blocks_ref.at[:, :, 1], right_ref)
    tri = matmul_nt(left_ref[...], right_ref[...]).astype(bf16)
    store_matrix(tri, send_ref, 0)


def middle_kernel(
    tri_ref, stack_ref, cot_ref, w_gate_ref, own_ref, other_ref,
    send_ref, gpre_ref, early_ref, tri_s, d_tri_s, tnorm_s, d_proj_s,
):
    is_first = lax.axis_index("ch") == 0
    for side in range(2):
        tri_s[side * 64 : (side + 1) * 64, :TILES] = tri_ref[:, side].astype(f32)
    w_out = both_halves(is_first, own_ref, other_ref, 256, 64)
    w_out_t = w_out.T.astype(bf16)
    w_out = w_out.astype(bf16)
    w_gate_t = w_gate_ref[...].astype(f32).T.astype(bf16)
    own_col, other_col = column(own_ref[320:321]), column(other_ref[320:321])
    low = jnp.where(is_first, own_col, other_col)
    high = jnp.where(is_first, other_col, own_col)
    gain = jnp.concatenate([low[:64], high[:64]], axis=0)
    bias = jnp.concatenate([low[64:], high[64:]], axis=0)
    gain = jnp.concatenate([gain, gain], axis=1)
    bias = jnp.concatenate([bias, bias], axis=1)
    gain_sum = jnp.zeros((128, 256), f32)
    bias_sum = jnp.zeros((128, 256), f32)
    gpre_sum = jnp.zeros((128, 256), f32)
    for q in range(0, TILES, 2):
        lanes = slice(q * 128, (q + 2) * 128)
        that, inverse = norm_over_rows(load_tiles(tri_s, q))
        tnorm = (that * gain + bias).astype(bf16)
        tnorm_s[:, lanes] = tnorm
        proj = matmul(w_out_t, tnorm)
        gate = sigmoid(matmul(w_gate_t, stack_ref[:128, lanes]))
        gated = pair_tiles(cot_ref, 0, q) * gate
        d_proj = gated.astype(bf16)
        d_proj_s[:, lanes] = d_proj
        d_gpre = gated * proj * (1.0 - gate)
        gpre_ref[:, lanes] = d_gpre.astype(bf16)
        gpre_sum = gpre_sum + d_gpre
        d_tnorm = matmul(w_out, d_proj)
        gain_sum = gain_sum + d_tnorm * that
        bias_sum = bias_sum + d_tnorm
        dth = d_tnorm * gain
        d_tri = (
            dth
            - jnp.mean(dth, axis=0, keepdims=True)
            - that * jnp.mean(dth * that, axis=0, keepdims=True)
        ) * inverse
        store_tiles(d_tri_s, q, d_tri)
    for side in range(2):
        send_ref[:, side] = d_tri_s[side * 64 : (side + 1) * 64, :TILES].astype(bf16)
    early_ref[0] = matmul_nt(tnorm_s[...], d_proj_s[...])
    early_ref[1] = gain_sum[:, :128] + gain_sum[:, 128:]
    early_ref[2] = bias_sum[:, :128] + bias_sum[:, 128:]
    early_ref[3] = gpre_sum[:, :128] + gpre_sum[:, 128:]


def back_kernel(blocks_ref, left_ref, right_ref, send_ref, d_tri_s):
    load_matrix(blocks_ref, d_tri_s)
    d_tri = d_tri_s[...]
    store_matrix(matmul(d_tri, right_ref[...]).astype(bf16), send_ref, 0)
    store_matrix(matmul_tn(d_tri, left_ref[...]).astype(bf16), send_ref, 16)


def grads_kernel(
    d_ref, mask_ref, stack_ref, gpre_ref, own_ref, other_ref, w_gate_ref, early_ref,
    delta_hbm, w_back_hbm, send_ref, delta_ref, w_back_ref, d_s, grads_s, sems,
):
    is_first = lax.axis_index("ch") == 0
    for side in range(2):
        d_s[side * 64 : (side + 1) * 64, :32] = d_ref[:, side].astype(f32)
    weights = [both_halves(is_first, own_ref, other_ref, n * 64, 64) for n in range(4)]
    w = jnp.concatenate(weights, axis=0).astype(bf16)
    for n in range(4):
        w_back_ref[:, n * 128 : (n + 1) * 128] = weights[n].T.astype(bf16)
    w_back_ref[:, 512:] = w_gate_ref[...]
    w_back_copy = pltpu.make_async_copy(w_back_ref, w_back_hbm, sems.at[1])
    w_back_copy.start()
    delta_ref[512:] = gpre_ref[...]
    delta_sums = [jnp.zeros((128, 256), f32)] * 4
    for q in range(0, TILES, 2):
        lanes = slice(q * 128, (q + 2) * 128)
        y = matmul(w, stack_ref[:128, lanes])
        m = mask_pair(mask_ref, q)
        for side in range(2):
            lin = y[side * 256 : side * 256 + 128]
            sig = sigmoid(y[side * 256 + 128 : side * 256 + 256])
            d_lin = load_tiles(d_s, side * TILES + q) * m * sig
            d_gate = d_lin * lin * (1.0 - sig)
            for n, d in ((2 * side, d_lin), (2 * side + 1, d_gate)):
                delta_ref[n * 128 : (n + 1) * 128, lanes] = d.astype(bf16)
                delta_sums[n] = delta_sums[n] + d
    copy = pltpu.make_async_copy(delta_ref, delta_hbm, sems.at[0])
    copy.start()
    grads = matmul_nt(delta_ref[...], stack_ref[...])
    for n in range(4):
        store_rows(grads_s, n, grads[n * 128 : (n + 1) * 128, :128])
    store_rows(grads_s, 4, early_ref[0])
    store_rows(grads_s, 5, grads[512:, :128])
    gain_sum = jnp.zeros((128, 128), f32)
    bias_sum = jnp.zeros((128, 128), f32)
    delta_sums = [d[:, :128] + d[:, 128:] for d in delta_sums] + [early_ref[3]]
    weights.append(w_gate_ref[...].astype(f32).T)
    for n in range(5):
        gain_sum = gain_sum + weights[n] * grads[n * 128 : (n + 1) * 128, 128:]
        bias_sum = bias_sum + weights[n] * jnp.sum(delta_sums[n], axis=1, keepdims=True)
    sums = (
        column(jnp.sum(gain_sum, axis=0, keepdims=True)),
        column(jnp.sum(bias_sum, axis=0, keepdims=True)),
        jnp.sum(early_ref[1], axis=1, keepdims=True),
        jnp.sum(early_ref[2], axis=1, keepdims=True),
    )
    lane = lax.broadcasted_iota(jnp.int32, (128, 128), 1)
    store_rows(
        grads_s,
        6,
        jnp.where(
            lane < 64, jnp.where(lane < 32, sums[0], sums[1]), jnp.where(lane < 96, sums[2], sums[3])
        ),
    )
    store_rows(grads_s, 7, jnp.zeros((128, 128), f32))
    send_ref[...] = grads_s[...].astype(bf16)
    w_back_copy.wait()
    copy.wait()


def pair_kernel(
    delta_hbm, w_back_hbm, zhat_hbm, inverse_hbm, gain_hbm, d_pair_hbm, d_own_hbm,
    delta_ref, w_back_ref, zhat_ref, inverse_ref, gain_ref, d_own_ref, sems,
):
    ch = lax.axis_index("ch")
    copies = start_copies(
        sems,
        (delta_hbm, delta_ref),
        (w_back_hbm, w_back_ref),
        (zhat_hbm, zhat_ref),
        (inverse_hbm, inverse_ref),
        (gain_hbm, gain_ref),
    )
    for copy in copies:
        copy.wait()
    gain = jnp.concatenate([gain_ref[...]] * 2, axis=1)
    w_back = w_back_ref[...]
    for q in range(0, TILES, 2):
        lanes = slice(q * 128, (q + 2) * 128)
        zhat = zhat_ref[:, lanes]
        dzh = matmul(w_back, delta_ref[:, lanes]) * gain
        d_pair = (
            dzh
            - jnp.mean(dzh, axis=0, keepdims=True)
            - zhat * jnp.mean(dzh * zhat, axis=0, keepdims=True)
        ) * mask_pair(inverse_ref, q)
        for n in range(2):
            rows = d_pair[:, n * 128 : (n + 1) * 128].T
            d_own_ref[q + n] = rows[:64]
            d_own_ref[TILES + q + n] = rows[64:]
    copies = start_copies(
        sems, (d_own_ref, d_pair_hbm.at[pl.ds(ch * 32, 32)]), (d_own_ref, d_own_hbm)
    )
    for copy in copies:
        copy.wait()


def sum_kernel(grads_ref, send_ref):
    total = jnp.sum(grads_ref[...].astype(f32), axis=0)
    send_ref[...] = jnp.broadcast_to(total.astype(bf16)[None], (128, 8, 128))


def place_kernel(other_ref, _, d_pair_ref, sems):
    ch = lax.axis_index("ch")
    copy = pltpu.make_async_copy(other_ref, d_pair_ref.at[pl.ds(32 - ch * 32, 32)], sems.at[0])
    copy.start()
    copy.wait()


def end_kernel(
    grads_ref,
    gain_ref, bias_ref, left_ref, left_gate_ref, right_ref, right_gate_ref, gate_ref,
    out_gain_ref, out_bias_ref, out_ref, grads_s,
):
    is_first = lax.axis_index("ch") == 0
    grads_s[...] = grads_ref[...].astype(f32)
    for n, ref in enumerate((left_ref, left_gate_ref, right_ref, right_gate_ref, out_ref)):
        whole = load_rows(grads_s, n)
        ref[...] = jnp.where(is_first, whole[:64], whole[64:])
    gate_ref[...] = load_rows(grads_s, 5).T
    sums = load_rows(grads_s, 6).T
    gain_ref[...] = sums[0:1]
    bias_ref[...] = sums[32:33]
    out_gain_ref[...] = jnp.where(is_first, sums[64:65, :64], sums[64:65, 64:])
    out_bias_ref[...] = jnp.where(is_first, sums[96:97, :64], sums[96:97, 64:])


VMEM = pl.BlockSpec(memory_space=pltpu.VMEM)
HBM = pl.BlockSpec(memory_space=pltpu.HBM)


def call(kernel, out_shapes, scratch, *args, in_specs=None, out_specs=None, aliases=None, us=None):
    out_specs = out_specs or [VMEM] * len(out_shapes)
    cost = None
    if us is not None:
        cost = pl.CostEstimate(flops=us * 10**9, bytes_accessed=us * 3 * 10**6, transcendentals=0)
    return pl.pallas_call(
        kernel,
        out_shape=[
            pltpu.HBM(s, t) if spec is HBM else jax.ShapeDtypeStruct(s, t)
            for (s, t), spec in zip(out_shapes, out_specs)
        ],
        in_specs=in_specs or [VMEM] * len(args),
        out_specs=out_specs,
        scratch_shapes=scratch,
        input_output_aliases=aliases or {},
        cost_estimate=cost,
        compiler_params=pltpu.CompilerParams(vmem_limit_bytes=VMEM_LIMIT),
    )(*args)


def in_hbm(*arrays):
    return [pltpu.with_memory_space_constraint(x, pltpu.HBM) for x in arrays]


def to_all(x):
    return lax.all_to_all(x, ALL, 0, 0, tiled=True)


def body(
    pair, cotangent, pair_mask, norm_gain, norm_bias, w_left, w_left_gate, w_right, w_right_gate,
    w_out_gate, out_norm_gain, out_norm_bias, w_out,
):
    pairs = 128 * TILES
    swap = [(0, 1), (1, 0)]
    with jax.named_scope("first"):
        send, stack, mask, packed, cot, w_gate, zhat, inverse, gain = call(
            first_kernel,
            [
                ((64, 64, 128), bf16),
                ((256, pairs), bf16),
                ((TILES, 128), f32),
                ((328, 128), f32),
                ((32, 64, 128), bf16),
                ((128, 128), bf16),
                ((128, pairs), f32),
                ((TILES, 128), f32),
                ((128, 128), f32),
            ],
            [
                pltpu.VMEM((128, pairs), f32),
                pltpu.VMEM((TILES, 128), f32),
                pltpu.VMEM((128, 128), f32),
                pltpu.VMEM((64, 64, 128), bf16),
                pltpu.VMEM((64, 64), jnp.int32),
                pltpu.VMEM((2, 1, 128), f32),
                pltpu.VMEM((256, 128), bf16),
                pltpu.VMEM((64, 128), bf16),
                pltpu.VMEM((1, 64), f32),
                pltpu.VMEM((1, 64), f32),
                pltpu.VMEM((2 * TILES, 128), f32),
                pltpu.VMEM((64, 72, 128), f32),
                pltpu.SemaphoreType.DMA((14,)),
                pltpu.SemaphoreType.DMA((3,)),
            ],
            *in_hbm(
                pair, pair_mask, norm_gain[None], norm_bias[None], w_left.T, w_left_gate.T, w_right.T,
                w_right_gate.T, w_out, out_norm_gain[None], out_norm_bias[None], cotangent, w_out_gate,
            ),
            in_specs=[HBM] * 13,
            out_specs=[VMEM] * 6 + [HBM] * 3,
        )
    with jax.named_scope("left_right"):
        blocks = lax.all_to_all(send, ("row", "col"), 0, 0, tiled=True)
    with jax.named_scope("weights"):
        blocks, own = lax.optimization_barrier((blocks, packed))
        other = lax.ppermute(own, "ch", swap)
    with jax.named_scope("triangle"):
        send, left, right = call(
            triangle_kernel,
            [((8, 8, 2, TILES, 128), bf16), ((512, 512), bf16), ((512, 512), bf16)],
            [],
            blocks.reshape(8, 8, 2, 2, TILES, 128),
        )
    with jax.named_scope("tri"):
        send, other = lax.optimization_barrier((send, other))
        tri = to_all(send.reshape(128, TILES, 128))
    with jax.named_scope("middle"):
        send, gpre, early = call(
            middle_kernel,
            [((64, 2, TILES, 128), bf16), ((128, pairs), bf16), ((4, 128, 128), f32)],
            [
                pltpu.VMEM((128, 24, 128), f32),
                pltpu.VMEM((128, 24, 128), f32),
                pltpu.VMEM((128, pairs), bf16),
                pltpu.VMEM((128, pairs), bf16),
            ],
            tri.reshape(64, 2, TILES, 128), stack, cot, w_gate, own, other,
        )
    with jax.named_scope("d_tri"):
        blocks = to_all(send.reshape(128, TILES, 128))
    with jax.named_scope("back"):
        (send,) = call(
            back_kernel,
            [((8, 8, 2, 2 * TILES, 128), bf16)],
            [pltpu.VMEM((512, 512), bf16)],
            blocks.reshape(8, 8, 2, TILES, 128), left, right,
        )
    with jax.named_scope("d_left_right"):
        d_full = to_all(send.reshape(128, 2 * TILES, 128))
    with jax.named_scope("grads"):
        delta, w_back, send = call(
            grads_kernel,
            [((640, pairs), bf16), ((128, 640), bf16), ((128, 8, 128), bf16)],
            [
                pltpu.VMEM((640, pairs), bf16),
                pltpu.VMEM((128, 640), bf16),
                pltpu.VMEM((128, 40, 128), f32),
                pltpu.VMEM((128, 8, 128), f32),
                pltpu.SemaphoreType.DMA((2,)),
            ],
            d_full.reshape(64, 2, 2 * TILES, 128), mask, stack, gpre, own, other, w_gate, early,
            out_specs=[HBM, HBM, VMEM],
        )
    with jax.named_scope("sums"):
        parts = to_all(send)
    with jax.named_scope("pair"):
        d_pair, d_own = call(
            pair_kernel,
            [((64, 64, 128), f32), ((32, 64, 128), f32)],
            [
                pltpu.VMEM((640, pairs), bf16),
                pltpu.VMEM((128, 640), bf16),
                pltpu.VMEM((128, pairs), f32),
                pltpu.VMEM((TILES, 128), f32),
                pltpu.VMEM((128, 128), f32),
                pltpu.VMEM((32, 64, 128), f32),
                pltpu.SemaphoreType.DMA((5,)),
            ],
            *in_hbm(delta, w_back, zhat, inverse, gain),
            in_specs=[HBM] * 5,
            out_specs=[HBM, HBM],
            us=4,
        )
        parts, d_own = lax.optimization_barrier((parts, d_own))
        d_other = lax.ppermute(d_own, "ch", swap)
    with jax.named_scope("sums"):
        (send,) = call(sum_kernel, [((128, 8, 128), bf16)], [], parts)
        parts = to_all(send)
    with jax.named_scope("place"):
        (d_pair,) = call(
            place_kernel,
            [((64, 64, 128), f32)],
            [pltpu.SemaphoreType.DMA((1,))],
            d_other, *in_hbm(d_pair),
            in_specs=[VMEM, HBM],
            out_specs=[HBM],
            aliases={1: 0},
            us=1,
        )
        parts, d_pair = lax.optimization_barrier((parts, d_pair))
    with jax.named_scope("end"):
        shapes = [
            ((1, 128), f32), ((1, 128), f32), ((64, 128), f32), ((64, 128), f32), ((64, 128), f32),
            ((64, 128), f32), ((128, 128), f32), ((1, 64), f32), ((1, 64), f32), ((64, 128), f32),
        ]
        gain, bias, left, left_gate, right, right_gate, gate, out_gain, out_bias, out = call(
            end_kernel, shapes, [pltpu.VMEM((128, 8, 128), f32)], parts
        )
    return (
        d_pair, gain[0], bias[0], left.T, left_gate.T, right.T, right_gate.T, gate, out_gain[0],
        out_bias[0], out,
    )


def solution(mesh):
    placed = (
        P("row", "col", None), P("row", "col", None), P("row", "col"), P(), P(), P(None, "ch"),
        P(None, "ch"), P(None, "ch"), P(None, "ch"), P(), P("ch"), P("ch"), P("ch", None),
    )
    return jax.shard_map(
        body,
        mesh=mesh,
        in_specs=placed,
        out_specs=(
            P("row", "col", None), P(), P(), P(None, "ch"), P(None, "ch"), P(None, "ch"),
            P(None, "ch"), P(), P("ch"), P("ch"), P("ch", None),
        ),
        check_vma=False,
    )
```

```python
import jax
import jax.numpy as jnp
from jax import lax
from jax.experimental import pallas as pl
from jax.experimental.pallas import tpu as pltpu
from jax.sharding import PartitionSpec as P

f32 = jnp.float32
bf16 = jnp.bfloat16
ALL = ("row", "col", "ch")
TILES = 16
EPS = 1e-05
VMEM_LIMIT = 10 * 1024 * 1024


def matmul(a, b):
    return lax.dot_general(a, b, (((1,), (0,)), ((), ())), preferred_element_type=f32)


def matmul_nt(a, b):
    return lax.dot_general(a, b, (((1,), (1,)), ((), ())), preferred_element_type=f32)


def matmul_tn(a, b):
    return lax.dot_general(a, b, (((0,), (0,)), ((), ())), preferred_element_type=f32)


def sigmoid(x):
    return 0.5 * jnp.tanh(0.5 * x) + 0.5


def column(row):
    return jnp.broadcast_to(row, (128, 128)).T


def norm_over_rows(x):
    mean = jnp.mean(x, axis=0, keepdims=True)
    centred = x - mean
    inverse = lax.rsqrt(jnp.mean(centred * centred, axis=0, keepdims=True) + EPS)
    return centred * inverse, inverse


def pair_tiles(ref, start, q):
    tiles = [
        jnp.concatenate([ref[start + q + n], ref[start + TILES + q + n]], axis=0).T.astype(f32)
        for n in range(2)
    ]
    return jnp.concatenate(tiles, axis=1)


def mask_rows(mask):
    return jnp.concatenate([mask[:TILES], mask[TILES:]], axis=1).astype(f32)


def mask_pair(rows, start):
    return jnp.concatenate([rows[pl.ds(start, 1)], rows[pl.ds(start + 1, 1)]], axis=1)


def store_rows(ref, row, value):
    rows, block, _ = ref.shape
    ref.reshape(rows * block, 128)[pl.ds(row, rows, stride=block)] = value


def load_rows(ref, row):
    rows, block, _ = ref.shape
    return ref.reshape(rows * block, 128)[pl.ds(row, rows, stride=block)]


def store_tiles(ref, row, value):
    store_rows(ref, row, value[:, :128])
    store_rows(ref, row + 1, value[:, 128:])


def load_tiles(ref, row):
    return jnp.concatenate([load_rows(ref, row + n) for n in range(2)], axis=1)


def both_halves(is_first, own_ref, other_ref, start, count):
    own, other = own_ref[start : start + count], other_ref[start : start + count]
    return jnp.concatenate(
        [jnp.where(is_first, own, other), jnp.where(is_first, other, own)], axis=0
    )


def exchange(a, b):
    return (
        jnp.concatenate([a[..., :64], b[..., :64]], axis=-1),
        jnp.concatenate([a[..., 64:], b[..., 64:]], axis=-1),
    )


def load_matrix(blocks, out):
    for pair in range(4):
        low, high = exchange(blocks[:, 2 * pair], blocks[:, 2 * pair + 1])
        out[:, pair * 128 : (pair + 1) * 128] = jnp.stack([low, high], axis=2).reshape(512, 128)


def store_matrix(matrix, blocks, at):
    for pair in range(4):
        part = matrix[:, pair * 128 : (pair + 1) * 128].reshape(8, 2, 2, 16, 128)
        first, second = exchange(part[:, :, 0], part[:, :, 1])
        blocks[:, 2 * pair, :, at : at + 16, :] = first
        blocks[:, 2 * pair + 1, :, at : at + 16, :] = second


def start_copies(sems, *pairs):
    copies = [
        pltpu.make_async_copy(source, target, sems.at[n]) for n, (source, target) in enumerate(pairs)
    ]
    for copy in copies:
        copy.start()
    return copies


def first_kernel(
    pair_hbm, mask_hbm, gain_hbm, bias_hbm, left_hbm, left_gate_hbm, right_hbm, right_gate_hbm,
    w_out_hbm, out_gain_hbm, out_bias_hbm, cot_hbm, w_gate_hbm,
    send_ref, stack_ref, mask_ref, packed_ref, cot_ref, w_gate_ref,
    zhat_hbm, inverse_hbm, gain_out_hbm, zhat_ref, inverse_ref, gain_ref,
    pair_s, mask_s, norm_s, w_s, w_out_s, out_gain_s, out_bias_s, rows_s, send_s, sems, out_sems,
):
    ch = lax.axis_index("ch")
    own, other = ch * 32, 32 - ch * 32
    copies = start_copies(
        sems,
        (pair_hbm.at[pl.ds(own, 32)], pair_s.at[0:32]),
        (gain_hbm, norm_s.at[0]),
        (bias_hbm, norm_s.at[1]),
        (mask_hbm.at[pl.ds(own, 32)], mask_s.at[0:32]),
        (left_hbm, w_s.at[0:64]),
        (left_gate_hbm, w_s.at[64:128]),
        (right_hbm, w_s.at[128:192]),
        (right_gate_hbm, w_s.at[192:256]),
        (pair_hbm.at[pl.ds(other, 32)], pair_s.at[32:64]),
        (mask_hbm.at[pl.ds(other, 32)], mask_s.at[32:64]),
        (w_out_hbm, w_out_s),
        (out_gain_hbm, out_gain_s),
        (out_bias_hbm, out_bias_s),
        (cot_hbm.at[pl.ds(own, 32)], cot_ref),
        (w_gate_hbm, w_gate_ref),
    )
    for copy in copies[:8]:
        copy.wait()
    gain, bias = column(norm_s[0]), column(norm_s[1])
    gain_ref[...] = gain
    gain = jnp.concatenate([gain, gain], axis=1)
    bias = jnp.concatenate([bias, bias], axis=1)
    rows_s[:TILES] = mask_rows(mask_s[:32])
    mask_ref[...] = rows_s[:TILES]
    w = w_s[...]
    for part in range(2):
        if part == 1:
            for copy in copies[8:13]:
                copy.wait()
            rows_s[TILES:] = mask_rows(mask_s[32:])
            packed_ref[:256] = w.astype(f32)
            packed_ref[256:320] = w_out_s[...].astype(f32)
            norms = jnp.concatenate([out_gain_s[...], out_bias_s[...]], axis=1)
            packed_ref[320:] = jnp.broadcast_to(norms, (8, 128))
            results = start_copies(
                out_sems, (zhat_ref, zhat_hbm), (inverse_ref, inverse_hbm), (gain_ref, gain_out_hbm)
            )
        row = part * TILES
        for q in range(0, TILES, 2):
            zhat, inverse = norm_over_rows(pair_tiles(pair_s, part * 32, q))
            normed = (zhat * gain + bias).astype(bf16)
            if part == 0:
                lanes = slice(q * 128, (q + 2) * 128)
                zhat_ref[:, lanes] = zhat
                inverse_ref[q : q + 1] = inverse[:, :128]
                inverse_ref[q + 1 : q + 2] = inverse[:, 128:]
                stack_ref[:128, lanes] = normed
                stack_ref[128:, lanes] = zhat.astype(bf16)
            y = matmul(w, normed)
            m = mask_pair(rows_s, row + q)
            store_tiles(send_s, row + q, m * sigmoid(y[64:128]) * y[:64])
            store_tiles(send_s, row + 32 + q, m * sigmoid(y[192:]) * y[128:192])
    for part, start in enumerate((own, other)):
        for side in range(2):
            target = pl.ds(pl.multiple_of(start // 2 + side * 32, TILES), TILES)
            row = part * TILES + side * 32
            send_ref[:, target] = send_s[:, row : row + TILES].astype(bf16)
    for copy in copies[13:] + results:
        copy.wait()


def triangle_kernel(blocks_ref, send_ref, left_ref, right_ref):
    load_matrix(blocks_ref.at[:, :, 0], left_ref)
    load_matrix(blocks_ref.at[:, :, 1], right_ref)
    tri = matmul_nt(left_ref[...], right_ref[...]).astype(bf16)
    store_matrix(tri, send_ref, 0)


def middle_kernel(
    tri_ref, stack_ref, cot_ref, w_gate_ref, own_ref, other_ref,
    send_ref, gpre_ref, early_ref, tri_s, d_tri_s, tnorm_s, d_proj_s,
):
    is_first = lax.axis_index("ch") == 0
    for side in range(2):
        tri_s[side * 64 : (side + 1) * 64, :TILES] = tri_ref[:, side].astype(f32)
    w_out = both_halves(is_first, own_ref, other_ref, 256, 64)
    w_out_t = w_out.T.astype(bf16)
    w_out = w_out.astype(bf16)
    w_gate_t = w_gate_ref[...].astype(f32).T.astype(bf16)
    own_col, other_col = column(own_ref[320:321]), column(other_ref[320:321])
    low = jnp.where(is_first, own_col, other_col)
    high = jnp.where(is_first, other_col, own_col)
    gain = jnp.concatenate([low[:64], high[:64]], axis=0)
    bias = jnp.concatenate([low[64:], high[64:]], axis=0)
    gain = jnp.concatenate([gain, gain], axis=1)
    bias = jnp.concatenate([bias, bias], axis=1)
    gain_sum = jnp.zeros((128, 256), f32)
    bias_sum = jnp.zeros((128, 256), f32)
    gpre_sum = jnp.zeros((128, 256), f32)
    for q in range(0, TILES, 2):
        lanes = slice(q * 128, (q + 2) * 128)
        that, inverse = norm_over_rows(load_tiles(tri_s, q))
        tnorm = (that * gain + bias).astype(bf16)
        tnorm_s[:, lanes] = tnorm
        proj = matmul(w_out_t, tnorm)
        gate = sigmoid(matmul(w_gate_t, stack_ref[:128, lanes]))
        gated = pair_tiles(cot_ref, 0, q) * gate
        d_proj = gated.astype(bf16)
        d_proj_s[:, lanes] = d_proj
        d_gpre = gated * proj * (1.0 - gate)
        gpre_ref[:, lanes] = d_gpre.astype(bf16)
        gpre_sum = gpre_sum + d_gpre
        d_tnorm = matmul(w_out, d_proj)
        gain_sum = gain_sum + d_tnorm * that
        bias_sum = bias_sum + d_tnorm
        dth = d_tnorm * gain
        d_tri = (
            dth
            - jnp.mean(dth, axis=0, keepdims=True)
            - that * jnp.mean(dth * that, axis=0, keepdims=True)
        ) * inverse
        store_tiles(d_tri_s, q, d_tri)
    for side in range(2):
        send_ref[:, side] = d_tri_s[side * 64 : (side + 1) * 64, :TILES].astype(bf16)
    early_ref[0] = matmul_nt(tnorm_s[...], d_proj_s[...])
    early_ref[1] = gain_sum[:, :128] + gain_sum[:, 128:]
    early_ref[2] = bias_sum[:, :128] + bias_sum[:, 128:]
    early_ref[3] = gpre_sum[:, :128] + gpre_sum[:, 128:]


def back_kernel(blocks_ref, left_ref, right_ref, send_ref, d_tri_s):
    load_matrix(blocks_ref, d_tri_s)
    d_tri = d_tri_s[...]
    store_matrix(matmul(d_tri, right_ref[...]).astype(bf16), send_ref, 0)
    store_matrix(matmul_tn(d_tri, left_ref[...]).astype(bf16), send_ref, 16)


def grads_kernel(
    d_ref, mask_ref, stack_ref, gpre_ref, own_ref, other_ref, w_gate_ref, early_ref,
    delta_hbm, w_back_hbm, send_hbm, delta_ref, w_back_ref, d_s, grads_s, send_ref, sems,
):
    is_first = lax.axis_index("ch") == 0
    for side in range(2):
        d_s[side * 64 : (side + 1) * 64, :32] = d_ref[:, side].astype(f32)
    weights = [both_halves(is_first, own_ref, other_ref, n * 64, 64) for n in range(4)]
    w = jnp.concatenate(weights, axis=0).astype(bf16)
    for n in range(4):
        w_back_ref[:, n * 128 : (n + 1) * 128] = weights[n].T.astype(bf16)
    w_back_ref[:, 512:] = w_gate_ref[...]
    copies = [
        pltpu.make_async_copy(w_back_ref, w_back_hbm, sems.at[0]),
        pltpu.make_async_copy(gpre_ref, delta_hbm.at[512:], sems.at[1]),
    ]
    copies[0].start()
    copies[1].start()
    delta_ref[512:] = gpre_ref[...]
    delta_sums = [jnp.zeros((128, 256), f32)] * 4
    for q in range(0, TILES, 2):
        lanes = slice(q * 128, (q + 2) * 128)
        y = matmul(w, stack_ref[:128, lanes])
        m = mask_pair(mask_ref, q)
        for side in range(2):
            lin = y[side * 256 : side * 256 + 128]
            sig = sigmoid(y[side * 256 + 128 : side * 256 + 256])
            d_lin = load_tiles(d_s, side * TILES + q) * m * sig
            d_gate = d_lin * lin * (1.0 - sig)
            for n, d in ((2 * side, d_lin), (2 * side + 1, d_gate)):
                delta_ref[n * 128 : (n + 1) * 128, lanes] = d.astype(bf16)
                delta_sums[n] = delta_sums[n] + d
        if q % 4 == 2:
            part = (slice(0, 512), slice((q - 2) * 128, (q + 2) * 128))
            copies.append(
                pltpu.make_async_copy(
                    delta_ref.at[part], delta_hbm.at[part], sems.at[len(copies)]
                )
            )
            copies[-1].start()
    grads = matmul_nt(delta_ref[...], stack_ref[...])
    for n in range(4):
        store_rows(grads_s, n, grads[n * 128 : (n + 1) * 128, :128])
    store_rows(grads_s, 4, early_ref[0])
    store_rows(grads_s, 5, grads[512:, :128])
    gain_sum = jnp.zeros((128, 128), f32)
    bias_sum = jnp.zeros((128, 128), f32)
    delta_sums = [d[:, :128] + d[:, 128:] for d in delta_sums] + [early_ref[3]]
    weights.append(w_gate_ref[...].astype(f32).T)
    for n in range(5):
        gain_sum = gain_sum + weights[n] * grads[n * 128 : (n + 1) * 128, 128:]
        bias_sum = bias_sum + weights[n] * jnp.sum(delta_sums[n], axis=1, keepdims=True)
    sums = (
        column(jnp.sum(gain_sum, axis=0, keepdims=True)),
        column(jnp.sum(bias_sum, axis=0, keepdims=True)),
        jnp.sum(early_ref[1], axis=1, keepdims=True),
        jnp.sum(early_ref[2], axis=1, keepdims=True),
    )
    lane = lax.broadcasted_iota(jnp.int32, (128, 128), 1)
    store_rows(
        grads_s,
        6,
        jnp.where(
            lane < 64, jnp.where(lane < 32, sums[0], sums[1]), jnp.where(lane < 96, sums[2], sums[3])
        ),
    )
    store_rows(grads_s, 7, jnp.zeros((128, 128), f32))
    send_ref[...] = grads_s[...].astype(bf16)
    copies.append(pltpu.make_async_copy(send_ref, send_hbm, sems.at[6]))
    copies[-1].start()
    for copy in copies:
        copy.wait()


def pair_kernel(
    delta_hbm, w_back_hbm, zhat_hbm, inverse_hbm, gain_hbm, d_pair_hbm, d_own_hbm,
    delta_ref, w_back_ref, zhat_ref, inverse_ref, gain_ref, d_own_ref, sems,
):
    ch = lax.axis_index("ch")
    copies = start_copies(
        sems,
        (delta_hbm, delta_ref),
        (w_back_hbm, w_back_ref),
        (zhat_hbm, zhat_ref),
        (inverse_hbm, inverse_ref),
        (gain_hbm, gain_ref),
    )
    for copy in copies:
        copy.wait()
    gain = jnp.concatenate([gain_ref[...]] * 2, axis=1)
    w_back = w_back_ref[...]
    for q in range(0, TILES, 2):
        lanes = slice(q * 128, (q + 2) * 128)
        zhat = zhat_ref[:, lanes]
        dzh = matmul(w_back, delta_ref[:, lanes]) * gain
        d_pair = (
            dzh
            - jnp.mean(dzh, axis=0, keepdims=True)
            - zhat * jnp.mean(dzh * zhat, axis=0, keepdims=True)
        ) * mask_pair(inverse_ref, q)
        for n in range(2):
            rows = d_pair[:, n * 128 : (n + 1) * 128].T
            d_own_ref[q + n] = rows[:64]
            d_own_ref[TILES + q + n] = rows[64:]
    copies = start_copies(
        sems, (d_own_ref, d_pair_hbm.at[pl.ds(ch * 32, 32)]), (d_own_ref, d_own_hbm)
    )
    for copy in copies:
        copy.wait()


def sum_kernel(grads_ref, send_ref):
    total = jnp.sum(grads_ref[...].astype(f32), axis=0)
    send_ref[...] = jnp.broadcast_to(total.astype(bf16)[None], (128, 8, 128))


def end_kernel(grads_ref, other_ref, _, d_pair_hbm, *refs):
    outs, scratch, grads_s, sems = refs[:10], refs[10:20], refs[20], refs[21]
    ch = lax.axis_index("ch")
    is_first = ch == 0
    copies = [
        pltpu.make_async_copy(other_ref, d_pair_hbm.at[pl.ds(32 - ch * 32, 32)], sems.at[10])
    ]
    copies[0].start()
    grads_s[...] = grads_ref[...].astype(f32)

    def own_half(x):
        return jnp.where(is_first, x[:64], x[64:])

    sums = load_rows(grads_s, 6).T
    low, high = sums[:, :64], sums[:, 64:]
    results = (
        sums[0:1],
        sums[32:33],
        *(own_half(load_rows(grads_s, n)) for n in range(4)),
        load_rows(grads_s, 5).T,
        jnp.where(is_first, low[64:65], high[64:65]),
        jnp.where(is_first, low[96:97], high[96:97]),
        own_half(load_rows(grads_s, 4)),
    )
    for n, result in enumerate(results):
        scratch[n][...] = result
        copies.append(pltpu.make_async_copy(scratch[n], outs[n], sems.at[n]))
        copies[-1].start()
    for copy in copies:
        copy.wait()


VMEM = pl.BlockSpec(memory_space=pltpu.VMEM)
HBM = pl.BlockSpec(memory_space=pltpu.HBM)


def call(kernel, out_shapes, scratch, *args, in_specs=None, out_specs=None, aliases=None, us=None):
    out_specs = out_specs or [VMEM] * len(out_shapes)
    cost = None
    if us is not None:
        cost = pl.CostEstimate(flops=us * 10**9, bytes_accessed=us * 3 * 10**6, transcendentals=0)
    return pl.pallas_call(
        kernel,
        out_shape=[
            pltpu.HBM(s, t) if spec is HBM else jax.ShapeDtypeStruct(s, t)
            for (s, t), spec in zip(out_shapes, out_specs)
        ],
        in_specs=in_specs or [VMEM] * len(args),
        out_specs=out_specs,
        scratch_shapes=scratch,
        input_output_aliases=aliases or {},
        cost_estimate=cost,
        compiler_params=pltpu.CompilerParams(vmem_limit_bytes=VMEM_LIMIT),
    )(*args)


def in_hbm(*arrays):
    return [pltpu.with_memory_space_constraint(x, pltpu.HBM) for x in arrays]


def to_all(x):
    return lax.all_to_all(x, ALL, 0, 0, tiled=True)


def body(
    pair, cotangent, pair_mask, norm_gain, norm_bias, w_left, w_left_gate, w_right, w_right_gate,
    w_out_gate, out_norm_gain, out_norm_bias, w_out,
):
    pairs = 128 * TILES
    swap = [(0, 1), (1, 0)]
    with jax.named_scope("first"):
        send, stack, mask, packed, cot, w_gate, zhat, inverse, gain = call(
            first_kernel,
            [
                ((64, 64, 128), bf16),
                ((256, pairs), bf16),
                ((TILES, 128), f32),
                ((328, 128), f32),
                ((32, 64, 128), bf16),
                ((128, 128), bf16),
                ((128, pairs), f32),
                ((TILES, 128), f32),
                ((128, 128), f32),
            ],
            [
                pltpu.VMEM((128, pairs), f32),
                pltpu.VMEM((TILES, 128), f32),
                pltpu.VMEM((128, 128), f32),
                pltpu.VMEM((64, 64, 128), bf16),
                pltpu.VMEM((64, 64), jnp.int32),
                pltpu.VMEM((2, 1, 128), f32),
                pltpu.VMEM((256, 128), bf16),
                pltpu.VMEM((64, 128), bf16),
                pltpu.VMEM((1, 64), f32),
                pltpu.VMEM((1, 64), f32),
                pltpu.VMEM((2 * TILES, 128), f32),
                pltpu.VMEM((64, 72, 128), f32),
                pltpu.SemaphoreType.DMA((15,)),
                pltpu.SemaphoreType.DMA((3,)),
            ],
            *in_hbm(
                pair, pair_mask, norm_gain[None], norm_bias[None], w_left.T, w_left_gate.T, w_right.T,
                w_right_gate.T, w_out, out_norm_gain[None], out_norm_bias[None], cotangent, w_out_gate,
            ),
            in_specs=[HBM] * 13,
            out_specs=[VMEM] * 6 + [HBM] * 3,
        )
    with jax.named_scope("left_right"):
        blocks = lax.all_to_all(send, ("row", "col"), 0, 0, tiled=True)
    with jax.named_scope("weights"):
        blocks, own = lax.optimization_barrier((blocks, packed))
        other = lax.ppermute(own, "ch", swap)
    with jax.named_scope("triangle"):
        send, left, right = call(
            triangle_kernel,
            [((8, 8, 2, TILES, 128), bf16), ((512, 512), bf16), ((512, 512), bf16)],
            [],
            blocks.reshape(8, 8, 2, 2, TILES, 128),
        )
    with jax.named_scope("tri"):
        send, other = lax.optimization_barrier((send, other))
        tri = to_all(send.reshape(128, TILES, 128))
    with jax.named_scope("middle"):
        send, gpre, early = call(
            middle_kernel,
            [((64, 2, TILES, 128), bf16), ((128, pairs), bf16), ((4, 128, 128), f32)],
            [
                pltpu.VMEM((128, 24, 128), f32),
                pltpu.VMEM((128, 24, 128), f32),
                pltpu.VMEM((128, pairs), bf16),
                pltpu.VMEM((128, pairs), bf16),
            ],
            tri.reshape(64, 2, TILES, 128), stack, cot, w_gate, own, other,
        )
    with jax.named_scope("d_tri"):
        blocks = to_all(send.reshape(128, TILES, 128))
    with jax.named_scope("back"):
        (send,) = call(
            back_kernel,
            [((8, 8, 2, 2 * TILES, 128), bf16)],
            [pltpu.VMEM((512, 512), bf16)],
            blocks.reshape(8, 8, 2, TILES, 128), left, right,
        )
    with jax.named_scope("d_left_right"):
        d_full = to_all(send.reshape(128, 2 * TILES, 128))
    with jax.named_scope("grads"):
        delta, w_back, send = call(
            grads_kernel,
            [((640, pairs), bf16), ((128, 640), bf16), ((128, 8, 128), bf16)],
            [
                pltpu.VMEM((640, pairs), bf16),
                pltpu.VMEM((128, 640), bf16),
                pltpu.VMEM((128, 40, 128), f32),
                pltpu.VMEM((128, 8, 128), f32),
                pltpu.VMEM((128, 8, 128), bf16),
                pltpu.SemaphoreType.DMA((7,)),
            ],
            d_full.reshape(64, 2, 2 * TILES, 128), mask, stack, gpre, own, other, w_gate, early,
            out_specs=[HBM, HBM, HBM],
        )
    with jax.named_scope("sums"):
        parts = to_all(send)
    with jax.named_scope("pair"):
        d_pair, d_own = call(
            pair_kernel,
            [((64, 64, 128), f32), ((32, 64, 128), f32)],
            [
                pltpu.VMEM((640, pairs), bf16),
                pltpu.VMEM((128, 640), bf16),
                pltpu.VMEM((128, pairs), f32),
                pltpu.VMEM((TILES, 128), f32),
                pltpu.VMEM((128, 128), f32),
                pltpu.VMEM((32, 64, 128), f32),
                pltpu.SemaphoreType.DMA((5,)),
            ],
            *in_hbm(delta, w_back, zhat, inverse, gain),
            in_specs=[HBM] * 5,
            out_specs=[HBM, HBM],
            us=4,
        )
        parts, d_own = lax.optimization_barrier((parts, d_own))
        d_other = lax.ppermute(d_own, "ch", swap)
    with jax.named_scope("sums"):
        (send,) = call(sum_kernel, [((128, 8, 128), bf16)], [], parts)
        parts = to_all(send)
    with jax.named_scope("end"):
        shapes = [
            ((64, 64, 128), f32), ((1, 128), f32), ((1, 128), f32), ((64, 128), f32), ((64, 128), f32), ((64, 128), f32),
            ((64, 128), f32), ((128, 128), f32), ((1, 64), f32), ((1, 64), f32), ((64, 128), f32),
        ]
        d_pair, gain, bias, left, left_gate, right, right_gate, gate, out_gain, out_bias, out = call(
            end_kernel,
            shapes,
            [pltpu.VMEM(shape, f32) for shape, _ in shapes[1:]]
            + [pltpu.VMEM((128, 8, 128), f32), pltpu.SemaphoreType.DMA((11,))],
            parts, d_other, *in_hbm(d_pair),
            in_specs=[VMEM, VMEM, HBM],
            out_specs=[HBM] * 11,
            aliases={2: 0},
        )
    return (
        d_pair, gain[0], bias[0], left.T, left_gate.T, right.T, right_gate.T, gate, out_gain[0],
        out_bias[0], out,
    )


def solution(mesh):
    placed = (
        P("row", "col", None), P("row", "col", None), P("row", "col"), P(), P(), P(None, "ch"),
        P(None, "ch"), P(None, "ch"), P(None, "ch"), P(), P("ch"), P("ch"), P("ch", None),
    )
    return jax.shard_map(
        body,
        mesh=mesh,
        in_specs=placed,
        out_specs=(
            P("row", "col", None), P(), P(), P(None, "ch"), P(None, "ch"), P(None, "ch"),
            P(None, "ch"), P(), P("ch"), P("ch"), P("ch", None),
        ),
        check_vma=False,
    )
```

```python
import jax
import jax.numpy as jnp
from jax import lax
from jax.experimental import pallas as pl
from jax.experimental.pallas import tpu as pltpu
from jax.sharding import PartitionSpec as P

f32 = jnp.float32
bf16 = jnp.bfloat16
ALL = ("row", "col", "ch")
TILES = 16
EPS = 1e-05
VMEM_LIMIT = 10 * 1024 * 1024


def matmul(a, b):
    return lax.dot_general(a, b, (((1,), (0,)), ((), ())), preferred_element_type=f32)


def matmul_nt(a, b):
    return lax.dot_general(a, b, (((1,), (1,)), ((), ())), preferred_element_type=f32)


def matmul_tn(a, b):
    return lax.dot_general(a, b, (((0,), (0,)), ((), ())), preferred_element_type=f32)


def sigmoid(x):
    return 0.5 * jnp.tanh(0.5 * x) + 0.5


def column(row):
    return jnp.broadcast_to(row, (128, 128)).T


def norm_over_rows(x):
    mean = jnp.mean(x, axis=0, keepdims=True)
    centred = x - mean
    inverse = lax.rsqrt(jnp.mean(centred * centred, axis=0, keepdims=True) + EPS)
    return centred * inverse, inverse


def pair_tiles(ref, start, q, group=2):
    tiles = [
        jnp.concatenate([ref[start + q + n], ref[start + TILES + q + n]], axis=0).T.astype(f32)
        for n in range(group)
    ]
    return jnp.concatenate(tiles, axis=1)


def mask_rows(mask):
    return jnp.concatenate([mask[:TILES], mask[TILES:]], axis=1).astype(f32)


def mask_pair(rows, start):
    return jnp.concatenate([rows[pl.ds(start, 1)], rows[pl.ds(start + 1, 1)]], axis=1)


def store_rows(ref, row, value):
    rows, block, _ = ref.shape
    ref.reshape(rows * block, 128)[pl.ds(row, rows, stride=block)] = value


def load_rows(ref, row):
    rows, block, _ = ref.shape
    return ref.reshape(rows * block, 128)[pl.ds(row, rows, stride=block)]


def store_tiles(ref, row, value):
    for n in range(value.shape[1] // 128):
        store_rows(ref, row + n, value[:, n * 128 : (n + 1) * 128])


def load_tiles(ref, row, group=2):
    return jnp.concatenate([load_rows(ref, row + n) for n in range(group)], axis=1)


def fold(x):
    return sum(x[:, n : n + 128] for n in range(0, x.shape[1], 128))


def both_halves(is_first, own_ref, other_ref, start, count):
    own, other = own_ref[start : start + count], other_ref[start : start + count]
    return jnp.concatenate(
        [jnp.where(is_first, own, other), jnp.where(is_first, other, own)], axis=0
    )


def exchange(a, b):
    return (
        jnp.concatenate([a[..., :64], b[..., :64]], axis=-1),
        jnp.concatenate([a[..., 64:], b[..., 64:]], axis=-1),
    )


def load_matrix(blocks, out):
    for pair in range(4):
        low, high = exchange(blocks[:, 2 * pair], blocks[:, 2 * pair + 1])
        out[:, pair * 128 : (pair + 1) * 128] = jnp.stack([low, high], axis=2).reshape(512, 128)


def store_matrix(matrix, blocks, at):
    for pair in range(4):
        part = matrix[:, pair * 128 : (pair + 1) * 128].reshape(8, 2, 2, 16, 128)
        first, second = exchange(part[:, :, 0], part[:, :, 1])
        blocks[:, 2 * pair, :, at : at + 16, :] = first
        blocks[:, 2 * pair + 1, :, at : at + 16, :] = second


def start_copies(sems, *pairs):
    copies = [
        pltpu.make_async_copy(source, target, sems.at[n]) for n, (source, target) in enumerate(pairs)
    ]
    for copy in copies:
        copy.start()
    return copies


def first_kernel(
    pair_hbm, mask_hbm, gain_hbm, bias_hbm, left_hbm, left_gate_hbm, right_hbm, right_gate_hbm,
    w_out_hbm, out_gain_hbm, out_bias_hbm, cot_hbm, w_gate_hbm,
    send_ref, stack_ref, mask_ref, packed_ref, cot_ref, w_gate_ref,
    zhat_hbm, inverse_hbm, gain_out_hbm, zhat_ref, inverse_ref, gain_ref,
    pair_s, mask_s, norm_s, w_s, w_out_s, out_gain_s, out_bias_s, rows_s, send_s, sems, out_sems,
):
    ch = lax.axis_index("ch")
    own, other = ch * 32, 32 - ch * 32
    copies = start_copies(
        sems,
        (pair_hbm.at[pl.ds(own, 32)], pair_s.at[0:32]),
        (gain_hbm, norm_s.at[0]),
        (bias_hbm, norm_s.at[1]),
        (mask_hbm.at[pl.ds(own, 32)], mask_s.at[0:32]),
        (left_hbm, w_s.at[0:64]),
        (left_gate_hbm, w_s.at[64:128]),
        (right_hbm, w_s.at[128:192]),
        (right_gate_hbm, w_s.at[192:256]),
        (pair_hbm.at[pl.ds(other, 32)], pair_s.at[32:64]),
        (mask_hbm.at[pl.ds(other, 32)], mask_s.at[32:64]),
        (w_out_hbm, w_out_s),
        (out_gain_hbm, out_gain_s),
        (out_bias_hbm, out_bias_s),
        (cot_hbm.at[pl.ds(own, 32)], cot_ref),
        (w_gate_hbm, w_gate_ref),
    )
    for copy in copies[:8]:
        copy.wait()
    gain, bias = column(norm_s[0]), column(norm_s[1])
    gain_ref[...] = gain
    gain = jnp.concatenate([gain, gain], axis=1)
    bias = jnp.concatenate([bias, bias], axis=1)
    rows_s[:TILES] = mask_rows(mask_s[:32])
    mask_ref[...] = rows_s[:TILES]
    w = w_s[...]
    for part in range(2):
        if part == 1:
            for copy in copies[8:13]:
                copy.wait()
            rows_s[TILES:] = mask_rows(mask_s[32:])
            packed_ref[:256] = w.astype(f32)
            packed_ref[256:320] = w_out_s[...].astype(f32)
            norms = jnp.concatenate([out_gain_s[...], out_bias_s[...]], axis=1)
            packed_ref[320:] = jnp.broadcast_to(norms, (8, 128))
            results = start_copies(
                out_sems, (zhat_ref, zhat_hbm), (inverse_ref, inverse_hbm), (gain_ref, gain_out_hbm)
            )
        row = part * TILES
        for q in range(0, TILES, 2):
            zhat, inverse = norm_over_rows(pair_tiles(pair_s, part * 32, q))
            normed = (zhat * gain + bias).astype(bf16)
            if part == 0:
                lanes = slice(q * 128, (q + 2) * 128)
                zhat_ref[:, lanes] = zhat
                inverse_ref[q : q + 1] = inverse[:, :128]
                inverse_ref[q + 1 : q + 2] = inverse[:, 128:]
                stack_ref[:128, lanes] = normed
                stack_ref[128:, lanes] = zhat.astype(bf16)
            y = matmul(w, normed)
            m = mask_pair(rows_s, row + q)
            store_tiles(send_s, row + q, m * sigmoid(y[64:128]) * y[:64])
            store_tiles(send_s, row + 32 + q, m * sigmoid(y[192:]) * y[128:192])
    for part, start in enumerate((own, other)):
        for side in range(2):
            target = pl.ds(pl.multiple_of(start // 2 + side * 32, TILES), TILES)
            row = part * TILES + side * 32
            send_ref[:, target] = send_s[:, row : row + TILES].astype(bf16)
    for copy in copies[13:] + results:
        copy.wait()


def triangle_kernel(blocks_ref, send_ref, left_ref, right_ref):
    load_matrix(blocks_ref.at[:, :, 0], left_ref)
    load_matrix(blocks_ref.at[:, :, 1], right_ref)
    tri = matmul_nt(left_ref[...], right_ref[...]).astype(bf16)
    store_matrix(tri, send_ref, 0)


def middle_kernel(
    tri_ref, stack_ref, cot_ref, w_gate_ref, own_ref, other_ref,
    send_ref, gpre_ref, early_ref, tri_s, d_tri_s, tnorm_s, d_proj_s,
):
    group = 8
    is_first = lax.axis_index("ch") == 0
    for side in range(2):
        tri_s[side * 64 : (side + 1) * 64, :TILES] = tri_ref[:, side].astype(f32)
    w_out = both_halves(is_first, own_ref, other_ref, 256, 64)
    w_out_t = w_out.T.astype(bf16)
    w_out = w_out.astype(bf16)
    w_gate_t = w_gate_ref[...].astype(f32).T.astype(bf16)
    own_col, other_col = column(own_ref[320:321]), column(other_ref[320:321])
    low = jnp.where(is_first, own_col, other_col)
    high = jnp.where(is_first, other_col, own_col)
    gain = jnp.concatenate([low[:64], high[:64]], axis=0)
    bias = jnp.concatenate([low[64:], high[64:]], axis=0)
    gain = jnp.concatenate([gain] * group, axis=1)
    bias = jnp.concatenate([bias] * group, axis=1)
    gain_sum = jnp.zeros((128, group * 128), f32)
    bias_sum = jnp.zeros((128, group * 128), f32)
    gpre_sum = jnp.zeros((128, group * 128), f32)
    for q in range(0, TILES, group):
        lanes = slice(q * 128, (q + group) * 128)
        that, inverse = norm_over_rows(load_tiles(tri_s, q, group))
        tnorm = (that * gain + bias).astype(bf16)
        tnorm_s[:, lanes] = tnorm
        proj = matmul(w_out_t, tnorm)
        gate = sigmoid(matmul(w_gate_t, stack_ref[:128, lanes]))
        gated = pair_tiles(cot_ref, 0, q, group) * gate
        d_proj = gated.astype(bf16)
        d_proj_s[:, lanes] = d_proj
        d_gpre = gated * proj * (1.0 - gate)
        gpre_ref[:, lanes] = d_gpre.astype(bf16)
        gpre_sum = gpre_sum + d_gpre
        d_tnorm = matmul(w_out, d_proj)
        gain_sum = gain_sum + d_tnorm * that
        bias_sum = bias_sum + d_tnorm
        dth = d_tnorm * gain
        d_tri = (
            dth
            - jnp.mean(dth, axis=0, keepdims=True)
            - that * jnp.mean(dth * that, axis=0, keepdims=True)
        ) * inverse
        store_tiles(d_tri_s, q, d_tri)
    for side in range(2):
        send_ref[:, side] = d_tri_s[side * 64 : (side + 1) * 64, :TILES].astype(bf16)
    early_ref[0] = matmul_nt(tnorm_s[...], d_proj_s[...])
    early_ref[1] = fold(gain_sum)
    early_ref[2] = fold(bias_sum)
    early_ref[3] = fold(gpre_sum)


def back_kernel(blocks_ref, left_ref, right_ref, send_ref, d_tri_s):
    load_matrix(blocks_ref, d_tri_s)
    d_tri = d_tri_s[...]
    store_matrix(matmul(d_tri, right_ref[...]).astype(bf16), send_ref, 0)
    store_matrix(matmul_tn(d_tri, left_ref[...]).astype(bf16), send_ref, 16)


def grads_kernel(
    d_ref, mask_ref, stack_ref, gpre_ref, own_ref, other_ref, w_gate_ref, early_ref,
    delta_hbm, w_back_hbm, send_hbm, delta_ref, w_back_ref, d_s, grads_s, send_ref, sems,
):
    is_first = lax.axis_index("ch") == 0
    for side in range(2):
        d_s[side * 64 : (side + 1) * 64, :32] = d_ref[:, side].astype(f32)
    weights = [both_halves(is_first, own_ref, other_ref, n * 64, 64) for n in range(4)]
    w = jnp.concatenate(weights, axis=0).astype(bf16)
    for n in range(4):
        w_back_ref[:, n * 128 : (n + 1) * 128] = weights[n].T.astype(bf16)
    w_back_ref[:, 512:] = w_gate_ref[...]
    copies = [
        pltpu.make_async_copy(w_back_ref, w_back_hbm, sems.at[0]),
        pltpu.make_async_copy(gpre_ref, delta_hbm.at[512:], sems.at[1]),
    ]
    copies[0].start()
    copies[1].start()
    delta_ref[512:] = gpre_ref[...]
    delta_sums = [jnp.zeros((128, 256), f32)] * 4
    for q in range(0, TILES, 2):
        lanes = slice(q * 128, (q + 2) * 128)
        y = matmul(w, stack_ref[:128, lanes])
        m = mask_pair(mask_ref, q)
        for side in range(2):
            lin = y[side * 256 : side * 256 + 128]
            sig = sigmoid(y[side * 256 + 128 : side * 256 + 256])
            d_lin = load_tiles(d_s, side * TILES + q) * m * sig
            d_gate = d_lin * lin * (1.0 - sig)
            for n, d in ((2 * side, d_lin), (2 * side + 1, d_gate)):
                delta_ref[n * 128 : (n + 1) * 128, lanes] = d.astype(bf16)
                delta_sums[n] = delta_sums[n] + d
        if q % 4 == 2:
            part = (slice(0, 512), slice((q - 2) * 128, (q + 2) * 128))
            copies.append(
                pltpu.make_async_copy(
                    delta_ref.at[part], delta_hbm.at[part], sems.at[len(copies)]
                )
            )
            copies[-1].start()
    grads = matmul_nt(delta_ref[...], stack_ref[...])
    for n in range(5):
        whole = early_ref[0] if n == 4 else grads[n * 128 : (n + 1) * 128, :128]
        low, high = exchange(whole[:64], whole[64:])
        store_rows(grads_s, n, low)
        store_rows(grads_s, 8 + n, high)
    gain_sum = jnp.zeros((128, 128), f32)
    bias_sum = jnp.zeros((128, 128), f32)
    delta_sums = [fold(d) for d in delta_sums] + [early_ref[3]]
    weights.append(w_gate_ref[...].astype(f32).T)
    for n in range(5):
        gain_sum = gain_sum + weights[n] * grads[n * 128 : (n + 1) * 128, 128:]
        bias_sum = bias_sum + weights[n] * jnp.sum(delta_sums[n], axis=1, keepdims=True)
    sums = (
        column(jnp.sum(gain_sum, axis=0, keepdims=True)),
        column(jnp.sum(bias_sum, axis=0, keepdims=True)),
        jnp.sum(early_ref[1], axis=1, keepdims=True),
        jnp.sum(early_ref[2], axis=1, keepdims=True),
    )
    lane = lax.broadcasted_iota(jnp.int32, (128, 128), 1) % 64
    sums = jnp.where(
        lane < 32, jnp.where(lane < 16, sums[0], sums[1]), jnp.where(lane < 48, sums[2], sums[3])
    )
    for n, whole in enumerate((grads[512:, :128], sums, jnp.zeros((128, 128), f32))):
        store_rows(grads_s, 5 + n, whole[:64])
        store_rows(grads_s, 13 + n, whole[64:])
    send_ref[...] = grads_s[:, :16].astype(bf16)
    copies.append(pltpu.make_async_copy(send_ref, send_hbm, sems.at[6]))
    copies[-1].start()
    for copy in copies:
        copy.wait()


def pair_kernel(
    delta_hbm, w_back_hbm, zhat_hbm, inverse_hbm, gain_hbm, d_pair_hbm, d_own_hbm,
    delta_ref, w_back_ref, zhat_ref, inverse_ref, gain_ref, d_own_ref, sems,
):
    ch = lax.axis_index("ch")
    copies = start_copies(
        sems,
        (delta_hbm, delta_ref),
        (w_back_hbm, w_back_ref),
        (zhat_hbm, zhat_ref),
        (inverse_hbm, inverse_ref),
        (gain_hbm, gain_ref),
    )
    for copy in copies:
        copy.wait()
    gain = jnp.concatenate([gain_ref[...]] * 2, axis=1)
    w_back = w_back_ref[...]
    for q in range(0, TILES, 2):
        lanes = slice(q * 128, (q + 2) * 128)
        zhat = zhat_ref[:, lanes]
        dzh = matmul(w_back, delta_ref[:, lanes]) * gain
        d_pair = (
            dzh
            - jnp.mean(dzh, axis=0, keepdims=True)
            - zhat * jnp.mean(dzh * zhat, axis=0, keepdims=True)
        ) * mask_pair(inverse_ref, q)
        for n in range(2):
            rows = d_pair[:, n * 128 : (n + 1) * 128].T
            d_own_ref[q + n] = rows[:64]
            d_own_ref[TILES + q + n] = rows[64:]
    copies = start_copies(
        sems, (d_own_ref, d_pair_hbm.at[pl.ds(ch * 32, 32)]), (d_own_ref, d_own_hbm)
    )
    for copy in copies:
        copy.wait()


def sum_kernel(grads_ref, send_ref):
    total = jnp.sum(grads_ref[...].astype(f32), axis=0)
    halves = exchange(
        jnp.concatenate([total[n : n + 1] for n in (0, 2, 5, 4)], axis=0),
        jnp.concatenate([total[n : n + 1] for n in (1, 3, 5, 6)], axis=0),
    )
    row = lax.broadcasted_iota(jnp.int32, (4, 128), 0)
    for side in range(2):
        rows = jnp.where(row == 2, total[5:6], halves[side])
        send_ref[:, side] = jnp.broadcast_to(rows.astype(bf16)[None], (64, 4, 128))


def end_kernel(grads_ref, other_ref, _, d_pair_hbm, *refs):
    outs, scratch, grads_s, sems = refs[:10], refs[10:20], refs[20], refs[21]
    ch = lax.axis_index("ch")
    is_first = ch == 0
    copies = [
        pltpu.make_async_copy(other_ref, d_pair_hbm.at[pl.ds(32 - ch * 32, 32)], sems.at[10])
    ]
    copies[0].start()
    for side in range(2):
        grads_s[:, side * 4 : side * 4 + 4] = grads_ref[:, side].astype(f32)
    rows = [load_rows(grads_s, n) for n in range(8)]
    out, sums = exchange(rows[3], rows[7])
    sums = jnp.concatenate([sums, sums], axis=0).T[:, :64]

    def vector(n):
        return jnp.concatenate([sums[n : n + 1], sums[64 + n : 65 + n]], axis=1)

    results = (
        vector(0),
        vector(16),
        *exchange(rows[0], rows[4]),
        *exchange(rows[1], rows[5]),
        jnp.concatenate([rows[2], rows[6]], axis=0).T,
        jnp.where(is_first, sums[32:33], sums[96:97]),
        jnp.where(is_first, sums[48:49], sums[112:113]),
        out,
    )
    for n, result in enumerate(results):
        scratch[n][...] = result
        copies.append(pltpu.make_async_copy(scratch[n], outs[n], sems.at[n]))
        copies[-1].start()
    for copy in copies:
        copy.wait()


VMEM = pl.BlockSpec(memory_space=pltpu.VMEM)
HBM = pl.BlockSpec(memory_space=pltpu.HBM)


def call(kernel, out_shapes, scratch, *args, in_specs=None, out_specs=None, aliases=None, us=None):
    out_specs = out_specs or [VMEM] * len(out_shapes)
    cost = None
    if us is not None:
        cost = pl.CostEstimate(flops=us * 10**9, bytes_accessed=us * 3 * 10**6, transcendentals=0)
    return pl.pallas_call(
        kernel,
        out_shape=[
            pltpu.HBM(s, t) if spec is HBM else jax.ShapeDtypeStruct(s, t)
            for (s, t), spec in zip(out_shapes, out_specs)
        ],
        in_specs=in_specs or [VMEM] * len(args),
        out_specs=out_specs,
        scratch_shapes=scratch,
        input_output_aliases=aliases or {},
        cost_estimate=cost,
        compiler_params=pltpu.CompilerParams(vmem_limit_bytes=VMEM_LIMIT),
    )(*args)


def in_hbm(*arrays):
    return [pltpu.with_memory_space_constraint(x, pltpu.HBM) for x in arrays]


def to_all(x):
    return lax.all_to_all(x, ALL, 0, 0, tiled=True)


def body(
    pair, cotangent, pair_mask, norm_gain, norm_bias, w_left, w_left_gate, w_right, w_right_gate,
    w_out_gate, out_norm_gain, out_norm_bias, w_out,
):
    pairs = 128 * TILES
    swap = [(0, 1), (1, 0)]
    with jax.named_scope("first"):
        send, stack, mask, packed, cot, w_gate, zhat, inverse, gain = call(
            first_kernel,
            [
                ((64, 64, 128), bf16),
                ((256, pairs), bf16),
                ((TILES, 128), f32),
                ((328, 128), f32),
                ((32, 64, 128), bf16),
                ((128, 128), bf16),
                ((128, pairs), f32),
                ((TILES, 128), f32),
                ((128, 128), f32),
            ],
            [
                pltpu.VMEM((128, pairs), f32),
                pltpu.VMEM((TILES, 128), f32),
                pltpu.VMEM((128, 128), f32),
                pltpu.VMEM((64, 64, 128), bf16),
                pltpu.VMEM((64, 64), jnp.int32),
                pltpu.VMEM((2, 1, 128), f32),
                pltpu.VMEM((256, 128), bf16),
                pltpu.VMEM((64, 128), bf16),
                pltpu.VMEM((1, 64), f32),
                pltpu.VMEM((1, 64), f32),
                pltpu.VMEM((2 * TILES, 128), f32),
                pltpu.VMEM((64, 72, 128), f32),
                pltpu.SemaphoreType.DMA((15,)),
                pltpu.SemaphoreType.DMA((3,)),
            ],
            *in_hbm(
                pair, pair_mask, norm_gain[None], norm_bias[None], w_left.T, w_left_gate.T, w_right.T,
                w_right_gate.T, w_out, out_norm_gain[None], out_norm_bias[None], cotangent, w_out_gate,
            ),
            in_specs=[HBM] * 13,
            out_specs=[VMEM] * 6 + [HBM] * 3,
        )
    with jax.named_scope("left_right"):
        blocks = lax.all_to_all(send, ("row", "col"), 0, 0, tiled=True)
    with jax.named_scope("weights"):
        blocks, own = lax.optimization_barrier((blocks, packed))
        other = lax.ppermute(own, "ch", swap)
    with jax.named_scope("triangle"):
        send, left, right = call(
            triangle_kernel,
            [((8, 8, 2, TILES, 128), bf16), ((512, 512), bf16), ((512, 512), bf16)],
            [],
            blocks.reshape(8, 8, 2, 2, TILES, 128),
        )
    with jax.named_scope("tri"):
        send, other = lax.optimization_barrier((send, other))
        tri = to_all(send.reshape(128, TILES, 128))
    with jax.named_scope("middle"):
        send, gpre, early = call(
            middle_kernel,
            [((64, 2, TILES, 128), bf16), ((128, pairs), bf16), ((4, 128, 128), f32)],
            [
                pltpu.VMEM((128, 24, 128), f32),
                pltpu.VMEM((128, 24, 128), f32),
                pltpu.VMEM((128, pairs), bf16),
                pltpu.VMEM((128, pairs), bf16),
            ],
            tri.reshape(64, 2, TILES, 128), stack, cot, w_gate, own, other,
        )
    with jax.named_scope("d_tri"):
        blocks = to_all(send.reshape(128, TILES, 128))
    with jax.named_scope("back"):
        (send,) = call(
            back_kernel,
            [((8, 8, 2, 2 * TILES, 128), bf16)],
            [pltpu.VMEM((512, 512), bf16)],
            blocks.reshape(8, 8, 2, TILES, 128), left, right,
        )
    with jax.named_scope("d_left_right"):
        d_full = to_all(send.reshape(128, 2 * TILES, 128))
    with jax.named_scope("grads"):
        delta, w_back, send = call(
            grads_kernel,
            [((640, pairs), bf16), ((128, 640), bf16), ((64, 16, 128), bf16)],
            [
                pltpu.VMEM((640, pairs), bf16),
                pltpu.VMEM((128, 640), bf16),
                pltpu.VMEM((128, 40, 128), f32),
                pltpu.VMEM((64, 24, 128), f32),
                pltpu.VMEM((64, 16, 128), bf16),
                pltpu.SemaphoreType.DMA((7,)),
            ],
            d_full.reshape(64, 2, 2 * TILES, 128), mask, stack, gpre, own, other, w_gate, early,
            out_specs=[HBM, HBM, HBM],
        )
    with jax.named_scope("sums"):
        parts = to_all(send.reshape(128, 8, 128))
    with jax.named_scope("pair"):
        d_pair, d_own = call(
            pair_kernel,
            [((64, 64, 128), f32), ((32, 64, 128), f32)],
            [
                pltpu.VMEM((640, pairs), bf16),
                pltpu.VMEM((128, 640), bf16),
                pltpu.VMEM((128, pairs), f32),
                pltpu.VMEM((TILES, 128), f32),
                pltpu.VMEM((128, 128), f32),
                pltpu.VMEM((32, 64, 128), f32),
                pltpu.SemaphoreType.DMA((5,)),
            ],
            *in_hbm(delta, w_back, zhat, inverse, gain),
            in_specs=[HBM] * 5,
            out_specs=[HBM, HBM],
            us=4,
        )
        parts, d_own = lax.optimization_barrier((parts, d_own))
        d_other = lax.ppermute(d_own, "ch", swap)
    with jax.named_scope("sums"):
        (send,) = call(sum_kernel, [((64, 2, 4, 128), bf16)], [], parts)
        parts = to_all(send.reshape(128, 4, 128)).reshape(64, 2, 4, 128)
    with jax.named_scope("end"):
        shapes = [
            ((64, 64, 128), f32), ((1, 128), f32), ((1, 128), f32), ((64, 128), f32), ((64, 128), f32), ((64, 128), f32),
            ((64, 128), f32), ((128, 128), f32), ((1, 64), f32), ((1, 64), f32), ((64, 128), f32),
        ]
        d_pair, gain, bias, left, left_gate, right, right_gate, gate, out_gain, out_bias, out = call(
            end_kernel,
            shapes,
            [pltpu.VMEM(shape, f32) for shape, _ in shapes[1:]]
            + [pltpu.VMEM((64, 8, 128), f32), pltpu.SemaphoreType.DMA((11,))],
            parts, d_other, *in_hbm(d_pair),
            in_specs=[VMEM, VMEM, HBM],
            out_specs=[HBM] * 11,
            aliases={2: 0},
        )
    return (
        d_pair, gain[0], bias[0], left.T, left_gate.T, right.T, right_gate.T, gate, out_gain[0],
        out_bias[0], out,
    )


def solution(mesh):
    placed = (
        P("row", "col", None), P("row", "col", None), P("row", "col"), P(), P(), P(None, "ch"),
        P(None, "ch"), P(None, "ch"), P(None, "ch"), P(), P("ch"), P("ch"), P("ch", None),
    )
    return jax.shard_map(
        body,
        mesh=mesh,
        in_specs=placed,
        out_specs=(
            P("row", "col", None), P(), P(), P(None, "ch"), P(None, "ch"), P(None, "ch"),
            P(None, "ch"), P(), P("ch"), P("ch"), P("ch", None),
        ),
        check_vma=False,
    )
```

```python
import jax
import jax.numpy as jnp
from jax import lax
from jax.experimental import pallas as pl
from jax.experimental.pallas import tpu as pltpu
from jax.sharding import PartitionSpec as P

f32 = jnp.float32
bf16 = jnp.bfloat16
ALL = ("row", "col", "ch")
TILES = 16
EPS = 1e-05
VMEM_LIMIT = 10 * 1024 * 1024


def matmul(a, b):
    return lax.dot_general(a, b, (((1,), (0,)), ((), ())), preferred_element_type=f32)


def matmul_nt(a, b):
    return lax.dot_general(a, b, (((1,), (1,)), ((), ())), preferred_element_type=f32)


def matmul_tn(a, b):
    return lax.dot_general(a, b, (((0,), (0,)), ((), ())), preferred_element_type=f32)


def sigmoid(x):
    return jax.nn.sigmoid(x)


def column(row):
    return jnp.broadcast_to(row, (128, 128)).T


def norm_over_rows(x):
    mean = jnp.mean(x, axis=0, keepdims=True)
    centred = x - mean
    inverse = lax.rsqrt(jnp.mean(centred * centred, axis=0, keepdims=True) + EPS)
    return centred * inverse, inverse


def pair_tiles(ref, start, q, group=2):
    tiles = [
        jnp.concatenate([ref[start + q + n], ref[start + TILES + q + n]], axis=0).T.astype(f32)
        for n in range(group)
    ]
    return jnp.concatenate(tiles, axis=1)


def mask_rows(mask):
    return jnp.concatenate([mask[:TILES], mask[TILES:]], axis=1).astype(f32)


def mask_pair(rows, start):
    return jnp.concatenate([rows[pl.ds(start, 1)], rows[pl.ds(start + 1, 1)]], axis=1)


def store_rows(ref, row, value):
    rows, block, _ = ref.shape
    ref.reshape(rows * block, 128)[pl.ds(row, rows, stride=block)] = value


def load_rows(ref, row):
    rows, block, _ = ref.shape
    return ref.reshape(rows * block, 128)[pl.ds(row, rows, stride=block)]


def store_tiles(ref, row, value):
    for n in range(value.shape[1] // 128):
        store_rows(ref, row + n, value[:, n * 128 : (n + 1) * 128])


def load_tiles(ref, row, group=2):
    return jnp.concatenate([load_rows(ref, row + n) for n in range(group)], axis=1)


def fold(x):
    return sum(x[:, n : n + 128] for n in range(0, x.shape[1], 128))


def both_halves(is_first, own_ref, other_ref, start, count):
    own, other = own_ref[start : start + count], other_ref[start : start + count]
    return jnp.concatenate(
        [jnp.where(is_first, own, other), jnp.where(is_first, other, own)], axis=0
    )


def exchange(a, b):
    return (
        jnp.concatenate([a[..., :64], b[..., :64]], axis=-1),
        jnp.concatenate([a[..., 64:], b[..., 64:]], axis=-1),
    )


def load_matrix(blocks, out):
    for pair in range(4):
        low, high = exchange(blocks[:, 2 * pair], blocks[:, 2 * pair + 1])
        out[:, pair * 128 : (pair + 1) * 128] = jnp.stack([low, high], axis=2).reshape(512, 128)


def store_matrix(matrix, blocks, at):
    for pair in range(4):
        part = matrix[:, pair * 128 : (pair + 1) * 128].reshape(8, 2, 2, 16, 128)
        first, second = exchange(part[:, :, 0], part[:, :, 1])
        blocks[:, 2 * pair, :, at : at + 16, :] = first
        blocks[:, 2 * pair + 1, :, at : at + 16, :] = second


def start_copies(sems, *pairs):
    copies = [
        pltpu.make_async_copy(source, target, sems.at[n]) for n, (source, target) in enumerate(pairs)
    ]
    for copy in copies:
        copy.start()
    return copies


def first_kernel(
    pair_hbm, mask_hbm, gain_hbm, bias_hbm, left_hbm, left_gate_hbm, right_hbm, right_gate_hbm,
    w_out_hbm, out_gain_hbm, out_bias_hbm, cot_hbm, w_gate_hbm,
    send_ref, stack_ref, mask_ref, packed_ref, cot_ref, w_gate_ref,
    pair_s, mask_s, norm_s, w_s, w_out_s, out_gain_s, out_bias_s, rows_s, send_s, sems,
):
    ch = lax.axis_index("ch")
    own, other = ch * 32, 32 - ch * 32
    copies = start_copies(
        sems,
        (pair_hbm.at[pl.ds(own, 32)], pair_s.at[0:32]),
        (gain_hbm, norm_s.at[0]),
        (bias_hbm, norm_s.at[1]),
        (mask_hbm.at[pl.ds(own, 32)], mask_s.at[0:32]),
        (left_hbm, w_s.at[0:64]),
        (left_gate_hbm, w_s.at[64:128]),
        (right_hbm, w_s.at[128:192]),
        (right_gate_hbm, w_s.at[192:256]),
        (pair_hbm.at[pl.ds(other, 32)], pair_s.at[32:64]),
        (mask_hbm.at[pl.ds(other, 32)], mask_s.at[32:64]),
        (w_out_hbm, w_out_s),
        (out_gain_hbm, out_gain_s),
        (out_bias_hbm, out_bias_s),
        (cot_hbm.at[pl.ds(own, 32)], cot_ref),
        (w_gate_hbm, w_gate_ref),
    )
    for copy in copies[:8]:
        copy.wait()
    gain, bias = column(norm_s[0]), column(norm_s[1])
    gain = jnp.concatenate([gain, gain], axis=1)
    bias = jnp.concatenate([bias, bias], axis=1)
    rows_s[:TILES] = mask_rows(mask_s[:32])
    mask_ref[...] = rows_s[:TILES]
    w = w_s[...]
    for part in range(2):
        if part == 1:
            for copy in copies[8:13]:
                copy.wait()
            rows_s[TILES:] = mask_rows(mask_s[32:])
            packed_ref[:256] = w.astype(f32)
            packed_ref[256:320] = w_out_s[...].astype(f32)
            norms = jnp.concatenate([out_gain_s[...], out_bias_s[...]], axis=1)
            packed_ref[320:328] = jnp.broadcast_to(norms, (8, 128))
        row = part * TILES
        for q in range(0, TILES, 2):
            zhat, _ = norm_over_rows(pair_tiles(pair_s, part * 32, q))
            normed = (zhat * gain + bias).astype(bf16)
            if part == 0:
                lanes = slice(q * 128, (q + 2) * 128)
                stack_ref[:128, lanes] = normed
                stack_ref[128:, lanes] = zhat.astype(bf16)
            y = matmul(w, normed)
            m = mask_pair(rows_s, row + q)
            store_tiles(send_s, row + q, m * sigmoid(y[64:128]) * y[:64])
            store_tiles(send_s, row + 32 + q, m * sigmoid(y[192:]) * y[128:192])
    for part, start in enumerate((own, other)):
        for side in range(2):
            target = pl.ds(pl.multiple_of(start // 2 + side * 32, TILES), TILES)
            row = part * TILES + side * 32
            send_ref[:, target] = send_s[:, row : row + TILES].astype(bf16)
    for copy in copies[13:]:
        copy.wait()


def triangle_kernel(blocks_ref, send_ref, left_ref, right_ref):
    load_matrix(blocks_ref.at[:, :, 0], left_ref)
    load_matrix(blocks_ref.at[:, :, 1], right_ref)
    tri = matmul_nt(left_ref[...], right_ref[...]).astype(bf16)
    store_matrix(tri, send_ref, 0)


def middle_kernel(
    tri_ref, stack_ref, cot_ref, w_gate_ref, own_ref, other_ref,
    send_ref, gpre_ref, early_ref, tri_s, d_tri_s, tnorm_s, d_proj_s,
):
    group = 16
    is_first = lax.axis_index("ch") == 0
    for side in range(2):
        tri_s[side * 64 : (side + 1) * 64, :TILES] = tri_ref[:, side].astype(f32)
    w_out = both_halves(is_first, own_ref, other_ref, 256, 64)
    w_out_t = w_out.T.astype(bf16)
    w_out = w_out.astype(bf16)
    w_gate_t = w_gate_ref[...].astype(f32).T.astype(bf16)
    own_col, other_col = column(own_ref[320:321]), column(other_ref[320:321])
    low = jnp.where(is_first, own_col, other_col)
    high = jnp.where(is_first, other_col, own_col)
    gain = jnp.concatenate([low[:64], high[:64]], axis=0)
    bias = jnp.concatenate([low[64:], high[64:]], axis=0)
    gain = jnp.concatenate([gain] * group, axis=1)
    bias = jnp.concatenate([bias] * group, axis=1)
    gain_sum = jnp.zeros((128, group * 128), f32)
    bias_sum = jnp.zeros((128, group * 128), f32)
    gpre_sum = jnp.zeros((128, group * 128), f32)
    for q in range(0, TILES, group):
        lanes = slice(q * 128, (q + group) * 128)
        that, inverse = norm_over_rows(load_tiles(tri_s, q, group))
        tnorm = (that * gain + bias).astype(bf16)
        tnorm_s[:, lanes] = tnorm
        proj = matmul(w_out_t, tnorm)
        gate = sigmoid(matmul(w_gate_t, stack_ref[:128, lanes]))
        gated = pair_tiles(cot_ref, 0, q, group) * gate
        d_proj = gated.astype(bf16)
        d_proj_s[:, lanes] = d_proj
        d_gpre = gated * proj * (1.0 - gate)
        gpre_ref[:, lanes] = d_gpre.astype(bf16)
        gpre_sum = gpre_sum + d_gpre
        d_tnorm = matmul(w_out, d_proj)
        gain_sum = gain_sum + d_tnorm * that
        bias_sum = bias_sum + d_tnorm
        dth = d_tnorm * gain
        d_tri = (
            dth
            - jnp.mean(dth, axis=0, keepdims=True)
            - that * jnp.mean(dth * that, axis=0, keepdims=True)
        ) * inverse
        store_tiles(d_tri_s, q, d_tri)
    for side in range(2):
        send_ref[:, side] = d_tri_s[side * 64 : (side + 1) * 64, :TILES].astype(bf16)
    early_ref[0] = matmul_nt(tnorm_s[...], d_proj_s[...])
    early_ref[1] = fold(gain_sum)
    early_ref[2] = fold(bias_sum)
    early_ref[3] = fold(gpre_sum)


def back_kernel(blocks_ref, left_ref, right_ref, send_ref, d_tri_s):
    load_matrix(blocks_ref, d_tri_s)
    d_tri = d_tri_s[...]
    store_matrix(matmul(d_tri, right_ref[...]).astype(bf16), send_ref, 0)
    store_matrix(matmul_tn(d_tri, left_ref[...]).astype(bf16), send_ref, 16)


def grads_kernel(
    d_ref, mask_ref, stack_ref, gpre_ref, own_ref, other_ref, w_gate_ref, early_ref,
    delta_hbm, w_back_hbm, send_hbm, delta_ref, w_back_ref, d_s, grads_s, send_ref, sems,
):
    is_first = lax.axis_index("ch") == 0
    for side in range(2):
        d_s[side * 64 : (side + 1) * 64, :32] = d_ref[:, side].astype(f32)
    weights = [both_halves(is_first, own_ref, other_ref, n * 64, 64) for n in range(4)]
    w = jnp.concatenate(weights, axis=0).astype(bf16)
    for n in range(4):
        w_back_ref[:, n * 128 : (n + 1) * 128] = weights[n].T.astype(bf16)
    w_back_ref[:, 512:] = w_gate_ref[...]
    copies = [
        pltpu.make_async_copy(w_back_ref, w_back_hbm, sems.at[0]),
        pltpu.make_async_copy(gpre_ref, delta_hbm.at[512:], sems.at[1]),
    ]
    copies[0].start()
    copies[1].start()
    delta_ref[512:] = gpre_ref[...]
    delta_sums = [jnp.zeros((128, 256), f32)] * 4
    for q in range(0, TILES, 2):
        lanes = slice(q * 128, (q + 2) * 128)
        y = matmul(w, stack_ref[:128, lanes])
        m = mask_pair(mask_ref, q)
        for side in range(2):
            lin = y[side * 256 : side * 256 + 128]
            sig = sigmoid(y[side * 256 + 128 : side * 256 + 256])
            d_lin = load_tiles(d_s, side * TILES + q) * m * sig
            d_gate = d_lin * lin * (1.0 - sig)
            for n, d in ((2 * side, d_lin), (2 * side + 1, d_gate)):
                delta_ref[n * 128 : (n + 1) * 128, lanes] = d.astype(bf16)
                delta_sums[n] = delta_sums[n] + d
        if q % 4 == 2:
            part = (slice(0, 512), slice((q - 2) * 128, (q + 2) * 128))
            copies.append(
                pltpu.make_async_copy(
                    delta_ref.at[part], delta_hbm.at[part], sems.at[len(copies)]
                )
            )
            copies[-1].start()
    grads = matmul_nt(delta_ref[...], stack_ref[...])
    for n in range(5):
        whole = early_ref[0] if n == 4 else grads[n * 128 : (n + 1) * 128, :128]
        low, high = exchange(whole[:64], whole[64:])
        store_rows(grads_s, n, low)
        store_rows(grads_s, 8 + n, high)
    gain_sum = jnp.zeros((128, 128), f32)
    bias_sum = jnp.zeros((128, 128), f32)
    delta_sums = [fold(d) for d in delta_sums] + [early_ref[3]]
    weights.append(w_gate_ref[...].astype(f32).T)
    for n in range(5):
        gain_sum = gain_sum + weights[n] * grads[n * 128 : (n + 1) * 128, 128:]
        bias_sum = bias_sum + weights[n] * jnp.sum(delta_sums[n], axis=1, keepdims=True)
    sums = (
        column(jnp.sum(gain_sum, axis=0, keepdims=True)),
        column(jnp.sum(bias_sum, axis=0, keepdims=True)),
        jnp.sum(early_ref[1], axis=1, keepdims=True),
        jnp.sum(early_ref[2], axis=1, keepdims=True),
    )
    lane = lax.broadcasted_iota(jnp.int32, (128, 128), 1) % 64
    sums = jnp.where(
        lane < 32, jnp.where(lane < 16, sums[0], sums[1]), jnp.where(lane < 48, sums[2], sums[3])
    )
    for n, whole in enumerate((grads[512:, :128], sums, jnp.zeros((128, 128), f32))):
        store_rows(grads_s, 5 + n, whole[:64])
        store_rows(grads_s, 13 + n, whole[64:])
    send_ref[...] = grads_s[:, :16].astype(bf16)
    copies.append(pltpu.make_async_copy(send_ref, send_hbm, sems.at[6]))
    copies[-1].start()
    for copy in copies:
        copy.wait()


def pair_kernel(
    delta_hbm, w_back_hbm, pair_hbm, gain_hbm, d_pair_hbm, d_own_ref,
    delta_ref, w_back_ref, pair_ref, gain_ref, sems, out_sems,
):
    ch = lax.axis_index("ch")
    group = 4
    parts = [slice(n * group * 128, (n + 1) * group * 128) for n in range(TILES // group)]
    copies = start_copies(
        sems,
        (w_back_hbm, w_back_ref),
        (gain_hbm, gain_ref),
        (pair_hbm.at[pl.ds(ch * 32, 32)], pair_ref),
        *((delta_hbm.at[:, part], delta_ref.at[:, part]) for part in parts),
    )
    for copy in copies[:3]:
        copy.wait()
    gain = jnp.concatenate([column(gain_ref[...])] * group, axis=1)
    w_back = w_back_ref[...]
    stores = []
    for n, part in enumerate(parts):
        q = n * group
        zhat, inverse = norm_over_rows(pair_tiles(pair_ref, 0, q, group))
        copies[3 + n].wait()
        dzh = matmul(w_back, delta_ref[:, part]) * gain
        d_pair = (
            dzh
            - jnp.mean(dzh, axis=0, keepdims=True)
            - zhat * jnp.mean(dzh * zhat, axis=0, keepdims=True)
        ) * inverse
        for k in range(group):
            rows = d_pair[:, k * 128 : (k + 1) * 128].T
            d_own_ref[q + k] = rows[:64]
            d_own_ref[TILES + q + k] = rows[64:]
        if n % 2 == 1:
            stores += start_copies(
                out_sems.at[n - 1 : n + 1],
                *(
                    (
                        d_own_ref.at[start : start + 2 * group],
                        d_pair_hbm.at[pl.ds(ch * 32 + start, 2 * group)],
                    )
                    for start in (q - group, TILES + q - group)
                ),
            )
    for copy in stores:
        copy.wait()


def sum_kernel(grads_ref, send_ref):
    total = jnp.sum(grads_ref[...].astype(f32), axis=0)
    halves = exchange(
        jnp.concatenate([total[n : n + 1] for n in (0, 2, 5, 4)], axis=0),
        jnp.concatenate([total[n : n + 1] for n in (1, 3, 5, 6)], axis=0),
    )
    row = lax.broadcasted_iota(jnp.int32, (4, 128), 0)
    for side in range(2):
        rows = jnp.where(row == 2, total[5:6], halves[side])
        send_ref[:, side] = jnp.broadcast_to(rows.astype(bf16)[None], (64, 4, 128))


def end_kernel(grads_ref, other_ref, _, d_pair_hbm, *refs):
    outs, scratch, grads_s, sems = refs[:10], refs[10:20], refs[20], refs[21]
    ch = lax.axis_index("ch")
    is_first = ch == 0
    copies = [
        pltpu.make_async_copy(other_ref, d_pair_hbm.at[pl.ds(32 - ch * 32, 32)], sems.at[10])
    ]
    copies[0].start()
    for side in range(2):
        grads_s[:, side * 4 : side * 4 + 4] = grads_ref[:, side].astype(f32)
    rows = [load_rows(grads_s, n) for n in range(8)]
    out, sums = exchange(rows[3], rows[7])
    sums = jnp.concatenate([sums, sums], axis=0).T[:, :64]

    def vector(n):
        return jnp.concatenate([sums[n : n + 1], sums[64 + n : 65 + n]], axis=1)

    results = (
        vector(0),
        vector(16),
        *exchange(rows[0], rows[4]),
        *exchange(rows[1], rows[5]),
        jnp.concatenate([rows[2], rows[6]], axis=0).T,
        jnp.where(is_first, sums[32:33], sums[96:97]),
        jnp.where(is_first, sums[48:49], sums[112:113]),
        out,
    )
    for n, result in enumerate(results):
        scratch[n][...] = result
        copies.append(pltpu.make_async_copy(scratch[n], outs[n], sems.at[n]))
        copies[-1].start()
    for copy in copies:
        copy.wait()


VMEM = pl.BlockSpec(memory_space=pltpu.VMEM)
HBM = pl.BlockSpec(memory_space=pltpu.HBM)


def call(kernel, out_shapes, scratch, *args, in_specs=None, out_specs=None, aliases=None, us=None):
    out_specs = out_specs or [VMEM] * len(out_shapes)
    cost = None
    if us is not None:
        cost = pl.CostEstimate(flops=us * 10**9, bytes_accessed=us * 3 * 10**6, transcendentals=0)
    return pl.pallas_call(
        kernel,
        out_shape=[
            pltpu.HBM(s, t) if spec is HBM else jax.ShapeDtypeStruct(s, t)
            for (s, t), spec in zip(out_shapes, out_specs)
        ],
        in_specs=in_specs or [VMEM] * len(args),
        out_specs=out_specs,
        scratch_shapes=scratch,
        input_output_aliases=aliases or {},
        cost_estimate=cost,
        compiler_params=pltpu.CompilerParams(vmem_limit_bytes=VMEM_LIMIT),
    )(*args)


def in_hbm(*arrays):
    return [pltpu.with_memory_space_constraint(x, pltpu.HBM) for x in arrays]


def to_all(x):
    return lax.all_to_all(x, ALL, 0, 0, tiled=True)


def body(
    pair, cotangent, pair_mask, norm_gain, norm_bias, w_left, w_left_gate, w_right, w_right_gate,
    w_out_gate, out_norm_gain, out_norm_bias, w_out,
):
    pairs = 128 * TILES
    swap = [(0, 1), (1, 0)]
    with jax.named_scope("first"):
        send, stack, mask, packed, cot, w_gate = call(
            first_kernel,
            [
                ((64, 64, 128), bf16),
                ((256, pairs), bf16),
                ((TILES, 128), f32),
                ((2048, 128), f32),
                ((32, 64, 128), bf16),
                ((128, 128), bf16),
            ],
            [
                pltpu.VMEM((64, 64, 128), bf16),
                pltpu.VMEM((64, 64), jnp.int32),
                pltpu.VMEM((2, 1, 128), f32),
                pltpu.VMEM((256, 128), bf16),
                pltpu.VMEM((64, 128), bf16),
                pltpu.VMEM((1, 64), f32),
                pltpu.VMEM((1, 64), f32),
                pltpu.VMEM((2 * TILES, 128), f32),
                pltpu.VMEM((64, 72, 128), f32),
                pltpu.SemaphoreType.DMA((15,)),
            ],
            *in_hbm(
                pair, pair_mask, norm_gain[None], norm_bias[None], w_left.T, w_left_gate.T, w_right.T,
                w_right_gate.T, w_out, out_norm_gain[None], out_norm_bias[None], cotangent, w_out_gate,
            ),
            in_specs=[HBM] * 13,
        )
    with jax.named_scope("left_right"):
        blocks = lax.all_to_all(send, ("row", "col"), 0, 0, tiled=True)
    with jax.named_scope("weights"):
        blocks, own = lax.optimization_barrier((blocks, packed))
        other = lax.ppermute(own, "ch", swap)
    with jax.named_scope("triangle"):
        send, left, right = call(
            triangle_kernel,
            [((8, 8, 2, TILES, 128), bf16), ((512, 512), bf16), ((512, 512), bf16)],
            [],
            blocks.reshape(8, 8, 2, 2, TILES, 128),
        )
    with jax.named_scope("tri"):
        tri = to_all(send.reshape(128, TILES, 128))
    with jax.named_scope("middle"):
        send, gpre, early = call(
            middle_kernel,
            [((64, 2, TILES, 128), bf16), ((128, pairs), bf16), ((4, 128, 128), f32)],
            [
                pltpu.VMEM((128, 24, 128), f32),
                pltpu.VMEM((128, 24, 128), f32),
                pltpu.VMEM((128, pairs), bf16),
                pltpu.VMEM((128, pairs), bf16),
            ],
            tri.reshape(64, 2, TILES, 128), stack, cot, w_gate, own, other,
        )
    with jax.named_scope("d_tri"):
        blocks = to_all(send.reshape(128, TILES, 128))
    with jax.named_scope("back"):
        (send,) = call(
            back_kernel,
            [((8, 8, 2, 2 * TILES, 128), bf16)],
            [pltpu.VMEM((512, 512), bf16)],
            blocks.reshape(8, 8, 2, TILES, 128), left, right,
        )
    with jax.named_scope("d_left_right"):
        d_full = to_all(send.reshape(128, 2 * TILES, 128))
    with jax.named_scope("grads"):
        delta, w_back, send = call(
            grads_kernel,
            [((640, pairs), bf16), ((128, 640), bf16), ((64, 16, 128), bf16)],
            [
                pltpu.VMEM((640, pairs), bf16),
                pltpu.VMEM((128, 640), bf16),
                pltpu.VMEM((128, 40, 128), f32),
                pltpu.VMEM((64, 24, 128), f32),
                pltpu.VMEM((64, 16, 128), bf16),
                pltpu.SemaphoreType.DMA((7,)),
            ],
            d_full.reshape(64, 2, 2 * TILES, 128), mask, stack, gpre, own, other, w_gate, early,
            out_specs=[HBM, HBM, HBM],
        )
    with jax.named_scope("sums"):
        parts = to_all(send.reshape(128, 8, 128))
    with jax.named_scope("pair"):
        d_pair, d_own = call(
            pair_kernel,
            [((64, 64, 128), f32), ((32, 64, 128), f32)],
            [
                pltpu.VMEM((640, pairs), bf16),
                pltpu.VMEM((128, 640), bf16),
                pltpu.VMEM((32, 64, 128), bf16),
                pltpu.VMEM((1, 128), f32),
                pltpu.SemaphoreType.DMA((7,)),
                pltpu.SemaphoreType.DMA((4,)),
            ],
            *in_hbm(delta, w_back, pair, norm_gain[None]),
            in_specs=[HBM] * 4,
            out_specs=[HBM, VMEM],
            us=4,
        )
        parts, d_own = lax.optimization_barrier((parts, d_own))
        d_other = lax.ppermute(d_own, "ch", swap)
    with jax.named_scope("sums"):
        (send,) = call(sum_kernel, [((64, 2, 4, 128), bf16)], [], parts)
        parts = to_all(send.reshape(128, 4, 128)).reshape(64, 2, 4, 128)
    with jax.named_scope("end"):
        shapes = [
            ((64, 64, 128), f32), ((1, 128), f32), ((1, 128), f32), ((64, 128), f32), ((64, 128), f32), ((64, 128), f32),
            ((64, 128), f32), ((128, 128), f32), ((1, 64), f32), ((1, 64), f32), ((64, 128), f32),
        ]
        d_pair, gain, bias, left, left_gate, right, right_gate, gate, out_gain, out_bias, out = call(
            end_kernel,
            shapes,
            [pltpu.VMEM(shape, f32) for shape, _ in shapes[1:]]
            + [pltpu.VMEM((64, 8, 128), f32), pltpu.SemaphoreType.DMA((11,))],
            parts, d_other, *in_hbm(d_pair),
            in_specs=[VMEM, VMEM, HBM],
            out_specs=[HBM] * 11,
            aliases={2: 0},
        )
    return (
        d_pair, gain[0], bias[0], left.T, left_gate.T, right.T, right_gate.T, gate, out_gain[0],
        out_bias[0], out,
    )


def solution(mesh):
    placed = (
        P("row", "col", None), P("row", "col", None), P("row", "col"), P(), P(), P(None, "ch"),
        P(None, "ch"), P(None, "ch"), P(None, "ch"), P(), P("ch"), P("ch"), P("ch", None),
    )
    return jax.shard_map(
        body,
        mesh=mesh,
        in_specs=placed,
        out_specs=(
            P("row", "col", None), P(), P(), P(None, "ch"), P(None, "ch"), P(None, "ch"),
            P(None, "ch"), P(), P("ch"), P("ch"), P("ch", None),
        ),
        check_vma=False,
    )
```

```python
import jax
import jax.numpy as jnp
from jax import lax
from jax.experimental import pallas as pl
from jax.experimental.pallas import tpu as pltpu
from jax.sharding import PartitionSpec as P

f32 = jnp.float32
bf16 = jnp.bfloat16
ALL = ("row", "col", "ch")
TILES = 16
EPS = 1e-05
VMEM_LIMIT = 10 * 1024 * 1024


def matmul(a, b):
    return lax.dot_general(a, b, (((1,), (0,)), ((), ())), preferred_element_type=f32)


def matmul_nt(a, b):
    return lax.dot_general(a, b, (((1,), (1,)), ((), ())), preferred_element_type=f32)


def matmul_tn(a, b):
    return lax.dot_general(a, b, (((0,), (0,)), ((), ())), preferred_element_type=f32)


def sigmoid(x):
    return jax.nn.sigmoid(x)


def column(row):
    return jnp.broadcast_to(row, (128, 128)).T


def norm_over_rows(x):
    mean = jnp.mean(x, axis=0, keepdims=True)
    centred = x - mean
    inverse = lax.rsqrt(jnp.mean(centred * centred, axis=0, keepdims=True) + EPS)
    return centred * inverse, inverse


def pair_tiles(ref, start, q, group=2):
    tiles = [
        jnp.concatenate([ref[start + q + n], ref[start + TILES + q + n]], axis=0).T.astype(f32)
        for n in range(group)
    ]
    return jnp.concatenate(tiles, axis=1)


def mask_rows(mask):
    return jnp.concatenate([mask[:TILES], mask[TILES:]], axis=1).astype(f32)


def mask_pair(rows, start):
    return jnp.concatenate([rows[pl.ds(start, 1)], rows[pl.ds(start + 1, 1)]], axis=1)


def store_rows(ref, row, value):
    rows, block, _ = ref.shape
    ref.reshape(rows * block, 128)[pl.ds(row, rows, stride=block)] = value


def load_rows(ref, row):
    rows, block, _ = ref.shape
    return ref.reshape(rows * block, 128)[pl.ds(row, rows, stride=block)]


def store_tiles(ref, row, value):
    for n in range(value.shape[1] // 128):
        store_rows(ref, row + n, value[:, n * 128 : (n + 1) * 128])


def load_tiles(ref, row, group=2):
    return jnp.concatenate([load_rows(ref, row + n) for n in range(group)], axis=1)


def fold(x):
    return sum(x[:, n : n + 128] for n in range(0, x.shape[1], 128))


def both_halves(is_first, own_ref, other_ref, start, count):
    own, other = own_ref[start : start + count], other_ref[start : start + count]
    return jnp.concatenate(
        [jnp.where(is_first, own, other), jnp.where(is_first, other, own)], axis=0
    )


def exchange(a, b):
    return (
        jnp.concatenate([a[..., :64], b[..., :64]], axis=-1),
        jnp.concatenate([a[..., 64:], b[..., 64:]], axis=-1),
    )


def load_matrix(blocks, out):
    for pair in range(4):
        low, high = exchange(blocks[:, 2 * pair], blocks[:, 2 * pair + 1])
        out[:, pair * 128 : (pair + 1) * 128] = jnp.stack([low, high], axis=2).reshape(512, 128)


def store_matrix(matrix, blocks, at):
    for pair in range(4):
        part = matrix[:, pair * 128 : (pair + 1) * 128].reshape(8, 2, 2, 16, 128)
        first, second = exchange(part[:, :, 0], part[:, :, 1])
        blocks[:, 2 * pair, :, at : at + 16, :] = first
        blocks[:, 2 * pair + 1, :, at : at + 16, :] = second


def start_copies(sems, *pairs):
    copies = [
        pltpu.make_async_copy(source, target, sems.at[n]) for n, (source, target) in enumerate(pairs)
    ]
    for copy in copies:
        copy.start()
    return copies


def first_kernel(
    pair_hbm, mask_hbm, gain_hbm, bias_hbm, left_hbm, left_gate_hbm, right_hbm, right_gate_hbm,
    w_out_hbm, out_gain_hbm, out_bias_hbm, send_ref, stack_ref, mask_ref, packed_ref,
    pair_s, mask_s, norm_s, w_s, w_out_s, out_gain_s, out_bias_s, rows_s, send_s, sems,
):
    ch = lax.axis_index("ch")
    own, other = ch * 32, 32 - ch * 32
    copies = start_copies(
        sems,
        (pair_hbm.at[pl.ds(own, 32)], pair_s.at[0:32]),
        (gain_hbm, norm_s.at[0]),
        (bias_hbm, norm_s.at[1]),
        (mask_hbm.at[pl.ds(own, 32)], mask_s.at[0:32]),
        (left_hbm, w_s.at[0:64]),
        (left_gate_hbm, w_s.at[64:128]),
        (right_hbm, w_s.at[128:192]),
        (right_gate_hbm, w_s.at[192:256]),
        (pair_hbm.at[pl.ds(other, 32)], pair_s.at[32:64]),
        (mask_hbm.at[pl.ds(other, 32)], mask_s.at[32:64]),
        (w_out_hbm, w_out_s),
        (out_gain_hbm, out_gain_s),
        (out_bias_hbm, out_bias_s),
    )
    for copy in copies[:8]:
        copy.wait()
    gain, bias = column(norm_s[0]), column(norm_s[1])
    gain = jnp.concatenate([gain, gain], axis=1)
    bias = jnp.concatenate([bias, bias], axis=1)
    rows_s[:TILES] = mask_rows(mask_s[:32])
    mask_ref[...] = rows_s[:TILES]
    w = w_s[...]
    for part in range(2):
        if part == 1:
            for copy in copies[8:13]:
                copy.wait()
            rows_s[TILES:] = mask_rows(mask_s[32:])
            packed_ref[:256] = w.astype(f32)
            packed_ref[256:320] = w_out_s[...].astype(f32)
            norms = jnp.concatenate([out_gain_s[...], out_bias_s[...]], axis=1)
            packed_ref[320:328] = jnp.broadcast_to(norms, (8, 128))
        row = part * TILES
        for q in range(0, TILES, 2):
            zhat, _ = norm_over_rows(pair_tiles(pair_s, part * 32, q))
            normed = (zhat * gain + bias).astype(bf16)
            if part == 0:
                lanes = slice(q * 128, (q + 2) * 128)
                stack_ref[:128, lanes] = normed
                stack_ref[128:, lanes] = zhat.astype(bf16)
            y = matmul(w, normed)
            m = mask_pair(rows_s, row + q)
            store_tiles(send_s, row + q, m * sigmoid(y[64:128]) * y[:64])
            store_tiles(send_s, row + 32 + q, m * sigmoid(y[192:]) * y[128:192])
    for part, start in enumerate((own, other)):
        for side in range(2):
            target = pl.ds(pl.multiple_of(start // 2 + side * 32, TILES), TILES)
            row = part * TILES + side * 32
            send_ref[:, target] = send_s[:, row : row + TILES].astype(bf16)


def triangle_kernel(blocks_ref, send_ref, left_ref, right_ref):
    load_matrix(blocks_ref.at[:, :, 0], left_ref)
    load_matrix(blocks_ref.at[:, :, 1], right_ref)
    tri = matmul_nt(left_ref[...], right_ref[...]).astype(bf16)
    store_matrix(tri, send_ref, 0)


def middle_kernel(
    tri_ref, stack_ref, cot_ref, w_gate_ref, own_ref, other_ref,
    send_ref, gpre_ref, early_ref, tri_s, d_tri_s, tnorm_s, d_proj_s,
):
    group = 16
    ch = lax.axis_index("ch")
    is_first = ch == 0
    for side in range(2):
        tri_s[side * 64 : (side + 1) * 64, :TILES] = tri_ref[:, side].astype(f32)
    w_out = both_halves(is_first, own_ref, other_ref, 256, 64)
    w_out_t = w_out.T.astype(bf16)
    w_out = w_out.astype(bf16)
    w_gate_t = w_gate_ref[...].astype(f32).T.astype(bf16)
    own_col, other_col = column(own_ref[320:321]), column(other_ref[320:321])
    low = jnp.where(is_first, own_col, other_col)
    high = jnp.where(is_first, other_col, own_col)
    gain = jnp.concatenate([low[:64], high[:64]], axis=0)
    bias = jnp.concatenate([low[64:], high[64:]], axis=0)
    gain = jnp.concatenate([gain] * group, axis=1)
    bias = jnp.concatenate([bias] * group, axis=1)
    gain_sum = jnp.zeros((128, group * 128), f32)
    bias_sum = jnp.zeros((128, group * 128), f32)
    gpre_sum = jnp.zeros((128, group * 128), f32)
    for q in range(0, TILES, group):
        lanes = slice(q * 128, (q + group) * 128)
        that, inverse = norm_over_rows(load_tiles(tri_s, q, group))
        tnorm = (that * gain + bias).astype(bf16)
        tnorm_s[:, lanes] = tnorm
        proj = matmul(w_out_t, tnorm)
        gate = sigmoid(matmul(w_gate_t, stack_ref[:128, lanes]))
        gated = pair_tiles(cot_ref, ch * 32, q, group) * gate
        d_proj = gated.astype(bf16)
        d_proj_s[:, lanes] = d_proj
        d_gpre = gated * proj * (1.0 - gate)
        gpre_ref[:, lanes] = d_gpre.astype(bf16)
        gpre_sum = gpre_sum + d_gpre
        d_tnorm = matmul(w_out, d_proj)
        gain_sum = gain_sum + d_tnorm * that
        bias_sum = bias_sum + d_tnorm
        dth = d_tnorm * gain
        d_tri = (
            dth
            - jnp.mean(dth, axis=0, keepdims=True)
            - that * jnp.mean(dth * that, axis=0, keepdims=True)
        ) * inverse
        store_tiles(d_tri_s, q, d_tri)
    for side in range(2):
        send_ref[:, side] = d_tri_s[side * 64 : (side + 1) * 64, :TILES].astype(bf16)
    early_ref[0] = matmul_nt(tnorm_s[...], d_proj_s[...])
    early_ref[1] = fold(gain_sum)
    early_ref[2] = fold(bias_sum)
    early_ref[3] = fold(gpre_sum)


def back_kernel(blocks_ref, left_ref, right_ref, send_ref, d_tri_s):
    load_matrix(blocks_ref, d_tri_s)
    d_tri = d_tri_s[...]
    store_matrix(matmul(d_tri, right_ref[...]).astype(bf16), send_ref, 0)
    store_matrix(matmul_tn(d_tri, left_ref[...]).astype(bf16), send_ref, 16)


def grads_kernel(
    d_ref, mask_ref, stack_ref, gpre_ref, own_ref, other_ref, w_gate_ref, early_ref,
    delta_hbm, w_back_hbm, send_hbm, delta_ref, w_back_ref, d_s, grads_s, send_ref, sems,
):
    is_first = lax.axis_index("ch") == 0
    for side in range(2):
        d_s[side * 64 : (side + 1) * 64, :32] = d_ref[:, side].astype(f32)
    weights = [both_halves(is_first, own_ref, other_ref, n * 64, 64) for n in range(4)]
    w = jnp.concatenate(weights, axis=0).astype(bf16)
    for n in range(4):
        w_back_ref[:, n * 128 : (n + 1) * 128] = weights[n].T.astype(bf16)
    w_back_ref[:, 512:] = w_gate_ref[...]
    copies = [
        pltpu.make_async_copy(w_back_ref, w_back_hbm, sems.at[0]),
        pltpu.make_async_copy(gpre_ref, delta_hbm.at[512:], sems.at[1]),
    ]
    copies[0].start()
    copies[1].start()
    delta_ref[512:] = gpre_ref[...]
    delta_sums = [jnp.zeros((128, 256), f32)] * 4
    for q in range(0, TILES, 2):
        lanes = slice(q * 128, (q + 2) * 128)
        y = matmul(w, stack_ref[:128, lanes])
        m = mask_pair(mask_ref, q)
        for side in range(2):
            lin = y[side * 256 : side * 256 + 128]
            sig = sigmoid(y[side * 256 + 128 : side * 256 + 256])
            d_lin = load_tiles(d_s, side * TILES + q) * m * sig
            d_gate = d_lin * lin * (1.0 - sig)
            for n, d in ((2 * side, d_lin), (2 * side + 1, d_gate)):
                delta_ref[n * 128 : (n + 1) * 128, lanes] = d.astype(bf16)
                delta_sums[n] = delta_sums[n] + d
        if q % 4 == 2:
            part = (slice(0, 512), slice((q - 2) * 128, (q + 2) * 128))
            copies.append(
                pltpu.make_async_copy(
                    delta_ref.at[part], delta_hbm.at[part], sems.at[len(copies)]
                )
            )
            copies[-1].start()
    grads = matmul_nt(delta_ref[...], stack_ref[...])
    for n in range(5):
        whole = early_ref[0] if n == 4 else grads[n * 128 : (n + 1) * 128, :128]
        low, high = exchange(whole[:64], whole[64:])
        store_rows(grads_s, n, low)
        store_rows(grads_s, 8 + n, high)
    gain_sum = jnp.zeros((128, 128), f32)
    bias_sum = jnp.zeros((128, 128), f32)
    delta_sums = [fold(d) for d in delta_sums] + [early_ref[3]]
    weights.append(w_gate_ref[...].astype(f32).T)
    for n in range(5):
        gain_sum = gain_sum + weights[n] * grads[n * 128 : (n + 1) * 128, 128:]
        bias_sum = bias_sum + weights[n] * jnp.sum(delta_sums[n], axis=1, keepdims=True)
    sums = (
        column(jnp.sum(gain_sum, axis=0, keepdims=True)),
        column(jnp.sum(bias_sum, axis=0, keepdims=True)),
        jnp.sum(early_ref[1], axis=1, keepdims=True),
        jnp.sum(early_ref[2], axis=1, keepdims=True),
    )
    lane = lax.broadcasted_iota(jnp.int32, (128, 128), 1) % 64
    sums = jnp.where(
        lane < 32, jnp.where(lane < 16, sums[0], sums[1]), jnp.where(lane < 48, sums[2], sums[3])
    )
    for n, whole in enumerate((grads[512:, :128], sums, jnp.zeros((128, 128), f32))):
        store_rows(grads_s, 5 + n, whole[:64])
        store_rows(grads_s, 13 + n, whole[64:])
    send_ref[...] = grads_s[:, :16].astype(bf16)
    copies.append(pltpu.make_async_copy(send_ref, send_hbm, sems.at[6]))
    copies[-1].start()
    for copy in copies:
        copy.wait()


def pair_kernel(
    delta_hbm, w_back_hbm, pair_hbm, gain_hbm, d_pair_hbm, d_own_ref,
    delta_ref, w_back_ref, pair_ref, gain_ref, sems, out_sems,
):
    ch = lax.axis_index("ch")
    group = 4
    parts = [slice(n * group * 128, (n + 1) * group * 128) for n in range(TILES // group)]
    copies = start_copies(
        sems,
        (w_back_hbm, w_back_ref),
        (gain_hbm, gain_ref),
        (pair_hbm.at[pl.ds(ch * 32, 32)], pair_ref),
        *((delta_hbm.at[:, part], delta_ref.at[:, part]) for part in parts),
    )
    for copy in copies[:3]:
        copy.wait()
    gain = jnp.concatenate([column(gain_ref[...])] * group, axis=1)
    w_back = w_back_ref[...]
    stores = []
    for n, part in enumerate(parts):
        q = n * group
        zhat, inverse = norm_over_rows(pair_tiles(pair_ref, 0, q, group))
        copies[3 + n].wait()
        dzh = matmul(w_back, delta_ref[:, part]) * gain
        d_pair = (
            dzh
            - jnp.mean(dzh, axis=0, keepdims=True)
            - zhat * jnp.mean(dzh * zhat, axis=0, keepdims=True)
        ) * inverse
        for k in range(group):
            rows = d_pair[:, k * 128 : (k + 1) * 128].T
            d_own_ref[q + k] = rows[:64]
            d_own_ref[TILES + q + k] = rows[64:]
        if n % 2 == 1:
            stores += start_copies(
                out_sems.at[n - 1 : n + 1],
                *(
                    (
                        d_own_ref.at[start : start + 2 * group],
                        d_pair_hbm.at[pl.ds(ch * 32 + start, 2 * group)],
                    )
                    for start in (q - group, TILES + q - group)
                ),
            )
    for copy in stores:
        copy.wait()


def sum_kernel(grads_ref, send_ref):
    total = jnp.sum(grads_ref[...].astype(f32), axis=0)
    halves = exchange(
        jnp.concatenate([total[n : n + 1] for n in (0, 2, 5, 4)], axis=0),
        jnp.concatenate([total[n : n + 1] for n in (1, 3, 5, 6)], axis=0),
    )
    row = lax.broadcasted_iota(jnp.int32, (4, 128), 0)
    for side in range(2):
        rows = jnp.where(row == 2, total[5:6], halves[side])
        send_ref[:, side] = jnp.broadcast_to(rows.astype(bf16)[None], (64, 4, 128))


def end_kernel(grads_ref, other_ref, _, d_pair_hbm, *refs):
    outs, scratch, grads_s, sems = refs[:10], refs[10:20], refs[20], refs[21]
    ch = lax.axis_index("ch")
    is_first = ch == 0
    copies = [
        pltpu.make_async_copy(other_ref, d_pair_hbm.at[pl.ds(32 - ch * 32, 32)], sems.at[10])
    ]
    copies[0].start()
    for side in range(2):
        grads_s[:, side * 4 : side * 4 + 4] = grads_ref[:, side].astype(f32)
    rows = [load_rows(grads_s, n) for n in range(8)]
    out, sums = exchange(rows[3], rows[7])
    sums = jnp.concatenate([sums, sums], axis=0).T[:, :64]

    def vector(n):
        return jnp.concatenate([sums[n : n + 1], sums[64 + n : 65 + n]], axis=1)

    results = (
        vector(0),
        vector(16),
        *exchange(rows[0], rows[4]),
        *exchange(rows[1], rows[5]),
        jnp.concatenate([rows[2], rows[6]], axis=0).T,
        jnp.where(is_first, sums[32:33], sums[96:97]),
        jnp.where(is_first, sums[48:49], sums[112:113]),
        out,
    )
    for n, result in enumerate(results):
        scratch[n][...] = result
        copies.append(pltpu.make_async_copy(scratch[n], outs[n], sems.at[n]))
        copies[-1].start()
    for copy in copies:
        copy.wait()


VMEM = pl.BlockSpec(memory_space=pltpu.VMEM)
HBM = pl.BlockSpec(memory_space=pltpu.HBM)


def call(kernel, out_shapes, scratch, *args, in_specs=None, out_specs=None, aliases=None, us=None):
    out_specs = out_specs or [VMEM] * len(out_shapes)
    cost = None
    if us is not None:
        cost = pl.CostEstimate(flops=us * 10**9, bytes_accessed=us * 3 * 10**6, transcendentals=0)
    return pl.pallas_call(
        kernel,
        out_shape=[
            pltpu.HBM(s, t) if spec is HBM else jax.ShapeDtypeStruct(s, t)
            for (s, t), spec in zip(out_shapes, out_specs)
        ],
        in_specs=in_specs or [VMEM] * len(args),
        out_specs=out_specs,
        scratch_shapes=scratch,
        input_output_aliases=aliases or {},
        cost_estimate=cost,
        compiler_params=pltpu.CompilerParams(vmem_limit_bytes=VMEM_LIMIT),
    )(*args)


def in_hbm(*arrays):
    return [pltpu.with_memory_space_constraint(x, pltpu.HBM) for x in arrays]


def to_all(x):
    return lax.all_to_all(x, ALL, 0, 0, tiled=True)


def body(
    pair, cotangent, pair_mask, norm_gain, norm_bias, w_left, w_left_gate, w_right, w_right_gate,
    w_out_gate, out_norm_gain, out_norm_bias, w_out,
):
    pairs = 128 * TILES
    swap = [(0, 1), (1, 0)]
    with jax.named_scope("first"):
        send, stack, mask, packed = call(
            first_kernel,
            [
                ((64, 64, 128), bf16),
                ((256, pairs), bf16),
                ((TILES, 128), f32),
                ((1024, 128), f32),
            ],
            [
                pltpu.VMEM((64, 64, 128), bf16),
                pltpu.VMEM((64, 64), jnp.int32),
                pltpu.VMEM((2, 1, 128), f32),
                pltpu.VMEM((256, 128), bf16),
                pltpu.VMEM((64, 128), bf16),
                pltpu.VMEM((1, 64), f32),
                pltpu.VMEM((1, 64), f32),
                pltpu.VMEM((2 * TILES, 128), f32),
                pltpu.VMEM((64, 72, 128), f32),
                pltpu.SemaphoreType.DMA((13,)),
            ],
            *in_hbm(
                pair, pair_mask, norm_gain[None], norm_bias[None], w_left.T, w_left_gate.T, w_right.T,
                w_right_gate.T, w_out, out_norm_gain[None], out_norm_bias[None],
            ),
            in_specs=[HBM] * 11,
        )
    with jax.named_scope("left_right"):
        blocks = lax.all_to_all(send, ("row", "col"), 0, 0, tiled=True)
    with jax.named_scope("weights"):
        blocks, own = lax.optimization_barrier((blocks, packed))
        other = lax.ppermute(own, "ch", swap)
    with jax.named_scope("triangle"):
        send, left, right = call(
            triangle_kernel,
            [((8, 8, 2, TILES, 128), bf16), ((512, 512), bf16), ((512, 512), bf16)],
            [],
            blocks.reshape(8, 8, 2, 2, TILES, 128),
        )
    with jax.named_scope("tri"):
        tri = to_all(send.reshape(128, TILES, 128))
    with jax.named_scope("middle"):
        send, gpre, early = call(
            middle_kernel,
            [((64, 2, TILES, 128), bf16), ((128, pairs), bf16), ((4, 128, 128), f32)],
            [
                pltpu.VMEM((128, 24, 128), f32),
                pltpu.VMEM((128, 24, 128), f32),
                pltpu.VMEM((128, pairs), bf16),
                pltpu.VMEM((128, pairs), bf16),
            ],
            tri.reshape(64, 2, TILES, 128), stack, cotangent, w_out_gate, own, other,
        )
    with jax.named_scope("d_tri"):
        blocks = to_all(send.reshape(128, TILES, 128))
    with jax.named_scope("back"):
        (send,) = call(
            back_kernel,
            [((8, 8, 2, 2 * TILES, 128), bf16)],
            [pltpu.VMEM((512, 512), bf16)],
            blocks.reshape(8, 8, 2, TILES, 128), left, right,
        )
    with jax.named_scope("d_left_right"):
        d_full = to_all(send.reshape(128, 2 * TILES, 128))
    with jax.named_scope("grads"):
        delta, w_back, send = call(
            grads_kernel,
            [((640, pairs), bf16), ((128, 640), bf16), ((64, 16, 128), bf16)],
            [
                pltpu.VMEM((640, pairs), bf16),
                pltpu.VMEM((128, 640), bf16),
                pltpu.VMEM((128, 40, 128), f32),
                pltpu.VMEM((64, 24, 128), f32),
                pltpu.VMEM((64, 16, 128), bf16),
                pltpu.SemaphoreType.DMA((7,)),
            ],
            d_full.reshape(64, 2, 2 * TILES, 128), mask, stack, gpre, own, other, w_out_gate, early,
            out_specs=[HBM, HBM, HBM],
        )
    with jax.named_scope("sums"):
        parts = to_all(send.reshape(128, 8, 128))
    with jax.named_scope("pair"):
        d_pair, d_own = call(
            pair_kernel,
            [((64, 64, 128), f32), ((32, 64, 128), f32)],
            [
                pltpu.VMEM((640, pairs), bf16),
                pltpu.VMEM((128, 640), bf16),
                pltpu.VMEM((32, 64, 128), bf16),
                pltpu.VMEM((1, 128), f32),
                pltpu.SemaphoreType.DMA((7,)),
                pltpu.SemaphoreType.DMA((4,)),
            ],
            *in_hbm(delta, w_back, pair, norm_gain[None]),
            in_specs=[HBM] * 4,
            out_specs=[HBM, VMEM],
            us=4,
        )
        parts, d_own = lax.optimization_barrier((parts, d_own))
        d_other = lax.ppermute(d_own, "ch", swap)
    with jax.named_scope("sums"):
        (send,) = call(sum_kernel, [((64, 2, 4, 128), bf16)], [], parts)
        parts = to_all(send.reshape(128, 4, 128)).reshape(64, 2, 4, 128)
    with jax.named_scope("end"):
        shapes = [
            ((64, 64, 128), f32), ((1, 128), f32), ((1, 128), f32), ((64, 128), f32), ((64, 128), f32), ((64, 128), f32),
            ((64, 128), f32), ((128, 128), f32), ((1, 64), f32), ((1, 64), f32), ((64, 128), f32),
        ]
        d_pair, gain, bias, left, left_gate, right, right_gate, gate, out_gain, out_bias, out = call(
            end_kernel,
            shapes,
            [pltpu.VMEM(shape, f32) for shape, _ in shapes[1:]]
            + [pltpu.VMEM((64, 8, 128), f32), pltpu.SemaphoreType.DMA((11,))],
            parts, d_other, *in_hbm(d_pair),
            in_specs=[VMEM, VMEM, HBM],
            out_specs=[HBM] * 11,
            aliases={2: 0},
        )
    return (
        d_pair, gain[0], bias[0], left.T, left_gate.T, right.T, right_gate.T, gate, out_gain[0],
        out_bias[0], out,
    )


def solution(mesh):
    placed = (
        P("row", "col", None), P("row", "col", None), P("row", "col"), P(), P(), P(None, "ch"),
        P(None, "ch"), P(None, "ch"), P(None, "ch"), P(), P("ch"), P("ch"), P("ch", None),
    )
    return jax.shard_map(
        body,
        mesh=mesh,
        in_specs=placed,
        out_specs=(
            P("row", "col", None), P(), P(), P(None, "ch"), P(None, "ch"), P(None, "ch"),
            P(None, "ch"), P(), P("ch"), P("ch"), P("ch", None),
        ),
        check_vma=False,
    )
```

```python
import jax
import jax.numpy as jnp
from jax import lax
from jax.experimental import pallas as pl
from jax.experimental.pallas import tpu as pltpu
from jax.sharding import PartitionSpec as P

f32 = jnp.float32
bf16 = jnp.bfloat16
ALL = ("row", "col", "ch")
TILES = 16
EPS = 1e-05
VMEM_LIMIT = 10 * 1024 * 1024


def matmul(a, b):
    return lax.dot_general(a, b, (((1,), (0,)), ((), ())), preferred_element_type=f32)


def matmul_nt(a, b):
    return lax.dot_general(a, b, (((1,), (1,)), ((), ())), preferred_element_type=f32)


def matmul_tn(a, b):
    return lax.dot_general(a, b, (((0,), (0,)), ((), ())), preferred_element_type=f32)


def sigmoid(x):
    return jax.nn.sigmoid(x)


def column(row):
    return jnp.broadcast_to(row, (128, 128)).T


def norm_over_rows(x):
    mean = jnp.mean(x, axis=0, keepdims=True)
    centred = x - mean
    inverse = lax.rsqrt(jnp.mean(centred * centred, axis=0, keepdims=True) + EPS)
    return centred * inverse, inverse


def pair_tiles(ref, start, q, group=2):
    tiles = [
        jnp.concatenate([ref[start + q + n], ref[start + TILES + q + n]], axis=0).T.astype(f32)
        for n in range(group)
    ]
    return jnp.concatenate(tiles, axis=1)


def mask_rows(mask):
    return jnp.concatenate([mask[:TILES], mask[TILES:]], axis=1).astype(f32)


def mask_pair(rows, start):
    return jnp.concatenate([rows[pl.ds(start, 1)], rows[pl.ds(start + 1, 1)]], axis=1)


def store_rows(ref, row, value):
    rows, block, _ = ref.shape
    ref.reshape(rows * block, 128)[pl.ds(row, rows, stride=block)] = value


def load_rows(ref, row):
    rows, block, _ = ref.shape
    return ref.reshape(rows * block, 128)[pl.ds(row, rows, stride=block)]


def store_tiles(ref, row, value):
    for n in range(value.shape[1] // 128):
        store_rows(ref, row + n, value[:, n * 128 : (n + 1) * 128])


def load_tiles(ref, row, group=2):
    return jnp.concatenate([load_rows(ref, row + n) for n in range(group)], axis=1)


def fold(x):
    return sum(x[:, n : n + 128] for n in range(0, x.shape[1], 128))


def both_halves(is_first, own_ref, other_ref, start, count):
    own, other = own_ref[start : start + count], other_ref[start : start + count]
    return jnp.concatenate(
        [jnp.where(is_first, own, other), jnp.where(is_first, other, own)], axis=0
    )


def exchange(a, b):
    return (
        jnp.concatenate([a[..., :64], b[..., :64]], axis=-1),
        jnp.concatenate([a[..., 64:], b[..., 64:]], axis=-1),
    )


def load_matrix(blocks, out):
    for pair in range(4):
        low, high = exchange(blocks[:, 2 * pair], blocks[:, 2 * pair + 1])
        out[:, pair * 128 : (pair + 1) * 128] = jnp.stack([low, high], axis=2).reshape(512, 128)


def store_matrix(matrix, blocks, at):
    for pair in range(4):
        part = matrix[:, pair * 128 : (pair + 1) * 128].reshape(8, 2, 2, 16, 128)
        first, second = exchange(part[:, :, 0], part[:, :, 1])
        blocks[:, 2 * pair, :, at : at + 16, :] = first
        blocks[:, 2 * pair + 1, :, at : at + 16, :] = second


def start_copies(sems, *pairs):
    copies = [
        pltpu.make_async_copy(source, target, sems.at[n]) for n, (source, target) in enumerate(pairs)
    ]
    for copy in copies:
        copy.start()
    return copies


def first_kernel(
    pair_hbm, mask_hbm, gain_hbm, bias_hbm, left_hbm, left_gate_hbm, right_hbm, right_gate_hbm,
    w_out_hbm, out_gain_hbm, out_bias_hbm, send_ref, stack_ref, mask_ref, packed_ref,
    pair_s, mask_s, norm_s, w_s, w_out_s, out_gain_s, out_bias_s, rows_s, send_s, sems,
):
    ch = lax.axis_index("ch")
    own, other = ch * 32, 32 - ch * 32
    copies = start_copies(
        sems,
        (pair_hbm.at[pl.ds(own, 32)], pair_s.at[0:32]),
        (gain_hbm, norm_s.at[0]),
        (bias_hbm, norm_s.at[1]),
        (mask_hbm.at[pl.ds(own, 32)], mask_s.at[0:32]),
        (left_hbm, w_s.at[0:64]),
        (left_gate_hbm, w_s.at[64:128]),
        (right_hbm, w_s.at[128:192]),
        (right_gate_hbm, w_s.at[192:256]),
        (pair_hbm.at[pl.ds(other, 32)], pair_s.at[32:64]),
        (mask_hbm.at[pl.ds(other, 32)], mask_s.at[32:64]),
        (w_out_hbm, w_out_s),
        (out_gain_hbm, out_gain_s),
        (out_bias_hbm, out_bias_s),
    )
    for copy in copies[:8]:
        copy.wait()
    gain, bias = column(norm_s[0]), column(norm_s[1])
    gain = jnp.concatenate([gain, gain], axis=1)
    bias = jnp.concatenate([bias, bias], axis=1)
    rows_s[:TILES] = mask_rows(mask_s[:32])
    mask_ref[...] = rows_s[:TILES]
    w = w_s[...]
    for part in range(2):
        if part == 1:
            for copy in copies[8:13]:
                copy.wait()
            rows_s[TILES:] = mask_rows(mask_s[32:])
            packed_ref[:256] = w.astype(f32)
            packed_ref[256:320] = w_out_s[...].astype(f32)
            norms = jnp.concatenate([out_gain_s[...], out_bias_s[...]], axis=1)
            packed_ref[320:328] = jnp.broadcast_to(norms, (8, 128))
        row = part * TILES
        for q in range(0, TILES, 2):
            zhat, _ = norm_over_rows(pair_tiles(pair_s, part * 32, q))
            normed = (zhat * gain + bias).astype(bf16)
            if part == 0:
                lanes = slice(q * 128, (q + 2) * 128)
                stack_ref[:128, lanes] = normed
                stack_ref[128:, lanes] = zhat.astype(bf16)
            y = matmul(w, normed)
            m = mask_pair(rows_s, row + q)
            store_tiles(send_s, row + q, m * sigmoid(y[64:128]) * y[:64])
            store_tiles(send_s, row + 32 + q, m * sigmoid(y[192:]) * y[128:192])
    for part, start in enumerate((own, other)):
        for side in range(2):
            target = pl.ds(pl.multiple_of(start // 2 + side * 32, TILES), TILES)
            row = part * TILES + side * 32
            send_ref[:, target] = send_s[:, row : row + TILES].astype(bf16)


def triangle_kernel(blocks_ref, send_ref, left_ref, right_ref):
    load_matrix(blocks_ref.at[:, :, 0], left_ref)
    load_matrix(blocks_ref.at[:, :, 1], right_ref)
    tri = matmul_nt(left_ref[...], right_ref[...]).astype(bf16)
    store_matrix(tri, send_ref, 0)


def middle_kernel(
    tri_ref, stack_ref, cot_ref, w_gate_ref, own_ref, other_ref,
    send_ref, gpre_ref, early_ref, tri_s, d_tri_s, tnorm_s, d_proj_s,
):
    group = 16
    ch = lax.axis_index("ch")
    is_first = ch == 0
    for side in range(2):
        tri_s[side * 64 : (side + 1) * 64, :TILES] = tri_ref[:, side].astype(f32)
    w_out = both_halves(is_first, own_ref, other_ref, 256, 64)
    w_out_t = w_out.T.astype(bf16)
    w_out = w_out.astype(bf16)
    w_gate_t = w_gate_ref[...].astype(f32).T.astype(bf16)
    own_col, other_col = column(own_ref[320:321]), column(other_ref[320:321])
    low = jnp.where(is_first, own_col, other_col)
    high = jnp.where(is_first, other_col, own_col)
    gain = jnp.concatenate([low[:64], high[:64]], axis=0)
    bias = jnp.concatenate([low[64:], high[64:]], axis=0)
    gain = jnp.concatenate([gain] * group, axis=1)
    bias = jnp.concatenate([bias] * group, axis=1)
    gain_sum = jnp.zeros((128, group * 128), f32)
    bias_sum = jnp.zeros((128, group * 128), f32)
    gpre_sum = jnp.zeros((128, group * 128), f32)
    for q in range(0, TILES, group):
        lanes = slice(q * 128, (q + group) * 128)
        that, inverse = norm_over_rows(load_tiles(tri_s, q, group))
        tnorm = (that * gain + bias).astype(bf16)
        tnorm_s[:, lanes] = tnorm
        proj = matmul(w_out_t, tnorm)
        gate = sigmoid(matmul(w_gate_t, stack_ref[:128, lanes]))
        gated = pair_tiles(cot_ref, ch * 32, q, group) * gate
        d_proj = gated.astype(bf16)
        d_proj_s[:, lanes] = d_proj
        d_gpre = gated * proj * (1.0 - gate)
        gpre_ref[:, lanes] = d_gpre.astype(bf16)
        gpre_sum = gpre_sum + d_gpre
        d_tnorm = matmul(w_out, d_proj)
        gain_sum = gain_sum + d_tnorm * that
        bias_sum = bias_sum + d_tnorm
        dth = d_tnorm * gain
        d_tri = (
            dth
            - jnp.mean(dth, axis=0, keepdims=True)
            - that * jnp.mean(dth * that, axis=0, keepdims=True)
        ) * inverse
        store_tiles(d_tri_s, q, d_tri)
    for side in range(2):
        send_ref[:, side] = d_tri_s[side * 64 : (side + 1) * 64, :TILES].astype(bf16)
    early_ref[0] = matmul_nt(tnorm_s[...], d_proj_s[...])
    early_ref[1] = fold(gain_sum)
    early_ref[2] = fold(bias_sum)
    early_ref[3] = fold(gpre_sum)


def back_kernel(blocks_ref, left_ref, right_ref, send_ref, d_tri_s):
    load_matrix(blocks_ref, d_tri_s)
    d_tri = d_tri_s[...]
    store_matrix(matmul(d_tri, right_ref[...]).astype(bf16), send_ref, 0)
    store_matrix(matmul_tn(d_tri, left_ref[...]).astype(bf16), send_ref, 16)


def grads_kernel(
    d_ref, mask_ref, stack_ref, gpre_ref, own_ref, other_ref, w_gate_ref, early_ref,
    delta_hbm, w_back_hbm, send_hbm, delta_ref, w_back_ref, d_s, grads_s, send_ref, sems,
):
    is_first = lax.axis_index("ch") == 0
    for side in range(2):
        d_s[side * 64 : (side + 1) * 64, :32] = d_ref[:, side].astype(f32)
    weights = [both_halves(is_first, own_ref, other_ref, n * 64, 64) for n in range(4)]
    w = jnp.concatenate(weights, axis=0).astype(bf16)
    for n in range(4):
        w_back_ref[:, n * 128 : (n + 1) * 128] = weights[n].T.astype(bf16)
    w_back_ref[:, 512:] = w_gate_ref[...]
    copies = [
        pltpu.make_async_copy(w_back_ref, w_back_hbm, sems.at[0]),
        pltpu.make_async_copy(gpre_ref, delta_hbm.at[512:], sems.at[1]),
    ]
    copies[0].start()
    copies[1].start()
    delta_ref[512:] = gpre_ref[...]
    delta_sums = [jnp.zeros((128, 256), f32)] * 4
    for q in range(0, TILES, 2):
        lanes = slice(q * 128, (q + 2) * 128)
        y = matmul(w, stack_ref[:128, lanes])
        m = mask_pair(mask_ref, q)
        for side in range(2):
            lin = y[side * 256 : side * 256 + 128]
            sig = sigmoid(y[side * 256 + 128 : side * 256 + 256])
            d_lin = load_tiles(d_s, side * TILES + q) * m * sig
            d_gate = d_lin * lin * (1.0 - sig)
            for n, d in ((2 * side, d_lin), (2 * side + 1, d_gate)):
                delta_ref[n * 128 : (n + 1) * 128, lanes] = d.astype(bf16)
                delta_sums[n] = delta_sums[n] + d
        if q % 4 == 2:
            part = (slice(0, 512), slice((q - 2) * 128, (q + 2) * 128))
            copies.append(
                pltpu.make_async_copy(
                    delta_ref.at[part], delta_hbm.at[part], sems.at[len(copies)]
                )
            )
            copies[-1].start()
    grads = matmul_nt(delta_ref[...], stack_ref[...])
    for n in range(5):
        whole = early_ref[0] if n == 4 else grads[n * 128 : (n + 1) * 128, :128]
        low, high = exchange(whole[:64], whole[64:])
        store_rows(grads_s, n, low)
        store_rows(grads_s, 8 + n, high)
    gain_sum = jnp.zeros((128, 128), f32)
    bias_sum = jnp.zeros((128, 128), f32)
    delta_sums = [fold(d) for d in delta_sums] + [early_ref[3]]
    weights.append(w_gate_ref[...].astype(f32).T)
    for n in range(5):
        gain_sum = gain_sum + weights[n] * grads[n * 128 : (n + 1) * 128, 128:]
        bias_sum = bias_sum + weights[n] * jnp.sum(delta_sums[n], axis=1, keepdims=True)
    sums = (
        column(jnp.sum(gain_sum, axis=0, keepdims=True)),
        column(jnp.sum(bias_sum, axis=0, keepdims=True)),
        jnp.sum(early_ref[1], axis=1, keepdims=True),
        jnp.sum(early_ref[2], axis=1, keepdims=True),
    )
    lane = lax.broadcasted_iota(jnp.int32, (128, 128), 1) % 64
    sums = jnp.where(
        lane < 32, jnp.where(lane < 16, sums[0], sums[1]), jnp.where(lane < 48, sums[2], sums[3])
    )
    for n, whole in enumerate((grads[512:, :128], sums, jnp.zeros((128, 128), f32))):
        store_rows(grads_s, 5 + n, whole[:64])
        store_rows(grads_s, 13 + n, whole[64:])
    send_ref[...] = grads_s[:, :16].astype(bf16)
    copies.append(pltpu.make_async_copy(send_ref, send_hbm, sems.at[6]))
    copies[-1].start()
    for copy in copies:
        copy.wait()


def pair_kernel(
    delta_hbm, w_back_hbm, pair_hbm, gain_hbm, d_pair_hbm, d_own_ref,
    delta_ref, w_back_ref, pair_ref, gain_ref, sems, out_sems,
):
    ch = lax.axis_index("ch")
    group = 4
    parts = [slice(n * group * 128, (n + 1) * group * 128) for n in range(TILES // group)]
    copies = start_copies(
        sems,
        (w_back_hbm, w_back_ref),
        (gain_hbm, gain_ref),
        (pair_hbm.at[pl.ds(ch * 32, 32)], pair_ref),
        *((delta_hbm.at[:, part], delta_ref.at[:, part]) for part in parts),
    )
    for copy in copies[:3]:
        copy.wait()
    gain = jnp.concatenate([column(gain_ref[...])] * group, axis=1)
    w_back = w_back_ref[...]
    stores = []
    for n, part in enumerate(parts):
        q = n * group
        zhat, inverse = norm_over_rows(pair_tiles(pair_ref, 0, q, group))
        copies[3 + n].wait()
        dzh = matmul(w_back, delta_ref[:, part]) * gain
        d_pair = (
            dzh
            - jnp.mean(dzh, axis=0, keepdims=True)
            - zhat * jnp.mean(dzh * zhat, axis=0, keepdims=True)
        ) * inverse
        for k in range(group):
            rows = d_pair[:, k * 128 : (k + 1) * 128].T
            d_own_ref[q + k] = rows[:64]
            d_own_ref[TILES + q + k] = rows[64:]
        if n % 2 == 1:
            stores += start_copies(
                out_sems.at[n - 1 : n + 1],
                *(
                    (
                        d_own_ref.at[start : start + 2 * group],
                        d_pair_hbm.at[pl.ds(ch * 32 + start, 2 * group)],
                    )
                    for start in (q - group, TILES + q - group)
                ),
            )
    for copy in stores:
        copy.wait()


def sum_kernel(grads_ref, send_ref):
    total = jnp.sum(grads_ref[...].astype(f32), axis=0)
    halves = exchange(
        jnp.concatenate([total[n : n + 1] for n in (0, 2, 5, 4)], axis=0),
        jnp.concatenate([total[n : n + 1] for n in (1, 3, 5, 6)], axis=0),
    )
    row = lax.broadcasted_iota(jnp.int32, (4, 128), 0)
    for side in range(2):
        rows = jnp.where(row == 2, total[5:6], halves[side])
        send_ref[:, side] = jnp.broadcast_to(rows.astype(bf16)[None], (64, 4, 128))


def end_kernel(grads_ref, other_ref, _, d_pair_hbm, *refs):
    outs, scratch, grads_s, sems = refs[:10], refs[10:20], refs[20], refs[21]
    ch = lax.axis_index("ch")
    is_first = ch == 0
    copies = [
        pltpu.make_async_copy(other_ref, d_pair_hbm.at[pl.ds(32 - ch * 32, 32)], sems.at[10])
    ]
    copies[0].start()
    for side in range(2):
        grads_s[:, side * 4 : side * 4 + 4] = grads_ref[:, side].astype(f32)
    rows = [load_rows(grads_s, n) for n in range(8)]
    out, sums = exchange(rows[3], rows[7])
    sums = jnp.concatenate([sums, sums], axis=0).T[:, :64]

    def vector(n):
        return jnp.concatenate([sums[n : n + 1], sums[64 + n : 65 + n]], axis=1)

    results = (
        vector(0),
        vector(16),
        *exchange(rows[0], rows[4]),
        *exchange(rows[1], rows[5]),
        jnp.concatenate([rows[2], rows[6]], axis=0).T,
        jnp.where(is_first, sums[32:33], sums[96:97]),
        jnp.where(is_first, sums[48:49], sums[112:113]),
        out,
    )
    for n, result in enumerate(results):
        scratch[n][...] = result
        copies.append(pltpu.make_async_copy(scratch[n], outs[n], sems.at[n]))
        copies[-1].start()
    for copy in copies:
        copy.wait()


VMEM = pl.BlockSpec(memory_space=pltpu.VMEM)
HBM = pl.BlockSpec(memory_space=pltpu.HBM)


def call(kernel, out_shapes, scratch, *args, in_specs=None, out_specs=None, aliases=None, us=None):
    out_specs = out_specs or [VMEM] * len(out_shapes)
    cost = None
    if us is not None:
        cost = pl.CostEstimate(flops=us * 10**9, bytes_accessed=us * 3 * 10**6, transcendentals=0)
    return pl.pallas_call(
        kernel,
        out_shape=[
            pltpu.HBM(s, t) if spec is HBM else jax.ShapeDtypeStruct(s, t)
            for (s, t), spec in zip(out_shapes, out_specs)
        ],
        in_specs=in_specs or [VMEM] * len(args),
        out_specs=out_specs,
        scratch_shapes=scratch,
        input_output_aliases=aliases or {},
        cost_estimate=cost,
        compiler_params=pltpu.CompilerParams(vmem_limit_bytes=VMEM_LIMIT),
    )(*args)


def in_hbm(*arrays):
    return [pltpu.with_memory_space_constraint(x, pltpu.HBM) for x in arrays]


def to_all(x):
    return lax.all_to_all(x, ALL, 0, 0, tiled=True)


def body(
    pair, cotangent, pair_mask, norm_gain, norm_bias, w_left, w_left_gate, w_right, w_right_gate,
    w_out_gate, out_norm_gain, out_norm_bias, w_out,
):
    pairs = 128 * TILES
    swap = [(0, 1), (1, 0)]
    with jax.named_scope("first"):
        send, stack, mask, packed = call(
            first_kernel,
            [
                ((64, 64, 128), bf16),
                ((256, pairs), bf16),
                ((TILES, 128), f32),
                ((512, 128), f32),
            ],
            [
                pltpu.VMEM((64, 64, 128), bf16),
                pltpu.VMEM((64, 64), jnp.int32),
                pltpu.VMEM((2, 1, 128), f32),
                pltpu.VMEM((256, 128), bf16),
                pltpu.VMEM((64, 128), bf16),
                pltpu.VMEM((1, 64), f32),
                pltpu.VMEM((1, 64), f32),
                pltpu.VMEM((2 * TILES, 128), f32),
                pltpu.VMEM((64, 72, 128), f32),
                pltpu.SemaphoreType.DMA((13,)),
            ],
            *in_hbm(
                pair, pair_mask, norm_gain[None], norm_bias[None], w_left.T, w_left_gate.T, w_right.T,
                w_right_gate.T, w_out, out_norm_gain[None], out_norm_bias[None],
            ),
            in_specs=[HBM] * 11,
        )
    with jax.named_scope("left_right"):
        blocks = lax.all_to_all(send, ("row", "col"), 0, 0, tiled=True)
    with jax.named_scope("weights"):
        blocks, own = lax.optimization_barrier((blocks, packed))
        other = lax.ppermute(own, "ch", swap)
    with jax.named_scope("triangle"):
        send, left, right = call(
            triangle_kernel,
            [((8, 8, 2, TILES, 128), bf16), ((512, 512), bf16), ((512, 512), bf16)],
            [],
            blocks.reshape(8, 8, 2, 2, TILES, 128),
        )
    with jax.named_scope("tri"):
        tri = to_all(send.reshape(128, TILES, 128))
    with jax.named_scope("middle"):
        send, gpre, early = call(
            middle_kernel,
            [((64, 2, TILES, 128), bf16), ((128, pairs), bf16), ((4, 128, 128), f32)],
            [
                pltpu.VMEM((128, 24, 128), f32),
                pltpu.VMEM((128, 24, 128), f32),
                pltpu.VMEM((128, pairs), bf16),
                pltpu.VMEM((128, pairs), bf16),
            ],
            tri.reshape(64, 2, TILES, 128), stack, cotangent, w_out_gate, own, other,
        )
    with jax.named_scope("d_tri"):
        blocks = to_all(send.reshape(128, TILES, 128))
    with jax.named_scope("back"):
        (send,) = call(
            back_kernel,
            [((8, 8, 2, 2 * TILES, 128), bf16)],
            [pltpu.VMEM((512, 512), bf16)],
            blocks.reshape(8, 8, 2, TILES, 128), left, right,
        )
    with jax.named_scope("d_left_right"):
        d_full = to_all(send.reshape(128, 2 * TILES, 128))
    with jax.named_scope("grads"):
        delta, w_back, send = call(
            grads_kernel,
            [((640, pairs), bf16), ((128, 640), bf16), ((64, 16, 128), bf16)],
            [
                pltpu.VMEM((640, pairs), bf16),
                pltpu.VMEM((128, 640), bf16),
                pltpu.VMEM((128, 40, 128), f32),
                pltpu.VMEM((64, 24, 128), f32),
                pltpu.VMEM((64, 16, 128), bf16),
                pltpu.SemaphoreType.DMA((7,)),
            ],
            d_full.reshape(64, 2, 2 * TILES, 128), mask, stack, gpre, own, other, w_out_gate, early,
            out_specs=[HBM, HBM, HBM],
        )
    with jax.named_scope("sums"):
        parts = to_all(send.reshape(128, 8, 128))
    with jax.named_scope("pair"):
        d_pair, d_own = call(
            pair_kernel,
            [((64, 64, 128), f32), ((32, 64, 128), f32)],
            [
                pltpu.VMEM((640, pairs), bf16),
                pltpu.VMEM((128, 640), bf16),
                pltpu.VMEM((32, 64, 128), bf16),
                pltpu.VMEM((1, 128), f32),
                pltpu.SemaphoreType.DMA((7,)),
                pltpu.SemaphoreType.DMA((4,)),
            ],
            *in_hbm(delta, w_back, pair, norm_gain[None]),
            in_specs=[HBM] * 4,
            out_specs=[HBM, VMEM],
            us=4,
        )
        parts, d_own = lax.optimization_barrier((parts, d_own))
        d_other = lax.ppermute(d_own, "ch", swap)
    with jax.named_scope("sums"):
        (send,) = call(sum_kernel, [((64, 2, 4, 128), bf16)], [], parts)
        parts = to_all(send.reshape(128, 4, 128)).reshape(64, 2, 4, 128)
    with jax.named_scope("end"):
        shapes = [
            ((64, 64, 128), f32), ((1, 128), f32), ((1, 128), f32), ((64, 128), f32), ((64, 128), f32), ((64, 128), f32),
            ((64, 128), f32), ((128, 128), f32), ((1, 64), f32), ((1, 64), f32), ((64, 128), f32),
        ]
        d_pair, gain, bias, left, left_gate, right, right_gate, gate, out_gain, out_bias, out = call(
            end_kernel,
            shapes,
            [pltpu.VMEM(shape, f32) for shape, _ in shapes[1:]]
            + [pltpu.VMEM((64, 8, 128), f32), pltpu.SemaphoreType.DMA((11,))],
            parts, d_other, *in_hbm(d_pair),
            in_specs=[VMEM, VMEM, HBM],
            out_specs=[HBM] * 11,
            aliases={2: 0},
        )
    return (
        d_pair, gain[0], bias[0], left.T, left_gate.T, right.T, right_gate.T, gate, out_gain[0],
        out_bias[0], out,
    )


def solution(mesh):
    placed = (
        P("row", "col", None), P("row", "col", None), P("row", "col"), P(), P(), P(None, "ch"),
        P(None, "ch"), P(None, "ch"), P(None, "ch"), P(), P("ch"), P("ch"), P("ch", None),
    )
    return jax.shard_map(
        body,
        mesh=mesh,
        in_specs=placed,
        out_specs=(
            P("row", "col", None), P(), P(), P(None, "ch"), P(None, "ch"), P(None, "ch"),
            P(None, "ch"), P(), P("ch"), P("ch"), P("ch", None),
        ),
        check_vma=False,
    )
```
